32 devices in a mesh: dp: 8 (over z, y), mp: 4 (over x, core).
Axes of the slice: x: 2, y: 2, z: 4, core: 2. Of those that a mesh axis runs over, the one named last changes fastest.
Arguments:
- patches: bfloat16 [4096, 1536], P('dp'), may hold values from -6 to 6
- cotangent: bfloat16 [4096, 1536], P('dp'), may hold values from -6 to 6
- item_lengths: int32 [4], replicated, may hold values from 1 to 1536, 3072 in all
- timesteps: int32 [5], replicated, may hold values from 0 to 999
- patch_rows: int32 [4096], P('dp'), may hold values from 0 to 63
- patch_cols: int32 [4096], P('dp'), may hold values from 0 to 63
- conditioning: bfloat16 [5, 1536], replicated, may hold values from -6 to 6
- text_states: bfloat16 [1280, 4096], P('dp', 'mp'), may hold values from -6 to 6
- gain_attn: bfloat16 [1536], P('dp'), may hold values from 0.5 to 1.5
- gain_ffn: bfloat16 [1536], P('dp'), may hold values from 0.5 to 1.5
- query_gain: bfloat16 [64], replicated, may hold values from 0.5 to 1.5
- key_gain: bfloat16 [64], replicated, may hold values from 0.5 to 1.5
- text_key_gain: bfloat16 [64], replicated, may hold values from 0.5 to 1.5
- cross_gate: bfloat16 [24], replicated, may hold values from -1.5 to 1.5
- w_query: bfloat16 [1536, 1536], P('dp', 'mp'), may hold values from -0.15625 to 0.15625
- w_key: bfloat16 [1536, 1536], P('dp', 'mp'), may hold values from -0.15625 to 0.15625
- w_value: bfloat16 [1536, 1536], P('dp', 'mp'), may hold values from -0.15625 to 0.15625
- w_out: bfloat16 [1536, 1536], P('dp', 'mp'), may hold values from -3 to 3
- w_text_key: bfloat16 [1536, 1536], P('dp', 'mp'), may hold values from -0.15625 to 0.15625
- w_text_value: bfloat16 [1536, 1536], P('dp', 'mp'), may hold values from -0.15625 to 0.15625
- w_gate: bfloat16 [1536, 4096], P('dp', 'mp'), may hold values from -0.15625 to 0.15625
- w_up: bfloat16 [1536, 4096], P('dp', 'mp'), may hold values from -0.15625 to 0.15625
- w_down: bfloat16 [1536, 4096], P('dp', 'mp'), may hold values from -0.09375 to 0.09375
- w_ada: bfloat16 [1536, 6144], P('dp', 'mp'), may hold values from -0.15625 to 0.15625
- w_text: bfloat16 [1536, 4096], P('dp', 'mp'), may hold values from -0.09375 to 0.09375
Outputs:
- mixed: bfloat16 [4096, 1536], P('dp')
- grad_patches: float32 [4096, 1536], P('dp')
- grad_conditioning: float32 [5, 1536], replicated
- grad_text: float32 [1280, 4096], P('dp', 'mp')
- grad_gain_attn: float32 [1536], P('dp')
- grad_gain_ffn: float32 [1536], P('dp')
- grad_query_gain: float32 [64], replicated
- grad_key_gain: float32 [64], replicated
- grad_text_key_gain: float32 [64], replicated
- grad_cross_gate: float32 [24], replicated
- grad_w_query: float32 [1536, 1536], P('dp', 'mp')
- grad_w_key: float32 [1536, 1536], P('dp', 'mp')
- grad_w_value: float32 [1536, 1536], P('dp', 'mp')
- grad_w_out: float32 [1536, 1536], P('dp', 'mp')
- grad_w_text_key: float32 [1536, 1536], P('dp', 'mp')
- grad_w_text_value: float32 [1536, 1536], P('dp', 'mp')
- grad_w_gate: float32 [1536, 4096], P('dp', 'mp')
- grad_w_up: float32 [1536, 4096], P('dp', 'mp')
- grad_w_down: float32 [1536, 4096], P('dp', 'mp')
- grad_w_ada: float32 [1536, 6144], P('dp', 'mp')
- grad_w_text: float32 [1536, 4096], P('dp', 'mp')
The draws below stay inside these ranges and needn't reach their ends.
Inputs may be any that keep to these rules, and one draw needn't show every extreme that they name: `item_lengths`: lengths of the 4 items that fill, in order, the rows after the first 128 of each index of dp; they sum to 3072.
All inputs are finite; a program needn't handle non-finite values.
Results may differ from the reference program's by a relative error of at most 0.035.
Values may be sent and summed in bfloat16 or wider, within the bound.
No kernel may reach another device: no remote copies, remote signals or barrier semaphores. Data moves between devices by JAX's collectives and lax.ppermute only.
A program may use at most 320 MiB of HBM per device.

```python
import math
import jax
import jax.numpy as jnp
import numpy as np
from jax import lax

D = 1536
HEADS = 24
HD = 64
FF = 4096
TD = 4096
TTOK = 256
TOK_DEV = 512
TOKENS = 4096
REST = 3072
NREST = 4
NITEMS = 5
MAXLEN = 1536
NT = 1280
N_DP = 8


def plant(array, rng, smallest, top_value):
    longest = array.shape.index(max(array.shape))
    spots = []
    for shift in (0, 1):
        where = [jax.random.randint(jax.random.fold_in(rng, axis), (), 0, length) for axis, length in enumerate(array.shape)]
        where[longest] = (where[longest] + shift) % array.shape[longest]
        spots.append(tuple(where))
    return array.at[spots[0]].set(smallest).at[spots[1]].set(top_value)


def levels(key, extent, pieces, smallest, high):
    gain, own = 1.0, jax.random.fold_in(key, 6)
    for dim, parts in pieces:
        heights = jnp.exp(jax.random.uniform(jax.random.fold_in(own, dim), (parts,), jnp.float32, smallest / len(pieces), high / len(pieces)))
        gain = gain * jnp.repeat(heights, extent[dim] // parts).reshape([-1 if axis == dim else 1 for axis in range(len(extent))])
    return gain


def length_profile(count, total, bound, lean):
    portions = [(1 << 20) // math.isqrt(standing ** lean) + 1 for standing in range(2, count + 1)]
    rest, counts = total - bound - (count - 1), [1] * (count - 1)
    while rest > 0:
        candidates = [i for i in range(count - 1) if counts[i] < bound]
        whole, remaining = sum([portions[i] for i in candidates]), rest
        for i in candidates:
            addition = min(bound - counts[i], max(1, remaining * portions[i] // whole), rest)
            counts[i] = counts[i] + addition
            rest = rest - addition
    return np.array([bound] + counts)


def ragged(own_key, number_of, total, most, slope):
    if number_of == 2:
        one = jax.random.randint(own_key, (), max(1, total - most), min(most, total - 1) + 1)
        return jnp.stack([one, total - one])
    sizes = jnp.asarray(length_profile(number_of, total, most, slope), jnp.int32)
    pairs = (number_of - 1) // 2
    giver, taker = sizes[1:1 + 2 * pairs:2], sizes[2:2 + 2 * pairs:2]
    room = jnp.minimum(giver - 1, most - taker)
    moved = jax.random.randint(jax.random.fold_in(own_key, 1), (pairs,), 0, 1 << 20) % (room + 1)
    sizes = sizes.at[1:1 + 2 * pairs:2].set(giver - moved).at[2:2 + 2 * pairs:2].set(taker + moved)
    return sizes[jax.random.permutation(jax.random.fold_in(own_key, 2), number_of)]


def noise(own_key, dims, width, limit, cuts=(), kind=jnp.bfloat16):
    values = jax.random.normal(own_key, dims, jnp.float32) * width
    if len(cuts) > 0:
        values = levels(own_key, dims, cuts, -0.22, 0.18) * values
    return jnp.clip(values, min=-limit, max=limit).astype(kind)


def setup_inputs(seed: int = 0) -> dict:
    arg_keys = jax.random.split(jax.random.key(seed), 26)
    return {
        "patches": noise(arg_keys[0], (TOKENS, D), 1.0, 6.0, ((0, 8),)),
        "cotangent": noise(arg_keys[1], (TOKENS, D), 1.0, 6.0, ((0, 8),)),
        "item_lengths": ragged(arg_keys[2], NREST, REST, MAXLEN, 2).astype(jnp.int32),
        "timesteps": plant(jax.random.randint(arg_keys[3], (NITEMS,), 0, 1000), jax.random.fold_in(arg_keys[3], 1), 0, 999).astype(jnp.int32),
        "patch_rows": plant(jax.random.randint(arg_keys[4], (TOKENS,), 0, 64), jax.random.fold_in(arg_keys[4], 1), 0, 63).astype(jnp.int32),
        "patch_cols": plant(jax.random.randint(arg_keys[5], (TOKENS,), 0, 64), jax.random.fold_in(arg_keys[5], 1), 0, 63).astype(jnp.int32),
        "conditioning": noise(arg_keys[6], (NITEMS, D), 1.0, 6.0),
        "text_states": noise(arg_keys[7], (NT, TD), 1.0, 6.0, ((0, 8), (1, 4))),
        "gain_attn": jnp.clip(1.0 + 0.1 * jax.random.normal(arg_keys[8], (D,), jnp.float32), 0.5, 1.5).astype(jnp.bfloat16),
        "gain_ffn": jnp.clip(1.0 + 0.1 * jax.random.normal(arg_keys[9], (D,), jnp.float32), 0.5, 1.5).astype(jnp.bfloat16),
        "query_gain": jnp.clip(1.0 + 0.1 * jax.random.normal(arg_keys[10], (HD,), jnp.float32), 0.5, 1.5).astype(jnp.bfloat16),
        "key_gain": jnp.clip(1.0 + 0.1 * jax.random.normal(arg_keys[11], (HD,), jnp.float32), 0.5, 1.5).astype(jnp.bfloat16),
        "text_key_gain": jnp.clip(1.0 + 0.1 * jax.random.normal(arg_keys[12], (HD,), jnp.float32), 0.5, 1.5).astype(jnp.bfloat16),
        "cross_gate": jnp.clip(jax.random.uniform(arg_keys[13], (HEADS,), jnp.float32, -1.5, 1.5), -1.5, 1.5).astype(jnp.bfloat16),
        "w_query": noise(arg_keys[14], (D, HEADS * HD), D ** -0.5, 0.15625, ((0, 8), (1, 4))),
        "w_key": noise(arg_keys[15], (D, HEADS * HD), D ** -0.5, 0.15625, ((0, 8), (1, 4))),
        "w_value": noise(arg_keys[16], (D, HEADS * HD), D ** -0.5, 0.15625, ((0, 8), (1, 4))),
        "w_out": noise(arg_keys[17], (D, HEADS * HD), 4 ** -0.5, 3.0, ((0, 8), (1, 4))),
        "w_text_key": noise(arg_keys[18], (D, HEADS * HD), D ** -0.5, 0.15625, ((0, 8), (1, 4))),
        "w_text_value": noise(arg_keys[19], (D, HEADS * HD), D ** -0.5, 0.15625, ((0, 8), (1, 4))),
        "w_gate": noise(arg_keys[20], (D, FF), D ** -0.5, 0.15625, ((0, 8), (1, 4))),
        "w_up": noise(arg_keys[21], (D, FF), D ** -0.5, 0.15625, ((0, 8), (1, 4))),
        "w_down": noise(arg_keys[22], (D, FF), FF ** -0.5, 0.09375, ((0, 8), (1, 4))),
        "w_ada": noise(arg_keys[23], (D, 4 * D), D ** -0.5, 0.15625, ((0, 8), (1, 4))),
        "w_text": noise(arg_keys[24], (D, TD), TD ** -0.5, 0.09375, ((0, 8), (1, 4))),
    }


HIGHEST = lax.Precision.HIGHEST
EPSILON = 1e-06
NEGATIVE = -1e+30
SCORE_BASE = 1.4426950408889634

@jax.custom_vjp
def low(v):
    return lax.optimization_barrier(v.astype(jnp.bfloat16)).astype(jnp.float32)

@jax.custom_vjp
def low_back(v):
    return v

def low_keep(v):
    return (low(v), None)

def low_pass(kept, grad):
    return (grad,)

def back_keep(v):
    return (v, None)

def back_low(kept, grad):
    return (low(grad),)
low.defvjp(low_keep, low_pass)
low_back.defvjp(back_keep, back_low)

def time_embed(steps, model_width):
    halfway = model_width // 2
    frequency = jnp.exp(-math.log(10000.0) * jnp.arange(halfway, dtype=jnp.float32) / halfway)
    phases = steps.astype(jnp.float32)[:, None] * frequency[None, :]
    return jnp.concatenate([jnp.cos(phases), jnp.sin(phases)], axis=1)

def rope_angles(rows_pos, cols_pos, head_dim):
    quarter = head_dim // 4
    frequency = jnp.exp(-math.log(10000.0) * jnp.arange(quarter, dtype=jnp.float32) / quarter)
    return jnp.concatenate([rows_pos.astype(jnp.float32)[:, None] * frequency[None, :], cols_pos.astype(jnp.float32)[:, None] * frequency[None, :]], axis=1)

def rotate(tensor, angles):
    quarter = tensor.shape[-1] // 4
    cosine = jnp.cos(angles)[:, None, :]
    sine = jnp.sin(angles)[:, None, :]
    first = tensor[..., :quarter]
    second = tensor[..., quarter:2 * quarter]
    third = tensor[..., 2 * quarter:3 * quarter]
    fourth = tensor[..., 3 * quarter:]
    row_cos, col_cos = (cosine[..., :quarter], cosine[..., quarter:])
    row_sin, col_sin = (sine[..., :quarter], sine[..., quarter:])
    return jnp.concatenate([first * row_cos - second * row_sin, first * row_sin + second * row_cos, third * col_cos - fourth * col_sin, third * col_sin + fourth * col_cos], axis=-1)

def item_ids(lengths, tok_dev, n_dev):
    wide_dev = tok_dev // 4
    boundary = jnp.cumsum(lengths).astype(jnp.int32)
    position = jnp.arange(tok_dev * n_dev, dtype=jnp.int32)
    within = position % tok_dev
    placed = position // tok_dev * (tok_dev - wide_dev) + within - wide_dev
    counted = lax.optimization_barrier(jnp.sum((boundary[None, :] <= placed[:, None]).astype(jnp.int32), axis=1))
    return jnp.where(within < wide_dev, lengths.shape[0], counted).astype(jnp.int32)

def rms_norm(values, gain_vec):
    return values * lax.rsqrt(lax.optimization_barrier(jnp.mean(values * values, axis=-1, keepdims=True)) + EPSILON) * gain_vec

def dense(left, right):
    return jnp.dot(left, right, precision=HIGHEST)

def attention(queries, query_items, key_rows, value_rows, key_items):
    scaling = key_rows.shape[-1] ** (-0.5) * SCORE_BASE
    raw_scores = jnp.einsum('qhd,khd->hqk', queries, key_rows, precision=HIGHEST)
    allowed = (query_items[:, None] == key_items[None, :])[None]
    scores = jnp.where(allowed, low_back(raw_scores) * scaling, NEGATIVE)
    row_top = jnp.ceil(lax.optimization_barrier(jnp.max(scores, axis=-1, keepdims=True)))
    weights = jnp.where(allowed, jnp.exp2(scores - row_top), 0.0)
    totals = lax.optimization_barrier(jnp.sum(weights, axis=-1))
    summed = jnp.einsum('hqk,khd->qhd', low(weights), value_rows, precision=HIGHEST)
    return low_back(summed) / jnp.transpose(totals)[:, :, None]

def blocked(queries, query_items, key_rows, value_rows, key_items):
    total_rows = queries.shape[0]
    blocksize = math.gcd(total_rows, 512)

    def one_block(pair):
        return attention(pair[0], pair[1], key_rows, value_rows, key_items)
    outputs = lax.map(jax.checkpoint(one_block), (queries.reshape(total_rows // blocksize, blocksize, queries.shape[1], queries.shape[2]), query_items.reshape(total_rows // blocksize, blocksize)))
    return outputs.reshape(queries.shape)

def reference(patches, cotangent, item_lengths, timesteps, patch_rows, patch_cols, conditioning, text_states, gain_attn, gain_ffn, query_gain, key_gain, text_key_gain, cross_gate, w_query, w_key, w_value, w_out, w_text_key, w_text_value, w_gate, w_up, w_down, w_ada, w_text):
    token_items = item_ids(item_lengths, TOK_DEV, N_DP)
    text_items = jnp.arange(NT, dtype=jnp.int32) // TTOK
    onehot = (token_items[:, None] == jnp.arange(NITEMS, dtype=jnp.int32)[None, :]).astype(jnp.float32)
    angles = rope_angles(patch_rows, patch_cols, HD)
    temb = time_embed(timesteps, D)

    def forward(inputs, cond, text, g_attn, g_ffn, q_gain, k_gain, tk_gain, gate_vec, wq_mat, wk_mat, wv_mat, wo_mat, wtk_mat, wtv_mat, wg_mat, wu_mat, wd_mat, wa_mat, wt_mat):
        embed = low(jax.nn.silu(cond + temb))
        modulation = dense(onehot, dense(embed, wa_mat))
        shift1, gate1, shift2, gate2 = jnp.split(modulation, 4, axis=1)
        hidden1 = low(rms_norm(inputs, g_attn) * (1.0 + shift1))
        q_pre = low_back(dense(hidden1, wq_mat)).reshape(TOKENS, HEADS, HD)
        k_pre = low_back(dense(hidden1, wk_mat)).reshape(TOKENS, HEADS, HD)
        queries = low(rotate(rms_norm(q_pre, q_gain), angles))
        key_rows = low(rotate(rms_norm(k_pre, k_gain), angles))
        value_rows = low_back(low(dense(hidden1, wv_mat))).reshape(TOKENS, HEADS, HD)
        words = low_back(low(dense(text, wt_mat.T)))
        tk_pre = low_back(dense(words, wtk_mat)).reshape(NT, HEADS, HD)
        text_keys = low(rms_norm(tk_pre, tk_gain))
        text_values = low_back(low(dense(words, wtv_mat))).reshape(NT, HEADS, HD)
        self_out = blocked(queries, token_items, key_rows, value_rows, token_items)
        cross_out = blocked(queries, token_items, text_keys, text_values, text_items)
        combined = low(self_out + jnp.tanh(gate_vec)[None, :, None] * cross_out).reshape(TOKENS, D)
        branch = low_back(dense(combined, wo_mat.T))
        middle = inputs + jnp.tanh(gate1) * branch
        hidden2 = low(rms_norm(middle, g_ffn) * (1.0 + shift2))
        gate_pre = low_back(dense(hidden2, wg_mat))
        up_pre = low_back(dense(hidden2, wu_mat))
        inner = low(jax.nn.silu(gate_pre) * up_pre)
        ffn_out = low_back(dense(inner, wd_mat.T))
        return middle + jnp.tanh(gate2) * ffn_out
    floats = [tensor.astype(jnp.float32) for tensor in (patches, conditioning, text_states, gain_attn, gain_ffn, query_gain, key_gain, text_key_gain, cross_gate, w_query, w_key, w_value, w_out, w_text_key, w_text_value, w_gate, w_up, w_down, w_ada, w_text)]
    result, pullback = jax.vjp(forward, *floats)
    grad_patches, grad_conditioning, grad_text, grad_gain_attn, grad_gain_ffn, grad_query_gain, grad_key_gain, grad_text_key_gain, grad_cross_gate, grad_w_query, grad_w_key, grad_w_value, grad_w_out, grad_w_text_key, grad_w_text_value, grad_w_gate, grad_w_up, grad_w_down, grad_w_ada, grad_w_text = pullback(cotangent.astype(jnp.float32))
    mixed = result.astype(jnp.bfloat16)
    return (mixed, grad_patches, grad_conditioning, grad_text, grad_gain_attn, grad_gain_ffn, grad_query_gain, grad_key_gain, grad_text_key_gain, grad_cross_gate, grad_w_query, grad_w_key, grad_w_value, grad_w_out, grad_w_text_key, grad_w_text_value, grad_w_gate, grad_w_up, grad_w_down, grad_w_ada, grad_w_text)
```

```python
import math

import jax
import jax.numpy as jnp
from jax import lax
from jax.sharding import PartitionSpec as P

TTOK = 256
HIGHEST = lax.Precision.HIGHEST
EPSILON = 1e-06
NEGATIVE = -1e30
SCORE_BASE = 1.4426950408889634
TWO_NATURAL = 0.6931471805599453
KEY_BLOCK = 1024
AXES = ("dp", "mp")
LANES = 128
F32 = jnp.float32
BF16 = jnp.bfloat16


def contract(left, right, pairing, precision=None):
    return lax.dot_general(
        left, right, (pairing, ((), ())), precision=precision, preferred_element_type=F32
    )


def multiply(left, right):
    return contract(left, right, ((1,), (0,)))


def multiply_trans(left, right, precision=None):
    return contract(left, right, ((1,), (1,)), precision)


def trans_multiply(left, right, precision=None):
    return contract(left, right, ((0,), (0,)), precision)


def time_embed(steps, model_width):
    halfway = model_width // 2
    frequency = jnp.exp(-math.log(10000.0) * jnp.arange(halfway, dtype=F32) / halfway)
    phases = steps.astype(F32)[:, None] * frequency[None, :]
    return jnp.concatenate([jnp.cos(phases), jnp.sin(phases)], axis=1)


def rope_angles(rows_pos, cols_pos, head_dim):
    quarter = head_dim // 4
    frequency = jnp.exp(-math.log(10000.0) * jnp.arange(quarter, dtype=F32) / quarter)
    return jnp.concatenate(
        [
            rows_pos.astype(F32)[:, None] * frequency[None, :],
            cols_pos.astype(F32)[:, None] * frequency[None, :],
        ],
        axis=1,
    )


def rotate(tensor, angles):
    quarter = tensor.shape[-1] // 4
    cosine = jnp.cos(angles)[:, None, :]
    sine = jnp.sin(angles)[:, None, :]
    first = tensor[..., :quarter]
    second = tensor[..., quarter : 2 * quarter]
    third = tensor[..., 2 * quarter : 3 * quarter]
    fourth = tensor[..., 3 * quarter :]
    row_cos, col_cos = (cosine[..., :quarter], cosine[..., quarter:])
    row_sin, col_sin = (sine[..., :quarter], sine[..., quarter:])
    return jnp.concatenate(
        [
            first * row_cos - second * row_sin,
            first * row_sin + second * row_cos,
            third * col_cos - fourth * col_sin,
            third * col_sin + fourth * col_cos,
        ],
        axis=-1,
    )


def item_ids(lengths, tok_dev, n_dev):
    wide_dev = tok_dev // 4
    boundary = jnp.cumsum(lengths)
    position = jnp.arange(tok_dev * n_dev, dtype=jnp.int32)
    within = position % tok_dev
    placed = position // tok_dev * (tok_dev - wide_dev) + within - wide_dev
    counted = jnp.sum((boundary[None, :] <= placed[:, None]).astype(jnp.int32), axis=1)
    return jnp.where(within < wide_dev, lengths.shape[0], counted)


def norm_fwd(values, gain_vec):
    scaling = lax.rsqrt(jnp.mean(values * values, axis=-1, keepdims=True) + EPSILON)
    return (values * scaling * gain_vec, scaling)


def norm_back(values, scaling, gain_vec, incoming):
    weighted = incoming * gain_vec
    inner_mean = jnp.mean(weighted * values, axis=-1, keepdims=True)
    return (
        scaling * weighted - values * scaling * scaling * scaling * inner_mean,
        incoming * values * scaling,
    )


def codes(index):
    data, model = divmod(index, 4)
    return (data // 4, data // 2 % 2, data % 2, model // 2, model % 2)


def place(dh, zl, dy, x, c):
    return ((dh * 2 + zl) * 2 + dy) * 4 + x * 2 + c


def move(values, where):
    count = lax.axis_size("dp") * lax.axis_size("mp")
    return lax.ppermute(values, AXES, [(i, place(*where(*codes(i)))) for i in range(count)])


def swap_roles(values):
    return move(values, lambda dh, zl, dy, x, c: (dh, c, dy, x, zl))


def other_core(values):
    return move(values, lambda dh, zl, dy, x, c: (dh, zl, dy, x, c ^ 1))


def other_y(values):
    return move(values, lambda dh, zl, dy, x, c: (dh, zl, dy ^ 1, x, c))


def other_high(values, high):
    return move(values, lambda dh, zl, dy, x, c: (dh ^ high, zl, dy, x, c))


def other_feature(values, other):
    return move(values, lambda dh, zl, dy, x, c: (dh, zl ^ (other & 1), dy, x ^ (other >> 1), c))


def pick(values, index, axis=0):
    return lax.dynamic_index_in_dim(values, index, axis, keepdims=False)


def after(values, *events):
    return lax.optimization_barrier((values, *events))[0]


class Place:
    def __init__(self):
        data, model = (lax.axis_index("dp"), lax.axis_index("mp"))
        self.data, self.model = (data, model)
        self.n_dp = lax.axis_size("dp")
        self.highs = self.n_dp // 4
        self.dh, self.zl, self.dy = (data // 4, data // 2 % 2, data % 2)
        self.x, self.c = (model // 2, model % 2)
        self.tokens = (self.dh * 2 + self.c) * 2 + self.dy
        self.features = self.x * 2 + self.zl


def unmix(parts, index):
    count = len(parts)
    ordered = []
    for spot in range(count):
        value = parts[spot]
        for other in range(1, count):
            value = jnp.where(index == other, parts[spot ^ other], value)
        ordered.append(value)
    return ordered


def gather_rows(shard, at, wait=()):
    rows, width = shard.shape
    half = rows // 2
    pair = shard.reshape(2, half, width)
    if wait:
        pair = after(pair, *wait)
    halves = (pick(pair, at.zl), pick(pair, 1 - at.zl))
    got = [
        move(
            halves[b],
            lambda dh, zl, dy, x, c, a=a, b=b: (dh ^ a, c, dy, x, zl ^ b),
        )
        for a in range(at.highs)
        for b in (0, 1)
    ]
    near = jnp.stack(got).reshape(at.highs, 2, half, width)
    beside = other_y(near)
    near_core = other_core(near)
    beside_core = other_core(beside)
    full = jnp.zeros((at.highs, 2, 2, 2, half, width), BF16)
    for block, dy, c in (
        (near, at.dy, at.c),
        (beside, 1 - at.dy, at.c),
        (near_core, at.dy, 1 - at.c),
        (beside_core, 1 - at.dy, 1 - at.c),
    ):
        for a in range(at.highs):
            for b in (0, 1):
                full = lax.dynamic_update_slice(
                    full,
                    block[a, b][None, None, None, None],
                    (at.dh ^ a, c ^ b, dy, c, 0, 0),
                )
    return (full.reshape(at.n_dp * rows, width), got)


def scatter_rows(grads, at):
    total, width = grads.shape
    half = total // at.n_dp // 2
    view = grads.astype(BF16).reshape(at.n_dp, 2, half, width)
    kept = pick(view, at.c, 1).astype(F32) + other_core(pick(view, 1 - at.c, 1)).astype(F32)
    kept = kept.reshape(at.highs, 2, 2, half, width)
    kept = pick(kept, at.dy, 2) + other_y(pick(kept, 1 - at.dy, 2).astype(BF16)).astype(F32)
    sums = [None, None]
    for a in range(at.highs):
        for b in (0, 1):
            piece = pick(pick(kept, at.dh ^ a), at.c ^ b).astype(BF16)
            got = move(
                piece, lambda dh, zl, dy, x, c, a=a, b=b: (dh ^ a, c ^ b, dy, x, zl)
            ).astype(F32)
            sums[b] = got if sums[b] is None else sums[b] + got
    return jnp.concatenate(unmix(sums, at.zl), axis=0)


def gather_tokens(block, at):
    near = [block] + [other_high(block, a) for a in range(1, at.highs)]
    near = jnp.stack(near)
    beside = other_y(near)
    return jnp.stack([near, beside, other_core(near), other_core(beside)])


def scatter_tokens(blocks, at):
    first = blocks[0].astype(F32) + other_core(blocks[2]).astype(F32)
    second = blocks[1].astype(F32) + other_core(blocks[3]).astype(F32)
    first = first + other_y(second.astype(BF16)).astype(F32)
    total = first[0]
    for a in range(1, at.highs):
        total = total + other_high(first[a].astype(BF16), a).astype(F32)
    return total


def relative_groups(at):
    return [
        ((at.dh ^ a) * 2 + (at.c ^ core)) * 2 + (at.dy ^ y)
        for core in (0, 1)
        for y in (0, 1)
        for a in range(at.highs)
    ]


def sum_quarters(part, at):
    rows, width = part.shape
    view = part.reshape(4, rows // 4, width)
    total = pick(view, at.features).astype(F32)
    for other in (1, 2, 3):
        total = total + other_feature(pick(view, at.features ^ other), other).astype(F32)
    return total


def gather_quarters(own, at):
    parts = [own] + [other_feature(own, other) for other in (1, 2, 3)]
    return jnp.concatenate(unmix(parts, at.features), axis=0)


def gather_output(own, at):
    near = [
        move(own, lambda dh, zl, dy, x, c, a=a: (dh, c, dy, x ^ a, zl)) for a in (0, 1)
    ]
    near = jnp.stack(unmix(near, at.x))
    far = other_core(near)
    first, second = (jnp.where(at.c == 0, near, far), jnp.where(at.c == 0, far, near))
    return jnp.stack([first, second], axis=1).reshape(4 * own.shape[0], own.shape[1])


def butterfly(values, at, data=True, model=True):
    bit = 1
    while data and bit < at.n_dp:
        values = values + lax.ppermute(values, "dp", [(i, i ^ bit) for i in range(at.n_dp)])
        bit *= 2
    for bit in (1, 2) if model else ():
        values = values + lax.ppermute(values, "mp", [(i, i ^ bit) for i in range(4)])
    return values


def rows_of(table, items):
    value = jnp.broadcast_to(table[0][None], (items.shape[0], table.shape[1]))
    for item in range(1, table.shape[0]):
        value = jnp.where(items[:, None] == item, table[item][None], value)
    return value


def touches(key_items, present):
    labels = jnp.arange(present.shape[0], dtype=jnp.int32)
    return jnp.any((key_items[:, None] == labels[None, :]) & present[None, :])


def block_scores(queries, key_block, query_items, key_items):
    scaling = queries.shape[-1] ** (-0.5) * SCORE_BASE
    raw_scores = jnp.einsum("qhd,khd->hqk", queries, key_block, preferred_element_type=F32)
    allowed = (query_items[:, None] == key_items[None, :])[None]
    return (jnp.where(allowed, raw_scores * scaling, NEGATIVE), allowed, scaling)


def absorb(state, queries, query_items, key_block, value_block, key_items):
    row_top, totals, summed = state
    scores, allowed, scaling = block_scores(queries, key_block, query_items, key_items)
    new_top = jnp.maximum(row_top, jnp.ceil(jnp.max(scores, axis=-1)))
    weights = jnp.where(allowed, jnp.exp2(scores - new_top[:, :, None]), 0.0)
    factor = jnp.exp2(row_top - new_top)
    totals = totals * factor + jnp.sum(weights, axis=-1)
    fresh = jnp.einsum(
        "hqk,khd->qhd",
        weights.astype(BF16),
        value_block,
        preferred_element_type=F32,
    )
    summed = summed * jnp.transpose(factor)[:, :, None] + fresh
    return (new_top, totals, summed)


def absorb_all(state, queries, query_items, key_rows, value_rows, key_items, present):
    key_count, row_width = key_rows.shape
    heads_local, head_dim = (queries.shape[1], queries.shape[2])
    blocksize = math.gcd(key_count, KEY_BLOCK)

    def absorb_advance(running, pieces):
        key_block, value_block, item_block = pieces

        def absorb_taken(current):
            return absorb(
                current,
                queries,
                query_items,
                key_block.reshape(blocksize, heads_local, head_dim),
                value_block.reshape(blocksize, heads_local, head_dim),
                item_block,
            )

        def absorb_passed(current):
            return current

        return (lax.cond(touches(item_block, present), absorb_taken, absorb_passed, running), None)

    running, _ = lax.scan(
        absorb_advance,
        state,
        (
            key_rows.reshape(key_count // blocksize, blocksize, row_width),
            value_rows.reshape(key_count // blocksize, blocksize, row_width),
            key_items.reshape(key_count // blocksize, blocksize),
        ),
    )
    return running


def release_all(
    queries,
    query_items,
    key_rows,
    value_rows,
    key_items,
    row_top,
    grad_summed,
    grad_totals,
    present,
):
    key_count, row_width = key_rows.shape
    heads_local, head_dim = (queries.shape[1], queries.shape[2])
    blocksize = math.gcd(key_count, KEY_BLOCK)

    def release_advance(grad_queries, pieces):
        key_block, value_block, item_block = pieces

        def release_taken(current):
            key_heads = key_block.reshape(blocksize, heads_local, head_dim)
            value_heads = value_block.reshape(blocksize, heads_local, head_dim)
            scores, allowed, scaling = block_scores(queries, key_heads, query_items, item_block)
            weights = jnp.where(allowed, jnp.exp2(scores - row_top[:, :, None]), 0.0)
            grad_weights = jnp.einsum(
                "qhd,khd->hqk", grad_summed, value_heads, preferred_element_type=F32
            )
            grad_raw = (
                weights * TWO_NATURAL * (grad_weights + grad_totals[:, :, None]) * scaling
            ).astype(BF16)
            updated = current + jnp.einsum(
                "hqk,khd->qhd", grad_raw, key_heads, preferred_element_type=F32
            )
            grad_keys = jnp.einsum("hqk,qhd->khd", grad_raw, queries, preferred_element_type=F32)
            grad_values = jnp.einsum(
                "hqk,qhd->khd",
                weights.astype(BF16),
                grad_summed,
                preferred_element_type=F32,
            )
            return (
                updated,
                jnp.concatenate(
                    [
                        grad_keys.reshape(blocksize, row_width),
                        grad_values.reshape(blocksize, row_width),
                    ],
                    axis=1,
                ).astype(BF16),
            )

        def release_passed(current):
            return (current, jnp.zeros((blocksize, 2 * row_width), BF16))

        return lax.cond(touches(item_block, present), release_taken, release_passed, grad_queries)

    grad_queries, key_terms = lax.scan(
        release_advance,
        jnp.zeros(queries.shape, F32),
        (
            key_rows.reshape(key_count // blocksize, blocksize, row_width),
            value_rows.reshape(key_count // blocksize, blocksize, row_width),
            key_items.reshape(key_count // blocksize, blocksize),
        ),
    )
    return (grad_queries, key_terms.reshape(key_count, 2 * row_width))


def head_grads(incoming, outputs, totals):
    totals_t = jnp.transpose(totals)[:, :, None]
    grad_summed = (incoming / totals_t).astype(BF16)
    grad_totals = -jnp.transpose(jnp.sum(incoming * outputs, axis=-1)) / totals
    return (grad_summed, grad_totals)


def interleave(arrays):
    pairs = arrays[0].shape[-1] // LANES
    return jnp.concatenate(
        [array[..., p * LANES : (p + 1) * LANES] for p in range(pairs) for array in arrays],
        axis=-1,
    )


def separate(array, kinds):
    pairs = array.shape[-1] // LANES // kinds
    return [
        jnp.concatenate(
            [
                array[..., (p * kinds + kind) * LANES : (p * kinds + kind + 1) * LANES]
                for p in range(pairs)
            ],
            axis=-1,
        )
        for kind in range(kinds)
    ]


def on_device(
    patches,
    cotangent,
    item_lengths,
    timesteps,
    patch_rows,
    patch_cols,
    conditioning,
    text_states,
    gain_attn,
    gain_ffn,
    query_gain,
    key_gain,
    text_key_gain,
    cross_gate,
    w_query,
    w_key,
    w_value,
    w_out,
    w_text_key,
    w_text_value,
    w_gate,
    w_up,
    w_down,
    w_ada,
    w_text,
):
    at = Place()
    tok_dev, model_width = patches.shape
    shard_rows = w_query.shape[0]
    head_dim = query_gain.shape[0]
    local_width = w_query.shape[1]
    heads_local = local_width // head_dim
    text_rows = text_states.shape[0]
    item_count = conditioning.shape[0]
    quarter = tok_dev // 4
    hidden_width = w_gate.shape[1]

    my_patches = swap_roles(patches)
    positions = swap_roles(jnp.stack([patch_rows, patch_cols]).astype(F32))
    my_text = swap_roles(text_states)
    embed_pre = conditioning.astype(F32) + time_embed(timesteps, model_width)
    embed = jax.nn.silu(embed_pre).astype(BF16)
    own_embed = lax.dynamic_slice_in_dim(embed, at.data * shard_rows, shard_rows, 1)
    gains = lax.dynamic_update_slice(
        jnp.zeros((2, model_width), F32),
        jnp.stack([gain_attn, gain_ffn]).astype(F32),
        (0, at.data * shard_rows),
    )
    head_sums = butterfly(
        jnp.concatenate([multiply(own_embed, w_ada), gains], axis=0), at, model=False
    )
    gain_attn32, gain_ffn32 = (head_sums[item_count], head_sums[item_count + 1])
    mod_part = head_sums[:item_count]
    shift1_t, gate1_t, shift2_t, gate2_t = unmix(
        [mod_part]
        + [
            lax.ppermute(mod_part, "mp", [(i, i ^ other) for i in range(4)])
            for other in (1, 2, 3)
        ],
        at.model,
    )

    full_qkv, sent = gather_rows(interleave([w_query, w_key, w_value]), at)
    my_cotangent = swap_roles(after(cotangent, *sent))
    full_text, sent_text = gather_rows(w_text, at, sent)
    full_tkv, sent_tkv = gather_rows(interleave([w_text_key, w_text_value]), at, sent)
    full_out, sent_out = gather_rows(w_out, at, sent_text)
    full_gu, sent_gu = gather_rows(
        jnp.concatenate([w_gate, w_up], axis=1), at, sent_tkv + sent_out
    )
    full_down, _ = gather_rows(w_down, at, sent_tkv + sent_out)

    token_items = item_ids(item_lengths, tok_dev, at.n_dp).reshape(at.n_dp, tok_dev)
    text_items = (jnp.arange(text_rows * at.n_dp, dtype=jnp.int32) // TTOK).reshape(
        at.n_dp, text_rows
    )
    groups = relative_groups(at)
    key_items = jnp.concatenate([pick(token_items, group) for group in groups])
    text_key_items = jnp.concatenate([pick(text_items, group) for group in groups])
    own_items = pick(token_items, at.tokens)
    item_labels = jnp.arange(item_count, dtype=jnp.int32)
    onehot = (own_items[:, None] == item_labels[None, :]).astype(F32)
    present = jnp.any(own_items[:, None] == item_labels[None, :], axis=0)
    few_items = lax.dynamic_slice_in_dim(own_items, at.features * quarter, quarter)
    few_onehot = lax.dynamic_slice_in_dim(onehot, at.features * quarter, quarter)

    shift1 = rows_of(shift1_t, own_items)
    inputs = my_patches.astype(F32)
    normed1, _ = norm_fwd(inputs, gain_attn32)
    hidden1 = (normed1 * (1.0 + shift1)).astype(BF16)

    angles = rope_angles(positions[0], positions[1], head_dim)
    qkv = multiply(hidden1, full_qkv)
    query_rows, key_pre_rows, value_pre = separate(qkv, 3)
    query_heads = query_rows.reshape(tok_dev, heads_local, head_dim)
    key_heads = key_pre_rows.reshape(tok_dev, heads_local, head_dim)
    query_gain32 = query_gain.astype(F32)
    key_gain32 = key_gain.astype(F32)
    text_gain32 = text_key_gain.astype(F32)
    query_normed, query_scale = norm_fwd(query_heads, query_gain32)
    key_normed, key_scale = norm_fwd(key_heads, key_gain32)
    queries = rotate(query_normed, angles).astype(BF16)
    key_rows = rotate(key_normed, angles).astype(BF16).reshape(tok_dev, local_width)
    own_kv = interleave([key_rows, value_pre.astype(BF16)])
    all_kv = gather_tokens(own_kv, at).reshape(at.n_dp * tok_dev, 2 * local_width)
    all_keys, all_values = separate(all_kv, 2)

    words = multiply_trans(my_text, full_text).astype(BF16)
    for other in (1, 2):
        words = (words.astype(F32) + other_feature(words, other).astype(F32)).astype(BF16)
    text_pre, text_value_pre = separate(multiply(words, full_tkv), 2)
    text_key_heads = text_pre.reshape(text_rows, heads_local, head_dim)
    text_key_normed, text_key_scale = norm_fwd(text_key_heads, text_gain32)
    own_text_kv = interleave(
        [
            text_key_normed.astype(BF16).reshape(text_rows, local_width),
            text_value_pre.astype(BF16),
        ]
    )
    all_text_kv = gather_tokens(own_text_kv, at).reshape(at.n_dp * text_rows, 2 * local_width)
    all_text_keys, all_text_values = separate(all_text_kv, 2)

    start_state = (
        jnp.full((heads_local, tok_dev), NEGATIVE, F32),
        jnp.zeros((heads_local, tok_dev), F32),
        jnp.zeros((tok_dev, heads_local, head_dim), F32),
    )
    self_top, self_totals, self_summed = absorb_all(
        start_state, queries, own_items, all_keys, all_values, key_items, present
    )
    cross_top, cross_totals, cross_summed = absorb_all(
        start_state, queries, own_items, all_text_keys, all_text_values, text_key_items, present
    )
    self_out = self_summed / jnp.transpose(self_totals)[:, :, None]
    cross_out = cross_summed / jnp.transpose(cross_totals)[:, :, None]
    gate_local = jnp.tanh(
        lax.dynamic_slice_in_dim(cross_gate.astype(F32), at.features * heads_local, heads_local)
    )
    combined = (
        (self_out + gate_local[None, :, None] * cross_out)
        .astype(BF16)
        .reshape(tok_dev, local_width)
    )
    few_inputs = lax.dynamic_slice_in_dim(inputs, at.features * quarter, quarter)
    few_normed1 = lax.dynamic_slice_in_dim(normed1, at.features * quarter, quarter)
    tanh_one = jnp.tanh(rows_of(gate1_t, few_items))
    tanh_two = jnp.tanh(rows_of(gate2_t, few_items))
    shift2 = rows_of(shift2_t, few_items)
    few_shift1 = rows_of(shift1_t, few_items)
    branch = sum_quarters(multiply_trans(combined, full_out).astype(BF16), at)
    middle = few_inputs + tanh_one * branch
    normed2, scale2 = norm_fwd(middle, gain_ffn32)
    hidden2 = gather_quarters((normed2 * (1.0 + shift2)).astype(BF16), at)
    gate_up = multiply(hidden2, full_gu)
    gate_pre, up_pre = (gate_up[:, :hidden_width], gate_up[:, hidden_width:])
    logistic = jax.nn.sigmoid(gate_pre)
    silu_gate = gate_pre * logistic
    inner_act = (silu_gate * up_pre).astype(BF16)

    grad_output = my_cotangent.astype(F32)
    few_output = lax.dynamic_slice_in_dim(grad_output, at.features * quarter, quarter)
    grad_ffn = (grad_output * rows_of(jnp.tanh(gate2_t), own_items)).astype(BF16)
    grad_inner = multiply(grad_ffn, full_down)
    grad_gate = (grad_inner * up_pre * logistic * (1.0 + gate_pre * (1.0 - logistic))).astype(BF16)
    grad_up = (grad_inner * silu_gate).astype(BF16)
    grad_gu = jnp.concatenate([grad_gate, grad_up], axis=1)
    grad_hidden2 = sum_quarters(multiply_trans(grad_gu, full_gu).astype(BF16), at)

    ffn_out = sum_quarters(multiply_trans(inner_act, full_down).astype(BF16), at)
    mixed_out = gather_output((middle + tanh_two * ffn_out).astype(BF16), at)

    grad_middle_norm, gain_ffn_term = norm_back(
        middle, scale2, gain_ffn32, grad_hidden2 * (1.0 + shift2)
    )
    grad_middle = few_output + grad_middle_norm
    grad_branch = gather_quarters((grad_middle * tanh_one).astype(BF16), at)
    grad_combined = multiply(grad_branch, full_out).reshape(tok_dev, heads_local, head_dim)
    grad_cross_out = grad_combined * gate_local[None, :, None]
    grad_gate_local = jnp.sum(grad_combined * cross_out, axis=(0, 2)) * (
        1.0 - gate_local * gate_local
    )
    grads_down = scatter_rows(trans_multiply(grad_ffn, inner_act), at)
    grads_gu = scatter_rows(trans_multiply(hidden2, grad_gu), at)
    grads_out = scatter_rows(trans_multiply(grad_branch, combined), at)

    self_grad_summed, self_grad_totals = head_grads(grad_combined, self_out, self_totals)
    cross_grad_summed, cross_grad_totals = head_grads(grad_cross_out, cross_out, cross_totals)
    self_grad_queries, shared_terms = release_all(
        queries,
        own_items,
        all_keys,
        all_values,
        key_items,
        self_top,
        self_grad_summed,
        self_grad_totals,
        present,
    )
    cross_grad_queries, text_terms = release_all(
        queries,
        own_items,
        all_text_keys,
        all_text_values,
        text_key_items,
        cross_top,
        cross_grad_summed,
        cross_grad_totals,
        present,
    )
    shared_back = scatter_tokens(
        shared_terms.reshape(4, at.highs, tok_dev, 2 * local_width), at
    )
    text_back = scatter_tokens(text_terms.reshape(4, at.highs, text_rows, 2 * local_width), at)
    grad_query_rot = rotate(self_grad_queries + cross_grad_queries, -angles)
    grad_query_heads, query_gain_term = norm_back(
        query_heads, query_scale, query_gain32, grad_query_rot
    )
    grad_query_pre = grad_query_heads.astype(BF16).reshape(tok_dev, local_width)
    grad_key_rot = rotate(
        shared_back[:, :local_width].reshape(tok_dev, heads_local, head_dim), -angles
    )
    grad_key_heads, key_gain_term = norm_back(key_heads, key_scale, key_gain32, grad_key_rot)
    grad_key_pre = grad_key_heads.astype(BF16).reshape(tok_dev, local_width)
    grad_values = shared_back[:, local_width:].astype(BF16)
    grad_qkv = interleave([grad_query_pre, grad_key_pre, grad_values])
    grad_text_heads, text_gain_term = norm_back(
        text_key_heads,
        text_key_scale,
        text_gain32,
        text_back[:, :local_width].reshape(text_rows, heads_local, head_dim),
    )
    grad_tkv = interleave(
        [
            grad_text_heads.astype(BF16).reshape(text_rows, local_width),
            text_back[:, local_width:].astype(BF16),
        ]
    )
    grad_hidden1 = sum_quarters(multiply_trans(grad_qkv, full_qkv).astype(BF16), at)
    grad_words = multiply_trans(grad_tkv, full_tkv).astype(BF16)
    for other in (1, 2):
        grad_words = (
            grad_words.astype(F32) + other_feature(grad_words, other).astype(F32)
        ).astype(BF16)

    few_scale1 = lax.rsqrt(jnp.mean(few_inputs * few_inputs, axis=-1, keepdims=True) + EPSILON)
    grad_inputs_norm, gain_attn_term = norm_back(
        few_inputs, few_scale1, gain_attn32, grad_hidden1 * (1.0 + few_shift1)
    )
    grad_patches = gather_output((grad_middle + grad_inputs_norm).astype(BF16), at).astype(F32)
    grad_text = swap_roles(multiply(grad_words, full_text).astype(BF16)).astype(F32)
    grads_qkv = scatter_rows(trans_multiply(hidden1, grad_qkv), at)
    grads_tkv = scatter_rows(trans_multiply(words, grad_tkv), at)
    grads_text = scatter_rows(trans_multiply(grad_words, my_text), at)

    def item_sums(rows):
        return trans_multiply(few_onehot, rows, HIGHEST)

    early = butterfly(
        jnp.concatenate(
            [
                item_sums(grad_middle * branch * (1.0 - tanh_one * tanh_one)),
                item_sums(grad_hidden2 * normed2),
                item_sums(few_output * ffn_out * (1.0 - tanh_two * tanh_two)),
                jnp.sum(gain_ffn_term, axis=0, keepdims=True),
            ],
            axis=0,
        ),
        at,
    )
    gate_full = lax.dynamic_update_slice_in_dim(
        jnp.zeros((cross_gate.shape[0],), F32),
        grad_gate_local,
        at.features * heads_local,
        0,
    )
    small = jnp.concatenate(
        [
            jnp.sum(query_gain_term, axis=(0, 1)),
            jnp.sum(key_gain_term, axis=(0, 1)),
            jnp.sum(text_gain_term, axis=(0, 1)),
            gate_full,
        ]
    )
    small = jnp.pad(small, (0, model_width - small.shape[0]))
    late = butterfly(
        jnp.concatenate(
            [
                item_sums(grad_hidden1 * few_normed1),
                jnp.sum(gain_attn_term, axis=0, keepdims=True),
                small[None],
            ],
            axis=0,
        ),
        at,
    )
    grad_modulation = jnp.stack(
        [late[:item_count]] + [early[i * item_count : (i + 1) * item_count] for i in range(3)]
    )
    grad_mod_own = pick(grad_modulation, at.model)
    small = late[item_count + 1]
    grad_ada = trans_multiply(own_embed.astype(F32), grad_mod_own, HIGHEST)
    grad_embed_part = multiply_trans(grad_mod_own, w_ada.astype(F32), HIGHEST)
    grad_embed = butterfly(
        lax.dynamic_update_slice(
            jnp.zeros((item_count, model_width), F32),
            grad_embed_part,
            (0, at.data * shard_rows),
        ),
        at,
    )
    embed_logistic = jax.nn.sigmoid(embed_pre)
    grad_conditioning = grad_embed * embed_logistic * (1.0 + embed_pre * (1.0 - embed_logistic))
    own_gain = lambda row: lax.dynamic_slice_in_dim(row, at.data * shard_rows, shard_rows)
    grad_wq, grad_wk, grad_wv = separate(grads_qkv, 3)
    grad_wtk, grad_wtv = separate(grads_tkv, 2)
    return (
        mixed_out,
        grad_patches,
        grad_conditioning,
        grad_text,
        own_gain(late[item_count]),
        own_gain(early[3 * item_count]),
        small[:head_dim],
        small[head_dim : 2 * head_dim],
        small[2 * head_dim : 3 * head_dim],
        small[3 * head_dim : 3 * head_dim + cross_gate.shape[0]],
        grad_wq,
        grad_wk,
        grad_wv,
        grads_out,
        grad_wtk,
        grad_wtv,
        grads_gu[:, :hidden_width],
        grads_gu[:, hidden_width:],
        grads_down,
        grad_ada,
        grads_text,
    )


def solution(mesh):
    rows, both, one = (P("dp", None), P("dp", "mp"), P("dp"))
    whole = P()
    in_specs = (
        (rows, rows, whole, whole, one, one, whole, both, one, one)
        + (whole,) * 4
        + (both,) * 11
    )
    out_specs = (
        (rows, rows, whole, both, one, one) + (whole,) * 4 + (both,) * 11
    )
    return jax.shard_map(
        on_device, mesh=mesh, in_specs=in_specs, out_specs=out_specs, check_vma=False
    )
```

```python
import functools
import math

import jax
import jax.numpy as jnp
from jax import lax
from jax.experimental import pallas as pl
from jax.experimental.pallas import tpu as pltpu
from jax.sharding import PartitionSpec as P

TTOK = 256
HIGHEST = lax.Precision.HIGHEST
EPSILON = 1e-06
SCORE_BASE = 1.4426950408889634
TWO_NATURAL = 0.6931471805599453
AXES = ("dp", "mp")
LANES = 128
F32 = jnp.float32
BF16 = jnp.bfloat16


def contract(left, right, pairing, precision=None):
    return lax.dot_general(
        left, right, (pairing, ((), ())), precision=precision, preferred_element_type=F32
    )


def multiply(left, right):
    return contract(left, right, ((1,), (0,)))


def multiply_trans(left, right, precision=None):
    return contract(left, right, ((1,), (1,)), precision)


def trans_multiply(left, right, precision=None):
    return contract(left, right, ((0,), (0,)), precision)


def time_embed(steps, model_width):
    halfway = model_width // 2
    frequency = jnp.exp(-math.log(10000.0) * jnp.arange(halfway, dtype=F32) / halfway)
    phases = steps.astype(F32)[:, None] * frequency[None, :]
    return jnp.concatenate([jnp.cos(phases), jnp.sin(phases)], axis=1)


def rope_angles(rows_pos, cols_pos, head_dim):
    quarter = head_dim // 4
    frequency = jnp.exp(-math.log(10000.0) * jnp.arange(quarter, dtype=F32) / quarter)
    return jnp.concatenate(
        [
            rows_pos.astype(F32)[:, None] * frequency[None, :],
            cols_pos.astype(F32)[:, None] * frequency[None, :],
        ],
        axis=1,
    )


def item_ids(lengths, tok_dev, n_dev):
    wide_dev = tok_dev // 4
    boundary = jnp.cumsum(lengths)
    position = jnp.arange(tok_dev * n_dev, dtype=jnp.int32)
    within = position % tok_dev
    placed = position // tok_dev * (tok_dev - wide_dev) + within - wide_dev
    counted = jnp.sum((boundary[None, :] <= placed[:, None]).astype(jnp.int32), axis=1)
    return jnp.where(within < wide_dev, lengths.shape[0], counted)


def norm_fwd(values, gain_vec):
    scaling = lax.rsqrt(jnp.mean(values * values, axis=-1, keepdims=True) + EPSILON)
    return (values * scaling * gain_vec, scaling)


def norm_back(values, scaling, gain_vec, incoming):
    weighted = incoming * gain_vec
    inner_mean = jnp.mean(weighted * values, axis=-1, keepdims=True)
    return (
        scaling * weighted - values * scaling * scaling * scaling * inner_mean,
        incoming * values * scaling,
    )


def codes(index):
    data, model = divmod(index, 4)
    return (data // 4, data // 2 % 2, data % 2, model // 2, model % 2)


def place(dh, zl, dy, x, c):
    return ((dh * 2 + zl) * 2 + dy) * 4 + x * 2 + c


def move(values, where):
    count = lax.axis_size("dp") * lax.axis_size("mp")
    return lax.ppermute(values, AXES, [(i, place(*where(*codes(i)))) for i in range(count)])


def swap_roles(values):
    return move(values, lambda dh, zl, dy, x, c: (dh, c, dy, x, zl))


def other_core(values):
    return move(values, lambda dh, zl, dy, x, c: (dh, zl, dy, x, c ^ 1))


def other_y(values):
    return move(values, lambda dh, zl, dy, x, c: (dh, zl, dy ^ 1, x, c))


def other_high(values, high):
    return move(values, lambda dh, zl, dy, x, c: (dh ^ high, zl, dy, x, c))


def other_feature(values, other):
    return move(values, lambda dh, zl, dy, x, c: (dh, zl ^ (other & 1), dy, x ^ (other >> 1), c))


def pick(values, index, axis=0):
    return lax.dynamic_index_in_dim(values, index, axis, keepdims=False)


def after(values, *events):
    return lax.optimization_barrier((values, *events))[0]


class Place:
    def __init__(self):
        data, model = (lax.axis_index("dp"), lax.axis_index("mp"))
        self.data, self.model = (data, model)
        self.n_dp = lax.axis_size("dp")
        self.highs = self.n_dp // 4
        self.dh, self.zl, self.dy = (data // 4, data // 2 % 2, data % 2)
        self.x, self.c = (model // 2, model % 2)
        self.tokens = (self.dh * 2 + self.c) * 2 + self.dy
        self.features = self.x * 2 + self.zl


def unmix(parts, index):
    count = len(parts)
    ordered = []
    for spot in range(count):
        value = parts[spot]
        for other in range(1, count):
            value = jnp.where(index == other, parts[spot ^ other], value)
        ordered.append(value)
    return ordered


def assemble_kernel(highs, near, beside, near_core, beside_core, full):
    data, core = (lax.axis_index("dp"), lax.axis_index("mp") % 2)
    high, y = (data // 4, data % 2)
    for block, from_y, from_core in (
        (near, y, core),
        (beside, y ^ 1, core),
        (near_core, y, core ^ 1),
        (beside_core, y ^ 1, core ^ 1),
    ):
        for a in range(highs):
            for b in (0, 1):
                full[high ^ a, from_core ^ b, from_y, from_core] = block[a, b]


def assemble(near, beside, near_core, beside_core):
    highs, _, half, width = near.shape
    step = math.gcd(width, 512) if width % 384 else 384
    part = pl.BlockSpec((highs, 2, half, step), lambda i: (0, 0, 0, i))
    return pl.pallas_call(
        functools.partial(assemble_kernel, highs),
        grid=(width // step,),
        in_specs=[part] * 4,
        out_specs=pl.BlockSpec((highs, 2, 2, 2, half, step), lambda i: (0,) * 5 + (i,)),
        out_shape=jax.ShapeDtypeStruct((highs, 2, 2, 2, half, width), near.dtype),
        compiler_params=params(),
        cost_estimate=pl.CostEstimate(
            flops=0, bytes_accessed=32 * highs * half * width, transcendentals=0
        ),
        name="assemble",
    )(near, beside, near_core, beside_core)


class Events:
    def __init__(self, **events):
        self.__dict__.update(events)


def gather_rows(shard, at, z_wait=(), y_wait=()):
    rows, width = shard.shape
    half = rows // 2
    pair = shard.reshape(2, half, width)
    if z_wait:
        pair = after(pair, *z_wait)
    pieces = (pick(pair, at.zl), pick(pair, 1 - at.zl))
    got = [
        move(
            pieces[b],
            lambda dh, zl, dy, x, c, a=a, b=b: (dh ^ a, c, dy, x, zl ^ b),
        )
        for a in range(at.highs)
        for b in (0, 1)
    ]
    near = jnp.stack(got).reshape(at.highs, 2, half, width)
    if y_wait:
        near = after(near, *y_wait)
    beside = other_y(near)
    near_core = other_core(near)
    beside_core = other_core(beside)
    full = assemble(near, beside, near_core, beside_core)
    return (
        full.reshape(at.n_dp * rows, width),
        Events(z=got, y=[beside], c=[beside_core]),
    )


def scatter_rows(grads, at, c_wait=(), y_wait=(), z_wait=()):
    total, width = grads.shape
    half = total // at.n_dp // 2
    view = grads.astype(BF16).reshape(at.n_dp, 2, half, width)
    if c_wait:
        view = after(view, *c_wait)
    from_core = other_core(pick(view, 1 - at.c, 1))
    kept = pick(view, at.c, 1).astype(F32) + from_core.astype(F32)
    kept = kept.reshape(at.highs, 2, 2, half, width)
    if y_wait:
        kept = after(kept, *y_wait)
    from_y = other_y(pick(kept, 1 - at.dy, 2).astype(BF16))
    kept = pick(kept, at.dy, 2) + from_y.astype(F32)
    if z_wait:
        kept = after(kept, *z_wait)
    sums, got = ([None, None], [])
    for a in range(at.highs):
        for b in (0, 1):
            piece = pick(pick(kept, at.dh ^ a), at.c ^ b).astype(BF16)
            got.append(
                move(piece, lambda dh, zl, dy, x, c, a=a, b=b: (dh ^ a, c ^ b, dy, x, zl))
            )
            fresh = got[-1].astype(F32)
            sums[b] = fresh if sums[b] is None else sums[b] + fresh
    return (
        jnp.concatenate(unmix(sums, at.zl), axis=0),
        Events(c=[from_core], y=[from_y], z=got),
    )


def gather_tokens(block, at):
    far = [other_high(block, a) for a in range(1, at.highs)]
    near = jnp.stack([block] + far)
    beside = other_y(near)
    return ([near, beside, other_core(near), other_core(beside)], Events(z=far, y=[beside]))


def scatter_tokens(blocks, at):
    first = blocks[0].astype(F32) + other_core(blocks[2]).astype(F32)
    second = blocks[1].astype(F32) + other_core(blocks[3]).astype(F32)
    from_y = other_y(second.astype(BF16))
    first = first + from_y.astype(F32)
    total, got = (first[0], [])
    for a in range(1, at.highs):
        got.append(other_high(first[a].astype(BF16), a))
        total = total + got[-1].astype(F32)
    return (total, Events(y=[from_y], z=got))


def relative_groups(at):
    return [
        ((at.dh ^ a) * 2 + (at.c ^ core)) * 2 + (at.dy ^ y)
        for core in (0, 1)
        for y in (0, 1)
        for a in range(at.highs)
    ]


def sum_quarters(part, at):
    rows, width = part.shape
    view = part.reshape(4, rows // 4, width)
    total = pick(view, at.features).astype(F32)
    for other in (1, 2, 3):
        total = total + other_feature(pick(view, at.features ^ other), other).astype(F32)
    return total


def gather_quarters(own, at):
    parts = [own] + [other_feature(own, other) for other in (1, 2, 3)]
    return jnp.concatenate(unmix(parts, at.features), axis=0)


def gather_output(own, at):
    near = [
        move(own, lambda dh, zl, dy, x, c, a=a: (dh, c, dy, x ^ a, zl)) for a in (0, 1)
    ]
    near = jnp.stack(unmix(near, at.x))
    far = other_core(near)
    first, second = (jnp.where(at.c == 0, near, far), jnp.where(at.c == 0, far, near))
    return jnp.stack([first, second], axis=1).reshape(4 * own.shape[0], own.shape[1])


def butterfly(values, at, data=True, model=True):
    bit = 1
    while data and bit < at.n_dp:
        values = values + lax.ppermute(values, "dp", [(i, i ^ bit) for i in range(at.n_dp)])
        bit *= 2
    for bit in (1, 2) if model else ():
        values = values + lax.ppermute(values, "mp", [(i, i ^ bit) for i in range(4)])
    return values


def rows_of(table, items):
    value = jnp.broadcast_to(table[0][None], (items.shape[0], table.shape[1]))
    for item in range(1, table.shape[0]):
        value = jnp.where(items[:, None] == item, table[item][None], value)
    return value


def halves(values):
    lane = lax.broadcasted_iota(jnp.int32, (1, LANES), 1)
    low = lane < LANES // 2
    zero = jnp.zeros((), values.dtype)
    return (jnp.where(low, values, zero), jnp.where(low, zero, values))


def pair_select(first, second):
    lane = lax.broadcasted_iota(jnp.int32, (1, LANES), 1)
    return jnp.where(lane < LANES // 2, first, second)


def pair_mean(values):
    low, high = halves(values)
    return pair_select(
        jnp.sum(low, axis=-1, keepdims=True), jnp.sum(high, axis=-1, keepdims=True)
    ) * (2.0 / LANES)


def partner(values):
    lane = lax.broadcasted_iota(jnp.int32, (1, LANES), 1)
    return jnp.where(
        lane % 32 < 16, pltpu.roll(values, LANES - 16, 1), pltpu.roll(values, 16, 1)
    )


def pair_norm(values, gain):
    return values * lax.rsqrt(pair_mean(values * values) + EPSILON) * gain


def pair_norm_back(values, gain, incoming):
    scaling = lax.rsqrt(pair_mean(values * values) + EPSILON)
    weighted = incoming * gain
    inner_mean = pair_mean(weighted * values)
    return (
        scaling * weighted - values * scaling * scaling * scaling * inner_mean,
        jnp.sum(incoming * values * scaling, axis=0, keepdims=True),
    )


def params(megabytes=48):
    return pltpu.CompilerParams(vmem_limit_bytes=megabytes * 1024 * 1024)


def whole(shape):
    return pl.BlockSpec(shape, lambda p, *_: (0,) * len(shape))


def columns(rows, width):
    return pl.BlockSpec((rows, width), lambda p, *_: (0, p))


def qkv_kernel(x, w, cosine, sine, q_gain, k_gain, q_pre, k_pre, q_out, kv_out):
    made = jnp.dot(x[...], w[...], preferred_element_type=F32)
    query, key = (made[:, :LANES], made[:, LANES : 2 * LANES])
    q_pre[...] = query
    k_pre[...] = key
    query = pair_norm(query, q_gain[...])
    key = pair_norm(key, k_gain[...])
    q_out[...] = (query * cosine[...] + partner(query) * sine[...]).astype(BF16)
    kv_out[:, :LANES] = (key * cosine[...] + partner(key) * sine[...]).astype(BF16)
    kv_out[:, LANES:] = made[:, 2 * LANES :].astype(BF16)


def qkv_call(hidden, weights, cosine, sine, q_gain, k_gain):
    rows, depth = hidden.shape
    pairs = weights.shape[1] // (3 * LANES)
    width = pairs * LANES
    return pl.pallas_call(
        qkv_kernel,
        grid=(pairs,),
        in_specs=[
            whole((rows, depth)),
            columns(depth, 3 * LANES),
            whole((rows, LANES)),
            whole((rows, LANES)),
            whole((1, LANES)),
            whole((1, LANES)),
        ],
        out_specs=[columns(rows, LANES)] * 3 + [columns(rows, 2 * LANES)],
        out_shape=[
            jax.ShapeDtypeStruct((rows, width), F32),
            jax.ShapeDtypeStruct((rows, width), F32),
            jax.ShapeDtypeStruct((rows, width), BF16),
            jax.ShapeDtypeStruct((rows, 2 * width), BF16),
        ],
        compiler_params=params(),
        cost_estimate=pl.CostEstimate(
            flops=6 * rows * depth * width, bytes_accessed=8_000_000, transcendentals=0
        ),
        name="qkv",
    )(hidden, weights, cosine, sine, q_gain, k_gain)


def qkv_back_kernel(dq, dkv, q_pre, k_pre, cosine, sine, q_gain, k_gain, out, dq_gain, dk_gain):
    query, key = (dq[...], dkv[:, :LANES])
    query = query * cosine[...] - partner(query) * sine[...]
    key = key * cosine[...] - partner(key) * sine[...]
    query, dq_gain[...] = pair_norm_back(q_pre[...], q_gain[...], query)
    key, dk_gain[...] = pair_norm_back(k_pre[...], k_gain[...], key)
    out[:, :LANES] = query.astype(BF16)
    out[:, LANES : 2 * LANES] = key.astype(BF16)
    out[:, 2 * LANES :] = dkv[:, LANES:].astype(BF16)


def qkv_back_call(dq, dkv, q_pre, k_pre, cosine, sine, q_gain, k_gain):
    rows, width = dq.shape
    pairs = width // LANES
    return pl.pallas_call(
        qkv_back_kernel,
        grid=(pairs,),
        in_specs=[columns(rows, LANES), columns(rows, 2 * LANES)]
        + [columns(rows, LANES)] * 2
        + [whole((rows, LANES))] * 2
        + [whole((1, LANES))] * 2,
        out_specs=[columns(rows, 3 * LANES), columns(1, LANES), columns(1, LANES)],
        out_shape=[
            jax.ShapeDtypeStruct((rows, 3 * width), BF16),
            jax.ShapeDtypeStruct((1, width), F32),
            jax.ShapeDtypeStruct((1, width), F32),
        ],
        compiler_params=params(),
        cost_estimate=pl.CostEstimate(flops=0, bytes_accessed=8_000_000, transcendentals=0),
        name="qkv_back",
    )(dq, dkv, q_pre, k_pre, cosine, sine, q_gain, k_gain)


def text_kernel(x, w, gain, k_pre, kv_out):
    made = jnp.dot(x[...], w[...], preferred_element_type=F32)
    k_pre[...] = made[:, :LANES]
    kv_out[:, :LANES] = pair_norm(made[:, :LANES], gain[...]).astype(BF16)
    kv_out[:, LANES:] = made[:, LANES:].astype(BF16)


def text_call(words, weights, gain):
    rows, depth = words.shape
    width = weights.shape[1] // 2
    return pl.pallas_call(
        text_kernel,
        grid=(width // LANES,),
        in_specs=[whole((rows, depth)), columns(depth, 2 * LANES), whole((1, LANES))],
        out_specs=[columns(rows, LANES), columns(rows, 2 * LANES)],
        out_shape=[
            jax.ShapeDtypeStruct((rows, width), F32),
            jax.ShapeDtypeStruct((rows, 2 * width), BF16),
        ],
        compiler_params=params(),
        cost_estimate=pl.CostEstimate(
            flops=4 * rows * depth * width, bytes_accessed=4_000_000, transcendentals=0
        ),
        name="text_kv",
    )(words, weights, gain)


def text_back_kernel(dkv, k_pre, gain, out, d_gain):
    key, d_gain[...] = pair_norm_back(k_pre[...], gain[...], dkv[:, :LANES])
    out[:, :LANES] = key.astype(BF16)
    out[:, LANES:] = dkv[:, LANES:].astype(BF16)


def text_back_call(dkv, k_pre, gain):
    rows, width = k_pre.shape
    return pl.pallas_call(
        text_back_kernel,
        grid=(width // LANES,),
        in_specs=[columns(rows, 2 * LANES), columns(rows, LANES), whole((1, LANES))],
        out_specs=[columns(rows, 2 * LANES), columns(1, LANES)],
        out_shape=[
            jax.ShapeDtypeStruct((rows, 2 * width), BF16),
            jax.ShapeDtypeStruct((1, width), F32),
        ],
        compiler_params=params(),
        cost_estimate=pl.CostEstimate(flops=0, bytes_accessed=2_000_000, transcendentals=0),
        name="text_kv_back",
    )(dkv, k_pre, gain)


class Meta:
    def __init__(self, ref, runs, blocks, wide, text_rows):
        self.ref, self.runs, self.blocks = (ref, runs, blocks)
        self.wide, self.text_rows = (wide, text_rows)

    def group(self, block):
        return self.ref[self.runs + block]

    def own(self):
        return self.ref[self.runs + self.blocks]

    def self_flag(self, block):
        return self.ref[self.runs + self.blocks + 1 + block]

    def cross_flag(self, block):
        return self.ref[self.runs + 2 * self.blocks + 1 + block]

    def run_items(self, group, count, axis):
        shape = (count, 1) if axis == 0 else (1, count)
        spot = lax.broadcasted_iota(jnp.int32, shape, axis) + group * count
        item = jnp.zeros(shape, jnp.int32)
        for run in range(self.runs):
            item = item + (spot >= self.ref[run]).astype(jnp.int32)
        return item

    def all_items(self, group, count, axis):
        shape = (count, 1) if axis == 0 else (1, count)
        row = lax.broadcasted_iota(jnp.int32, shape, axis)
        spot = row - self.wide + group * (count - self.wide)
        item = jnp.zeros(shape, jnp.int32)
        for run in range(self.runs):
            item = item + (spot >= self.ref[run]).astype(jnp.int32)
        return jnp.where(row < self.wide, self.runs, item)

    def text_items(self, group, axis):
        shape = (self.text_rows, 1) if axis == 0 else (1, self.text_rows)
        return (lax.broadcasted_iota(jnp.int32, shape, axis) + group * self.text_rows) // TTOK


def nt_dot(left, right):
    return lax.dot_general(left, right, (((1,), (1,)), ((), ())), preferred_element_type=F32)


def nn_dot(left, right):
    return jnp.dot(left, right, preferred_element_type=F32)


def tn_dot(left, right):
    return lax.dot_general(left, right, (((0,), (0,)), ((), ())), preferred_element_type=F32)


SCALING = 64 ** (-0.5) * SCORE_BASE
GRAD_SCALING = 64 ** (-0.5) * SCORE_BASE * TWO_NATURAL


def attend(query, key, value, allowed):
    sums, totals = (None, [])
    for query_head, value_head in zip(halves(query), halves(value)):
        weights = jnp.exp2(nt_dot(query_head, key) * SCALING)
        if allowed is not None:
            weights = jnp.where(allowed, weights, 0.0)
        totals.append(jnp.sum(weights, axis=-1, keepdims=True))
        fresh = nn_dot(weights.astype(BF16), value_head)
        sums = fresh if sums is None else sums + fresh
    return (sums, pair_select(*totals))


def attention_kernel(
    runs, highs, wide, text_rows, ref, q, kv0, kv1, kv2, kv3, t0, t1, t2, t3, gate,
    combined, self_out, cross_out, self_total, cross_total,
):
    meta = Meta(ref, runs, 4 * highs, wide, text_rows)
    rows = q.shape[0]
    run_rows = rows - wide
    self_out[...] = jnp.zeros(self_out.shape, F32)
    self_total[...] = jnp.zeros(self_total.shape, F32)
    cross_out[...] = jnp.zeros(cross_out.shape, F32)
    cross_total[...] = jnp.zeros(cross_total.shape, F32)
    own = meta.own()
    run_items = meta.run_items(own, run_rows, 0)
    all_items = meta.all_items(own, rows, 0)
    for number, (kv, text) in enumerate(((kv0, t0), (kv1, t1), (kv2, t2), (kv3, t3))):
        keys = kv[:, :wide, :LANES].reshape(highs * wide, LANES)
        values = kv[:, :wide, LANES:].reshape(highs * wide, LANES)
        sums, totals = attend(q[:wide, :], keys, values, None)
        self_out[:wide, :] += sums
        self_total[:wide, :] += totals

        @pl.loop(0, highs)
        def _(high, number=number, kv=kv, text=text):
            block = number * highs + high

            @pl.when(meta.self_flag(block) > 0)
            def _():
                allowed = run_items == meta.run_items(meta.group(block), run_rows, 1)
                sums, totals = attend(
                    q[wide:, :], kv[high, wide:, :LANES], kv[high, wide:, LANES:], allowed
                )
                self_out[wide:, :] += sums
                self_total[wide:, :] += totals

            @pl.when(meta.cross_flag(block) > 0)
            def _():
                allowed = all_items == meta.text_items(meta.group(block), 1)
                sums, totals = attend(
                    q[...], text[high, :, :LANES], text[high, :, LANES:], allowed
                )
                cross_out[...] += sums
                cross_total[...] += totals

    ours = self_out[...] / self_total[...]
    across = cross_out[...] / cross_total[...]
    self_out[...] = ours
    cross_out[...] = across
    combined[...] = (ours + gate[...] * across).astype(BF16)


def attention_call(meta, queries, kvs, texts, gate, runs):
    rows, width = queries.shape
    highs, text_rows = (kvs[0].shape[0], texts[0].shape[1])
    wide = rows // 4
    kv_spec = pl.BlockSpec((highs, rows, 2 * LANES), lambda p, *_: (0, 0, p))
    text_spec = pl.BlockSpec((highs, text_rows, 2 * LANES), lambda p, *_: (0, 0, p))
    float_out = jax.ShapeDtypeStruct((rows, width), F32)
    return pl.pallas_call(
        functools.partial(attention_kernel, runs, highs, wide, text_rows),
        grid_spec=pltpu.PrefetchScalarGridSpec(
            num_scalar_prefetch=1,
            grid=(width // LANES,),
            in_specs=[columns(rows, LANES)]
            + [kv_spec] * 4
            + [text_spec] * 4
            + [columns(1, LANES)],
            out_specs=[columns(rows, LANES)] * 5,
        ),
        out_shape=[jax.ShapeDtypeStruct((rows, width), BF16)] + [float_out] * 4,
        compiler_params=params(56),
        cost_estimate=pl.CostEstimate(
            flops=20_000_000_000, bytes_accessed=20_000_000, transcendentals=0
        ),
        name="attention",
    )(meta, queries, *kvs, *texts, gate)


def attend_back(query, grad, less, key, value, allowed):
    d_key, d_value, d_query = (None, None, None)
    for query_head, grad_head, less_head, key_head in zip(
        halves(query), halves(grad), less, halves(key)
    ):
        weights = jnp.exp2(nt_dot(key, query_head) * SCALING)
        if allowed is not None:
            weights = jnp.where(allowed, weights, 0.0)
        raw = weights * (nt_dot(value, grad_head) + less_head) * GRAD_SCALING
        raw = raw.astype(BF16)
        terms = (
            nn_dot(raw, query_head),
            nn_dot(weights.astype(BF16), grad_head),
            tn_dot(raw, key_head),
        )
        if d_key is None:
            d_key, d_value, d_query = terms
        else:
            d_key, d_value, d_query = (
                d_key + terms[0],
                d_value + terms[1],
                d_query + terms[2],
            )
    return (d_key.astype(BF16), d_value.astype(BF16), d_query)


def attention_back_kernel(
    runs, highs, wide, text_rows, ref, q, g, self_out, cross_out, self_total, cross_total, gate,
    kv0, kv1, kv2, kv3, t0, t1, t2, t3,
    dq, dkv0, dkv1, dkv2, dkv3, dt0, dt1, dt2, dt3, d_gate, self_grad, cross_grad,
):
    meta = Meta(ref, runs, 4 * highs, wide, text_rows)
    rows = q.shape[0]
    run_rows = rows - wide
    own = meta.own()
    run_items = meta.run_items(own, run_rows, 1)
    all_items = meta.all_items(own, rows, 1)
    incoming = g[...]
    d_gate[...] = jnp.sum(incoming * cross_out[...], axis=0, keepdims=True)
    scaled = incoming / self_total[...]
    self_grad[...] = scaled.astype(BF16)
    turned = jnp.transpose(scaled * self_out[...])
    self_less = (
        -jnp.sum(turned[: LANES // 2], axis=0, keepdims=True),
        -jnp.sum(turned[LANES // 2 :], axis=0, keepdims=True),
    )
    scaled = incoming * gate[...] / cross_total[...]
    cross_grad[...] = scaled.astype(BF16)
    turned = jnp.transpose(scaled * cross_out[...])
    cross_less = (
        -jnp.sum(turned[: LANES // 2], axis=0, keepdims=True),
        -jnp.sum(turned[LANES // 2 :], axis=0, keepdims=True),
    )
    wide_less = tuple(row[:, :wide] for row in self_less)
    run_less = tuple(row[:, wide:] for row in self_less)
    dq[...] = jnp.zeros(dq.shape, F32)
    arrays = ((kv0, t0, dkv0, dt0), (kv1, t1, dkv1, dt1), (kv2, t2, dkv2, dt2), (kv3, t3, dkv3, dt3))
    for number, (kv, text, dkv, dtext) in enumerate(arrays):
        keys = kv[:, :wide, :LANES].reshape(highs * wide, LANES)
        values = kv[:, :wide, LANES:].reshape(highs * wide, LANES)
        d_key, d_value, d_query = attend_back(
            q[:wide, :], self_grad[:wide, :], wide_less, keys, values, None
        )
        dkv[:, :wide, :LANES] = d_key.reshape(highs, wide, LANES)
        dkv[:, :wide, LANES:] = d_value.reshape(highs, wide, LANES)
        dq[:wide, :] += d_query

        @pl.loop(0, highs)
        def _(high, number=number, kv=kv, text=text, dkv=dkv, dtext=dtext):
            block = number * highs + high

            @pl.when(meta.self_flag(block) > 0)
            def _():
                allowed = meta.run_items(meta.group(block), run_rows, 0) == run_items
                d_key, d_value, d_query = attend_back(
                    q[wide:, :],
                    self_grad[wide:, :],
                    run_less,
                    kv[high, wide:, :LANES],
                    kv[high, wide:, LANES:],
                    allowed,
                )
                dkv[high, wide:, :LANES] = d_key
                dkv[high, wide:, LANES:] = d_value
                dq[wide:, :] += d_query

            @pl.when(meta.self_flag(block) == 0)
            def _():
                dkv[high, wide:, :] = jnp.zeros((run_rows, 2 * LANES), BF16)

            @pl.when(meta.cross_flag(block) > 0)
            def _():
                allowed = meta.text_items(meta.group(block), 0) == all_items
                d_key, d_value, d_query = attend_back(
                    q[...],
                    cross_grad[...],
                    cross_less,
                    text[high, :, :LANES],
                    text[high, :, LANES:],
                    allowed,
                )
                dtext[high, :, :LANES] = d_key
                dtext[high, :, LANES:] = d_value
                dq[...] += d_query

            @pl.when(meta.cross_flag(block) == 0)
            def _():
                dtext[high] = jnp.zeros((text_rows, 2 * LANES), BF16)


def attention_back_call(
    meta, queries, incoming, self_out, cross_out, self_total, cross_total, gate, kvs, texts, runs
):
    rows, width = queries.shape
    highs, text_rows = (kvs[0].shape[0], texts[0].shape[1])
    wide = rows // 4
    kv_spec = pl.BlockSpec((highs, rows, 2 * LANES), lambda p, *_: (0, 0, p))
    text_spec = pl.BlockSpec((highs, text_rows, 2 * LANES), lambda p, *_: (0, 0, p))
    results = pl.pallas_call(
        functools.partial(attention_back_kernel, runs, highs, wide, text_rows),
        grid_spec=pltpu.PrefetchScalarGridSpec(
            num_scalar_prefetch=1,
            grid=(width // LANES,),
            in_specs=[columns(rows, LANES)] * 6
            + [columns(1, LANES)]
            + [kv_spec] * 4
            + [text_spec] * 4,
            out_specs=[columns(rows, LANES)]
            + [kv_spec] * 4
            + [text_spec] * 4
            + [columns(1, LANES)],
            scratch_shapes=[pltpu.VMEM((rows, LANES), BF16)] * 2,
        ),
        out_shape=[jax.ShapeDtypeStruct((rows, width), F32)]
        + [jax.ShapeDtypeStruct(kvs[0].shape, BF16)] * 4
        + [jax.ShapeDtypeStruct(texts[0].shape, BF16)] * 4
        + [jax.ShapeDtypeStruct((1, width), F32)],
        compiler_params=params(60),
        cost_estimate=pl.CostEstimate(
            flops=40_000_000_000, bytes_accessed=30_000_000, transcendentals=0
        ),
        name="attention_back",
    )(
        meta, queries, incoming, self_out, cross_out, self_total, cross_total, gate, *kvs, *texts
    )
    return (results[0], results[1:5], results[5:9], results[9])


def interleave(arrays):
    pairs = arrays[0].shape[-1] // LANES
    return jnp.concatenate(
        [array[..., p * LANES : (p + 1) * LANES] for p in range(pairs) for array in arrays],
        axis=-1,
    )


def separate(array, kinds):
    pairs = array.shape[-1] // LANES // kinds
    return [
        jnp.concatenate(
            [
                array[..., (p * kinds + kind) * LANES : (p * kinds + kind + 1) * LANES]
                for p in range(pairs)
            ],
            axis=-1,
        )
        for kind in range(kinds)
    ]


def on_device(
    patches,
    cotangent,
    item_lengths,
    timesteps,
    patch_rows,
    patch_cols,
    conditioning,
    text_states,
    gain_attn,
    gain_ffn,
    query_gain,
    key_gain,
    text_key_gain,
    cross_gate,
    w_query,
    w_key,
    w_value,
    w_out,
    w_text_key,
    w_text_value,
    w_gate,
    w_up,
    w_down,
    w_ada,
    w_text,
):
    at = Place()
    tok_dev, model_width = patches.shape
    shard_rows = w_query.shape[0]
    head_dim = query_gain.shape[0]
    local_width = w_query.shape[1]
    heads_local = local_width // head_dim
    text_rows = text_states.shape[0]
    item_count = conditioning.shape[0]
    quarter = tok_dev // 4
    hidden_width = w_gate.shape[1]

    my_patches = swap_roles(patches)
    positions = swap_roles(jnp.stack([patch_rows, patch_cols]).astype(F32))
    embed_pre = conditioning.astype(F32) + time_embed(timesteps, model_width)
    embed = jax.nn.silu(embed_pre).astype(BF16)
    own_embed = lax.dynamic_slice_in_dim(embed, at.data * shard_rows, shard_rows, 1)
    gains = lax.dynamic_update_slice(
        jnp.zeros((2, model_width), F32),
        jnp.stack([gain_attn, gain_ffn]).astype(F32),
        (0, at.data * shard_rows),
    )
    head_sums = butterfly(
        jnp.concatenate([multiply(own_embed, w_ada), gains], axis=0), at, model=False
    )
    gain_attn32, gain_ffn32 = (head_sums[item_count], head_sums[item_count + 1])
    mod_part = head_sums[:item_count]
    shift1_t, gate1_t, shift2_t, gate2_t = unmix(
        [mod_part]
        + [
            lax.ppermute(mod_part, "mp", [(i, i ^ other) for i in range(4)])
            for other in (1, 2, 3)
        ],
        at.model,
    )

    full_qkv, qkv_sent = gather_rows(interleave([w_query, w_key, w_value]), at)
    my_text = swap_roles(after(text_states, *qkv_sent.z))
    full_text, text_sent = gather_rows(w_text, at, qkv_sent.z, qkv_sent.y)
    full_tkv, tkv_sent = gather_rows(
        interleave([w_text_key, w_text_value]), at, qkv_sent.y, text_sent.y
    )

    token_items = item_ids(item_lengths, tok_dev, at.n_dp).reshape(at.n_dp, tok_dev)
    own_items = pick(token_items, at.tokens)
    item_labels = jnp.arange(item_count, dtype=jnp.int32)
    onehot = (own_items[:, None] == item_labels[None, :]).astype(F32)
    runs = item_lengths.shape[0]
    groups = jnp.stack(relative_groups(at)).astype(jnp.int32)
    firsts, lasts = (token_items[:, tok_dev // 4], token_items[:, tok_dev - 1])
    my_first, my_last = (pick(firsts, at.tokens), pick(lasts, at.tokens))
    self_flags = (firsts[groups] <= my_last) & (lasts[groups] >= my_first)
    text_first = groups * text_rows // TTOK
    text_last = (groups * text_rows + text_rows - 1) // TTOK
    cross_flags = ((text_first <= my_last) & (text_last >= my_first)) | (text_last >= runs)
    meta = jnp.concatenate(
        [
            jnp.cumsum(item_lengths),
            groups,
            at.tokens[None],
            self_flags.astype(jnp.int32),
            cross_flags.astype(jnp.int32),
        ]
    ).astype(jnp.int32)
    few_items = lax.dynamic_slice_in_dim(own_items, at.features * quarter, quarter)
    few_onehot = lax.dynamic_slice_in_dim(onehot, at.features * quarter, quarter)

    shift1 = rows_of(shift1_t, own_items)
    inputs = my_patches.astype(F32)
    normed1, _ = norm_fwd(inputs, gain_attn32)
    hidden1 = (normed1 * (1.0 + shift1)).astype(BF16)

    angles = rope_angles(positions[0], positions[1], head_dim)
    both_heads = (1, LANES // head_dim)
    cosine, sine = (jnp.cos(angles), jnp.sin(angles))
    split = head_dim // 4
    cosine = jnp.tile(
        jnp.concatenate([cosine[:, :split]] * 2 + [cosine[:, split:]] * 2, axis=1), both_heads
    )
    sine = jnp.tile(
        jnp.concatenate(
            [-sine[:, :split], sine[:, :split], -sine[:, split:], sine[:, split:]], axis=1
        ),
        both_heads,
    )
    query_gain32, key_gain32, text_gain32 = (
        jnp.tile(gain.astype(F32)[None], both_heads)
        for gain in (query_gain, key_gain, text_key_gain)
    )
    query_pre, key_pre, queries, own_kv = qkv_call(
        hidden1, full_qkv, cosine, sine, query_gain32, key_gain32
    )
    all_kv, kv_sent = gather_tokens(own_kv, at)
    full_out, _ = gather_rows(w_out, at, tkv_sent.z + [own_kv], kv_sent.y)
    full_gu, gu_sent = gather_rows(
        jnp.concatenate([w_gate, w_up], axis=1), at, kv_sent.z, kv_sent.y
    )
    full_down, _ = gather_rows(w_down, at, gu_sent.z, gu_sent.y)
    my_cotangent = swap_roles(after(cotangent, *gu_sent.z))

    words = multiply_trans(my_text, full_text).astype(BF16)
    for other in (1, 2):
        words = (words.astype(F32) + other_feature(words, other).astype(F32)).astype(BF16)
    text_pre, own_text_kv = text_call(words, full_tkv, text_gain32)
    all_text_kv, _ = gather_tokens(own_text_kv, at)
    gate_local = jnp.tanh(
        lax.dynamic_slice_in_dim(cross_gate.astype(F32), at.features * heads_local, heads_local)
    )
    gate_wide = jnp.repeat(gate_local, head_dim)[None]
    combined, self_out, cross_out, self_total, cross_total = attention_call(
        meta, queries, all_kv, all_text_kv, gate_wide, runs
    )
    few_inputs = lax.dynamic_slice_in_dim(inputs, at.features * quarter, quarter)
    few_normed1 = lax.dynamic_slice_in_dim(normed1, at.features * quarter, quarter)
    tanh_one = jnp.tanh(rows_of(gate1_t, few_items))
    tanh_two = jnp.tanh(rows_of(gate2_t, few_items))
    shift2 = rows_of(shift2_t, few_items)
    few_shift1 = rows_of(shift1_t, few_items)
    branch = sum_quarters(multiply_trans(combined, full_out).astype(BF16), at)
    middle = few_inputs + tanh_one * branch
    normed2, scale2 = norm_fwd(middle, gain_ffn32)
    hidden2 = gather_quarters((normed2 * (1.0 + shift2)).astype(BF16), at)
    gate_up = multiply(hidden2, full_gu)
    gate_pre, up_pre = (gate_up[:, :hidden_width], gate_up[:, hidden_width:])
    logistic = jax.nn.sigmoid(gate_pre)
    silu_gate = gate_pre * logistic
    inner_act = (silu_gate * up_pre).astype(BF16)

    grad_output = my_cotangent.astype(F32)
    few_output = lax.dynamic_slice_in_dim(grad_output, at.features * quarter, quarter)
    grad_ffn = (grad_output * rows_of(jnp.tanh(gate2_t), own_items)).astype(BF16)
    grad_inner = multiply(grad_ffn, full_down)
    grad_gate = (grad_inner * up_pre * logistic * (1.0 + gate_pre * (1.0 - logistic))).astype(BF16)
    grad_up = (grad_inner * silu_gate).astype(BF16)
    grad_gu = jnp.concatenate([grad_gate, grad_up], axis=1)
    grad_hidden2 = sum_quarters(multiply_trans(grad_gu, full_gu).astype(BF16), at)


    grad_middle_norm, gain_ffn_term = norm_back(
        middle, scale2, gain_ffn32, grad_hidden2 * (1.0 + shift2)
    )
    grad_middle = few_output + grad_middle_norm
    grad_branch = gather_quarters((grad_middle * tanh_one).astype(BF16), at)
    ffn_part = after(multiply_trans(inner_act, full_down).astype(BF16), grad_hidden2)
    ffn_out = sum_quarters(ffn_part, at)
    grad_combined = multiply(grad_branch, full_out)
    mixed_out = gather_output(
        after((middle + tanh_two * ffn_out).astype(BF16), grad_branch), at
    )
    grads_down, down_sums = scatter_rows(trans_multiply(grad_ffn, inner_act), at)
    grads_gu, gu_sums = scatter_rows(trans_multiply(hidden2, grad_gu), at, (), down_sums.y)
    grad_combined = after(grad_combined, *(down_sums.z + gu_sums.y))

    grad_queries, shared_terms, text_terms, gate_terms = attention_back_call(
        meta,
        queries,
        grad_combined,
        self_out,
        cross_out,
        self_total,
        cross_total,
        gate_wide,
        all_kv,
        all_text_kv,
        runs,
    )
    grad_gate_local = jnp.sum(gate_terms.reshape(heads_local, head_dim), axis=1) * (
        1.0 - gate_local * gate_local
    )
    text_back, _ = scatter_tokens(text_terms, at)
    shared_back, kv_sums = scatter_tokens(shared_terms, at)
    grads_out, _ = scatter_rows(
        trans_multiply(grad_branch, combined), at, (), kv_sums.y, kv_sums.z
    )
    grad_qkv, query_gain_term, key_gain_term = qkv_back_call(
        grad_queries, shared_back, query_pre, key_pre, cosine, sine, query_gain32, key_gain32
    )
    grad_tkv, text_gain_term = text_back_call(text_back, text_pre, text_gain32)
    grad_hidden1 = sum_quarters(multiply_trans(grad_qkv, full_qkv).astype(BF16), at)
    grad_words = multiply_trans(grad_tkv, full_tkv).astype(BF16)
    for other in (1, 2):
        grad_words = (
            grad_words.astype(F32) + other_feature(grad_words, other).astype(F32)
        ).astype(BF16)

    few_scale1 = lax.rsqrt(jnp.mean(few_inputs * few_inputs, axis=-1, keepdims=True) + EPSILON)
    grad_inputs_norm, gain_attn_term = norm_back(
        few_inputs, few_scale1, gain_attn32, grad_hidden1 * (1.0 + few_shift1)
    )
    grad_patches = gather_output((grad_middle + grad_inputs_norm).astype(BF16), at).astype(F32)
    grad_text = swap_roles(multiply(grad_words, full_text).astype(BF16)).astype(F32)
    grads_qkv, _ = scatter_rows(trans_multiply(hidden1, grad_qkv), at)
    grads_tkv, _ = scatter_rows(trans_multiply(words, grad_tkv), at)
    grads_text, _ = scatter_rows(trans_multiply(grad_words, my_text), at)

    def item_sums(rows):
        return trans_multiply(few_onehot, rows, HIGHEST)

    early = butterfly(
        jnp.concatenate(
            [
                item_sums(grad_middle * branch * (1.0 - tanh_one * tanh_one)),
                item_sums(grad_hidden2 * normed2),
                item_sums(few_output * ffn_out * (1.0 - tanh_two * tanh_two)),
                jnp.sum(gain_ffn_term, axis=0, keepdims=True),
            ],
            axis=0,
        ),
        at,
    )
    gate_full = lax.dynamic_update_slice_in_dim(
        jnp.zeros((cross_gate.shape[0],), F32),
        grad_gate_local,
        at.features * heads_local,
        0,
    )
    small = jnp.concatenate(
        [
            jnp.sum(query_gain_term.reshape(heads_local, head_dim), axis=0),
            jnp.sum(key_gain_term.reshape(heads_local, head_dim), axis=0),
            jnp.sum(text_gain_term.reshape(heads_local, head_dim), axis=0),
            gate_full,
        ]
    )
    small = jnp.pad(small, (0, model_width - small.shape[0]))
    late = butterfly(
        jnp.concatenate(
            [
                item_sums(grad_hidden1 * few_normed1),
                jnp.sum(gain_attn_term, axis=0, keepdims=True),
                small[None],
            ],
            axis=0,
        ),
        at,
    )
    grad_modulation = jnp.stack(
        [late[:item_count]] + [early[i * item_count : (i + 1) * item_count] for i in range(3)]
    )
    grad_mod_own = pick(grad_modulation, at.model)
    small = late[item_count + 1]
    grad_ada = trans_multiply(own_embed.astype(F32), grad_mod_own, HIGHEST)
    grad_embed_part = multiply_trans(grad_mod_own, w_ada.astype(F32), HIGHEST)
    grad_embed = butterfly(
        lax.dynamic_update_slice(
            jnp.zeros((item_count, model_width), F32),
            grad_embed_part,
            (0, at.data * shard_rows),
        ),
        at,
    )
    embed_logistic = jax.nn.sigmoid(embed_pre)
    grad_conditioning = grad_embed * embed_logistic * (1.0 + embed_pre * (1.0 - embed_logistic))
    own_gain = lambda row: lax.dynamic_slice_in_dim(row, at.data * shard_rows, shard_rows)
    grad_wq, grad_wk, grad_wv = separate(grads_qkv, 3)
    grad_wtk, grad_wtv = separate(grads_tkv, 2)
    return (
        mixed_out,
        grad_patches,
        grad_conditioning,
        grad_text,
        own_gain(late[item_count]),
        own_gain(early[3 * item_count]),
        small[:head_dim],
        small[head_dim : 2 * head_dim],
        small[2 * head_dim : 3 * head_dim],
        small[3 * head_dim : 3 * head_dim + cross_gate.shape[0]],
        grad_wq,
        grad_wk,
        grad_wv,
        grads_out,
        grad_wtk,
        grad_wtv,
        grads_gu[:, :hidden_width],
        grads_gu[:, hidden_width:],
        grads_down,
        grad_ada,
        grads_text,
    )


def solution(mesh):
    rows, both, one = (P("dp", None), P("dp", "mp"), P("dp"))
    whole = P()
    in_specs = (
        (rows, rows, whole, whole, one, one, whole, both, one, one)
        + (whole,) * 4
        + (both,) * 11
    )
    out_specs = (
        (rows, rows, whole, both, one, one) + (whole,) * 4 + (both,) * 11
    )
    return jax.shard_map(
        on_device, mesh=mesh, in_specs=in_specs, out_specs=out_specs, check_vma=False
    )
```

```python
import functools
import math

import jax
import jax.numpy as jnp
from jax import lax
from jax.experimental import pallas as pl
from jax.experimental.pallas import tpu as pltpu
from jax.sharding import PartitionSpec as P

TTOK = 256
HIGHEST = lax.Precision.HIGHEST
EPSILON = 1e-06
SCORE_BASE = 1.4426950408889634
TWO_NATURAL = 0.6931471805599453
AXES = ("dp", "mp")
DEPTH = 2
LANES = 128
F32 = jnp.float32
BF16 = jnp.bfloat16


def contract(left, right, pairing, precision=None):
    return lax.dot_general(
        left, right, (pairing, ((), ())), precision=precision, preferred_element_type=F32
    )


def multiply(left, right):
    return contract(left, right, ((1,), (0,)))


def multiply_trans(left, right, precision=None):
    return contract(left, right, ((1,), (1,)), precision)


def trans_multiply(left, right, precision=None):
    return contract(left, right, ((0,), (0,)), precision)


def time_embed(steps, model_width):
    halfway = model_width // 2
    frequency = jnp.exp(-math.log(10000.0) * jnp.arange(halfway, dtype=F32) / halfway)
    phases = steps.astype(F32)[:, None] * frequency[None, :]
    return jnp.concatenate([jnp.cos(phases), jnp.sin(phases)], axis=1)


def rope_angles(rows_pos, cols_pos, head_dim):
    quarter = head_dim // 4
    frequency = jnp.exp(-math.log(10000.0) * jnp.arange(quarter, dtype=F32) / quarter)
    return jnp.concatenate(
        [
            rows_pos.astype(F32)[:, None] * frequency[None, :],
            cols_pos.astype(F32)[:, None] * frequency[None, :],
        ],
        axis=1,
    )


def item_ids(lengths, tok_dev, n_dev):
    wide_dev = tok_dev // 4
    boundary = jnp.cumsum(lengths)
    position = jnp.arange(tok_dev * n_dev, dtype=jnp.int32)
    within = position % tok_dev
    placed = position // tok_dev * (tok_dev - wide_dev) + within - wide_dev
    counted = jnp.sum((boundary[None, :] <= placed[:, None]).astype(jnp.int32), axis=1)
    return jnp.where(within < wide_dev, lengths.shape[0], counted)


def norm_fwd(values, gain_vec):
    scaling = lax.rsqrt(jnp.mean(values * values, axis=-1, keepdims=True) + EPSILON)
    return (values * scaling * gain_vec, scaling)


def norm_back(values, scaling, gain_vec, incoming):
    weighted = incoming * gain_vec
    inner_mean = jnp.mean(weighted * values, axis=-1, keepdims=True)
    return (
        scaling * weighted - values * scaling * scaling * scaling * inner_mean,
        incoming * values * scaling,
    )


def codes(index):
    data, model = divmod(index, 4)
    return (data // 4, data // 2 % 2, data % 2, model // 2, model % 2)


def place(dh, zl, dy, x, c):
    return ((dh * 2 + zl) * 2 + dy) * 4 + x * 2 + c


def move(values, where, only=None):
    count = lax.axis_size("dp") * lax.axis_size("mp")
    pairs = [
        (i, place(*where(*codes(i)))) for i in range(count) if only is None or only(*codes(i))
    ]
    return lax.ppermute(values, AXES, pairs)


def swap_roles(values):
    return move(values, lambda dh, zl, dy, x, c: (dh, c, dy, x, zl))


def swap_rows(values, at):
    rows, width = values.shape
    away = lambda dh, zl, dy, x, c: zl != c
    over_z = lambda piece: move(piece, lambda dh, zl, dy, x, c: (dh, zl ^ 1, dy, x, c ^ 1), away)
    got = at.along_z.send(over_z, pick(values.reshape(2, rows // 2, width), at.x))
    other = move(got, lambda dh, zl, dy, x, c: (dh, zl, dy, x ^ 1, c), away)
    swapped = jnp.concatenate(unmix([got, other], at.x), axis=0)
    return jnp.where(at.c == at.zl, values, swapped)


def other_core(values):
    return move(values, lambda dh, zl, dy, x, c: (dh, zl, dy, x, c ^ 1))


def other_y(values):
    return move(values, lambda dh, zl, dy, x, c: (dh, zl, dy ^ 1, x, c))


def other_high(values, high):
    return move(values, lambda dh, zl, dy, x, c: (dh ^ high, zl, dy, x, c))


def other_feature(values, other):
    return move(values, lambda dh, zl, dy, x, c: (dh, zl ^ (other & 1), dy, x ^ (other >> 1), c))


def pick(values, index, axis=0):
    return lax.dynamic_index_in_dim(values, index, axis, keepdims=False)


def after(values, *events):
    if not events:
        return values
    return lax.optimization_barrier((values, *events))[0]


class Link:
    def __init__(self, depth):
        self.depth = depth
        self.ended = []

    def send(self, how, values, *rest):
        if len(self.ended) >= self.depth:
            values = after(values, self.ended[-self.depth])
        result = how(values, *rest)
        self.ended.append(result)
        return result


class Place:
    def __init__(self):
        self.along_z, self.along_y = (Link(DEPTH), Link(DEPTH))
        data, model = (lax.axis_index("dp"), lax.axis_index("mp"))
        self.data, self.model = (data, model)
        self.n_dp = lax.axis_size("dp")
        self.highs = self.n_dp // 4
        self.dh, self.zl, self.dy = (data // 4, data // 2 % 2, data % 2)
        self.x, self.c = (model // 2, model % 2)
        self.tokens = (self.dh * 2 + self.c) * 2 + self.dy
        self.features = self.x * 2 + self.zl


def unmix(parts, index):
    count = len(parts)
    ordered = []
    for spot in range(count):
        value = parts[spot]
        for other in range(1, count):
            value = jnp.where(index == other, parts[spot ^ other], value)
        ordered.append(value)
    return ordered


def pack_kernel(order, *refs):
    core = lax.axis_index("mp") % 2
    for out, side in zip(refs[-2:], (core, core ^ 1)):
        start = 0
        for source, first, width in order:
            out[:, start : start + width] = refs[source][side, :, first : first + width]
            start += width


def pack(shards, order):
    half = shards[0].shape[0] // 2
    width = sum(part[2] for part in order)
    result = jax.ShapeDtypeStruct((half, width), shards[0].dtype)
    return pl.pallas_call(
        functools.partial(pack_kernel, order),
        out_shape=[result, result],
        compiler_params=params(),
        cost_estimate=pl.CostEstimate(
            flops=0, bytes_accessed=8 * half * width, transcendentals=0
        ),
        name="pack",
    )(*[shard.reshape(2, half, shard.shape[1]) for shard in shards])


def by_pairs(shards):
    return [
        (source, first, LANES)
        for first in range(0, shards[0].shape[1], LANES)
        for source in range(len(shards))
    ]


def side_by_side(shards):
    return [(source, 0, shard.shape[1]) for source, shard in enumerate(shards)]


def pack_kernel(order, *refs):
    core = lax.axis_index("mp") % 2
    for out, side in zip(refs[-2:], (core, core ^ 1)):
        start = 0
        for source, first, width in order:
            out[:, start : start + width] = refs[source][side, :, first : first + width]
            start += width


def pack(shards, order):
    half = shards[0].shape[0] // 2
    width = sum(part[2] for part in order)
    result = jax.ShapeDtypeStruct((half, width), shards[0].dtype)
    return pl.pallas_call(
        functools.partial(pack_kernel, order),
        out_shape=[result, result],
        compiler_params=params(),
        cost_estimate=pl.CostEstimate(
            flops=0, bytes_accessed=8 * half * width, transcendentals=0
        ),
        name="pack",
    )(*[shard.reshape(2, half, shard.shape[1]) for shard in shards])


def by_pairs(shards):
    return [
        (source, first, LANES)
        for first in range(0, shards[0].shape[1], LANES)
        for source in range(len(shards))
    ]


def side_by_side(shards):
    return [(source, 0, shard.shape[1]) for source, shard in enumerate(shards)]


def assemble_kernel(highs, near, beside, near_core, beside_core, full):
    data, core = (lax.axis_index("dp"), lax.axis_index("mp") % 2)
    high, y = (data // 4, data % 2)
    for block, from_y, from_core in (
        (near, y, core),
        (beside, y ^ 1, core),
        (near_core, y, core ^ 1),
        (beside_core, y ^ 1, core ^ 1),
    ):
        for a in range(highs):
            for b in (0, 1):
                full[high ^ a, from_core ^ b, from_y, from_core] = block[a, b]


def assemble(near, beside, near_core, beside_core):
    highs, _, half, width = near.shape
    step = math.gcd(width, 512) if width % 384 else 384
    part = pl.BlockSpec((highs, 2, half, step), lambda i: (0, 0, 0, i))
    return pl.pallas_call(
        functools.partial(assemble_kernel, highs),
        grid=(width // step,),
        in_specs=[part] * 4,
        out_specs=pl.BlockSpec((highs, 2, 2, 2, half, step), lambda i: (0,) * 5 + (i,)),
        out_shape=jax.ShapeDtypeStruct((highs, 2, 2, 2, half, width), near.dtype),
        compiler_params=params(),
        cost_estimate=pl.CostEstimate(
            flops=0, bytes_accessed=32 * highs * half * width, transcendentals=0
        ),
        name="assemble",
    )(near, beside, near_core, beside_core)


class Events:
    def __init__(self, **events):
        self.__dict__.update(events)


def assemble_kernel(near, beside, near_core, beside_core, full):
    y, core = (lax.axis_index("dp") % 2, lax.axis_index("mp") % 2)
    for block, from_y, from_core in (
        (near, y, core),
        (beside, y ^ 1, core),
        (near_core, y, core ^ 1),
        (beside_core, y ^ 1, core ^ 1),
    ):
        for z in range(near.shape[0]):
            full[z, from_y, from_core] = block[z]


def assemble(blocks, first, width):
    count, half, _ = blocks[0].shape
    step = next(step for step in (512, 384, 256, LANES) if first % step == width % step == 0)
    part = pl.BlockSpec((count, half, step), lambda i: (0, 0, first // step + i))
    full = pl.pallas_call(
        assemble_kernel,
        grid=(width // step,),
        in_specs=[part] * 4,
        out_specs=pl.BlockSpec((count, 2, 2, half, step), lambda i: (0,) * 4 + (i,)),
        out_shape=jax.ShapeDtypeStruct((count, 2, 2, half, width), BF16),
        compiler_params=params(),
        cost_estimate=pl.CostEstimate(
            flops=0, bytes_accessed=16 * count * half * width, transcendentals=0
        ),
        name="assemble",
    )(*blocks)
    return full.reshape(4 * count * half, width)


def exchange_z(values):
    count = lax.axis_size("dp")
    return lax.all_to_all(
        values, "dp", 0, 0, axis_index_groups=[list(range(y, count, 2)) for y in (0, 1)], tiled=True
    )


def exchange_features(values):
    highs = lax.axis_size("dp") // 4
    groups = [
        [place(dh, zl, dy, x, c) for x in (0, 1) for zl in (0, 1)]
        for dh in range(highs)
        for dy in (0, 1)
        for c in (0, 1)
    ]
    return lax.all_to_all(values, AXES, 0, 0, axis_index_groups=groups, tiled=True)


def share(shards, order, at, c_wait=()):
    mine, theirs = pack([after(shard, *c_wait) for shard in shards], order)
    got = other_core(theirs)
    return (jnp.where(at.c == 0, mine, got), jnp.where(at.c == 0, got, mine), got)


class GatherRows:
    def __init__(self, shared, first, widths, at):
        self.at, self.widths = (at, widths)
        pieces = [piece[:, first : first + sum(widths)] for piece in shared[:2]]
        self.stacked = jnp.stack(pieces * at.highs)

    def z(self):
        self.near = self.at.along_z.send(exchange_z, self.stacked)

    def y(self):
        self.beside = self.at.along_y.send(other_y, self.near)

    def core(self, *events):
        near, beside = (after(self.near, *events), after(self.beside, *events))
        blocks = (near, beside, other_core(near), other_core(beside))
        fulls, start = ([], 0)
        for width in self.widths:
            fulls.append(assemble(blocks, start, width))
            start += width
        return fulls


class ScatterRows:
    def __init__(self, grads, at):
        self.at = at
        half = grads[0].shape[0] // at.n_dp // 2
        self.views = [grad.astype(BF16).reshape(at.n_dp // 2, 2, 2, half, -1) for grad in grads]
        self.from_core = other_core(
            jnp.concatenate([pick(view, 1 - at.c, 2) for view in self.views], axis=-1)
        )
        self.to_y = self.kept_rows(1 - at.dy).astype(BF16)

    def kept_rows(self, y):
        own = [pick(pick(view, y, 1), self.at.c, 1) for view in self.views]
        own = jnp.concatenate(own, axis=-1).astype(F32)
        return own + pick(self.from_core, y, 1).astype(F32)

    def y(self):
        from_y = self.at.along_y.send(other_y, self.to_y)
        self.to_z = (self.kept_rows(self.at.dy) + from_y.astype(F32)).astype(BF16)

    def z(self):
        self.from_z = self.at.along_z.send(exchange_z, self.to_z)

    def result(self):
        at = self.at
        sums = [
            sum(self.from_z[2 * a + zl].astype(F32) for a in range(at.highs)) for zl in (0, 1)
        ]
        mine, theirs = (jnp.where(at.c == 0, *sums), jnp.where(at.c == 0, *sums[::-1]))
        other = other_core(theirs.astype(BF16)).astype(F32)
        return jnp.concatenate(unmix([mine, other], at.c), axis=0)


class GatherTokens:
    def __init__(self, block, at):
        self.block, self.at = (block, at)

    def z(self):
        far = [
            self.at.along_z.send(other_high, self.block, a) for a in range(1, self.at.highs)
        ]
        self.near = jnp.stack([self.block] + far)

    def y(self):
        self.beside = self.at.along_y.send(other_y, self.near)

    def core(self):
        return [self.near, self.beside, other_core(self.near), other_core(self.beside)]


class ScatterTokens:
    def __init__(self, same, other, at):
        self.at = at
        self.total = same.astype(F32) + other_core(other).astype(F32)
        self.to_y = self.total[1].astype(BF16)

    def y(self):
        from_y = self.at.along_y.send(other_y, self.to_y)
        self.total = self.total[0] + from_y.astype(F32)

    def z(self):
        result = self.total[0]
        for a in range(1, self.at.highs):
            got = self.at.along_z.send(other_high, self.total[a].astype(BF16), a)
            result = result + got.astype(F32)
        return result


def relative_groups(at):
    return [
        ((at.dh ^ a) * 2 + (at.c ^ core)) * 2 + (at.dy ^ y)
        for core in (0, 1)
        for y in (0, 1)
        for a in range(at.highs)
    ]


def sum_quarters(part, at):
    rows, width = part.shape
    parts = at.along_z.send(exchange_features, part.reshape(4, rows // 4, width))
    return jnp.sum(parts.astype(F32), axis=0)


def gather_quarters(own, at):
    rows, width = own.shape
    parts = at.along_z.send(
        exchange_features, jnp.broadcast_to(own[None], (4, rows, width))
    )
    return parts.reshape(4 * rows, width)


def sum_features(part, at):
    for other, link in ((1, at.along_z), (2, None)):
        got = link.send(other_feature, part, other) if link else other_feature(part, other)
        part = (part.astype(F32) + got.astype(F32)).astype(BF16)
    return part


def gather_output(own, at):
    to_x = lambda part, a: move(part, lambda dh, zl, dy, x, c: (dh, c, dy, x ^ a, zl))
    near = [at.along_z.send(to_x, own, a) for a in (0, 1)]
    near = jnp.stack(unmix(near, at.x))
    far = other_core(near)
    first, second = (jnp.where(at.c == 0, near, far), jnp.where(at.c == 0, far, near))
    return jnp.stack([first, second], axis=1).reshape(4 * own.shape[0], own.shape[1])


def butterfly(values, at, data=True, model=True, z_wait=()):
    for bit in (1, 2) if model else ():
        values = values + lax.ppermute(values, "mp", [(i, i ^ bit) for i in range(4)])
    bit = 1
    while data and bit < at.n_dp:
        if bit == 2:
            values = after(values, *z_wait)
        values = values + lax.ppermute(values, "dp", [(i, i ^ bit) for i in range(at.n_dp)])
        bit *= 2
    return values


def rows_of(table, items):
    value = jnp.broadcast_to(table[0][None], (items.shape[0], table.shape[1]))
    for item in range(1, table.shape[0]):
        value = jnp.where(items[:, None] == item, table[item][None], value)
    return value


def halves(values):
    lane = lax.broadcasted_iota(jnp.int32, (1, LANES), 1)
    low = lane < LANES // 2
    zero = jnp.zeros((), values.dtype)
    return (jnp.where(low, values, zero), jnp.where(low, zero, values))


def pair_select(first, second):
    lane = lax.broadcasted_iota(jnp.int32, (1, LANES), 1)
    return jnp.where(lane < LANES // 2, first, second)


def pair_mean(values):
    low, high = halves(values)
    return pair_select(
        jnp.sum(low, axis=-1, keepdims=True), jnp.sum(high, axis=-1, keepdims=True)
    ) * (2.0 / LANES)


def partner(values):
    lane = lax.broadcasted_iota(jnp.int32, (1, LANES), 1)
    return jnp.where(
        lane % 32 < 16, pltpu.roll(values, LANES - 16, 1), pltpu.roll(values, 16, 1)
    )


def pair_norm(values, gain):
    return values * lax.rsqrt(pair_mean(values * values) + EPSILON) * gain


def pair_norm_back(values, gain, incoming):
    scaling = lax.rsqrt(pair_mean(values * values) + EPSILON)
    weighted = incoming * gain
    inner_mean = pair_mean(weighted * values)
    return (
        scaling * weighted - values * scaling * scaling * scaling * inner_mean,
        jnp.sum(incoming * values * scaling, axis=0, keepdims=True),
    )


def params(megabytes=48):
    return pltpu.CompilerParams(vmem_limit_bytes=megabytes * 1024 * 1024)


def whole(shape):
    return pl.BlockSpec(shape, lambda p, *_: (0,) * len(shape))


def columns(rows, width):
    return pl.BlockSpec((rows, width), lambda p, *_: (0, p))


def qkv_kernel(x, w, cosine, sine, q_gain, k_gain, q_pre, k_pre, q_out, kv_out):
    made = jnp.dot(x[...], w[...], preferred_element_type=F32)
    query, key = (made[:, :LANES], made[:, LANES : 2 * LANES])
    q_pre[...] = query
    k_pre[...] = key
    query = pair_norm(query, q_gain[...])
    key = pair_norm(key, k_gain[...])
    q_out[...] = (query * cosine[...] + partner(query) * sine[...]).astype(BF16)
    kv_out[:, :LANES] = (key * cosine[...] + partner(key) * sine[...]).astype(BF16)
    kv_out[:, LANES:] = made[:, 2 * LANES :].astype(BF16)


def qkv_call(hidden, weights, cosine, sine, q_gain, k_gain):
    rows, depth = hidden.shape
    pairs = weights.shape[1] // (3 * LANES)
    width = pairs * LANES
    return pl.pallas_call(
        qkv_kernel,
        grid=(pairs,),
        in_specs=[
            whole((rows, depth)),
            columns(depth, 3 * LANES),
            whole((rows, LANES)),
            whole((rows, LANES)),
            whole((1, LANES)),
            whole((1, LANES)),
        ],
        out_specs=[columns(rows, LANES)] * 3 + [columns(rows, 2 * LANES)],
        out_shape=[
            jax.ShapeDtypeStruct((rows, width), F32),
            jax.ShapeDtypeStruct((rows, width), F32),
            jax.ShapeDtypeStruct((rows, width), BF16),
            jax.ShapeDtypeStruct((rows, 2 * width), BF16),
        ],
        compiler_params=params(),
        cost_estimate=pl.CostEstimate(
            flops=6 * rows * depth * width, bytes_accessed=8_000_000, transcendentals=0
        ),
        name="qkv",
    )(hidden, weights, cosine, sine, q_gain, k_gain)


def qkv_back_kernel(dq, dkv, q_pre, k_pre, cosine, sine, q_gain, k_gain, out, dq_gain, dk_gain):
    query, key = (dq[...], dkv[:, :LANES])
    query = query * cosine[...] - partner(query) * sine[...]
    key = key * cosine[...] - partner(key) * sine[...]
    query, dq_gain[...] = pair_norm_back(q_pre[...], q_gain[...], query)
    key, dk_gain[...] = pair_norm_back(k_pre[...], k_gain[...], key)
    out[:, :LANES] = query.astype(BF16)
    out[:, LANES : 2 * LANES] = key.astype(BF16)
    out[:, 2 * LANES :] = dkv[:, LANES:].astype(BF16)


def qkv_back_call(dq, dkv, q_pre, k_pre, cosine, sine, q_gain, k_gain):
    rows, width = dq.shape
    pairs = width // LANES
    return pl.pallas_call(
        qkv_back_kernel,
        grid=(pairs,),
        in_specs=[columns(rows, LANES), columns(rows, 2 * LANES)]
        + [columns(rows, LANES)] * 2
        + [whole((rows, LANES))] * 2
        + [whole((1, LANES))] * 2,
        out_specs=[columns(rows, 3 * LANES), columns(1, LANES), columns(1, LANES)],
        out_shape=[
            jax.ShapeDtypeStruct((rows, 3 * width), BF16),
            jax.ShapeDtypeStruct((1, width), F32),
            jax.ShapeDtypeStruct((1, width), F32),
        ],
        compiler_params=params(),
        cost_estimate=pl.CostEstimate(flops=0, bytes_accessed=8_000_000, transcendentals=0),
        name="qkv_back",
    )(dq, dkv, q_pre, k_pre, cosine, sine, q_gain, k_gain)


def text_kernel(x, w, gain, k_pre, kv_out):
    made = jnp.dot(x[...], w[...], preferred_element_type=F32)
    k_pre[...] = made[:, :LANES]
    kv_out[:, :LANES] = pair_norm(made[:, :LANES], gain[...]).astype(BF16)
    kv_out[:, LANES:] = made[:, LANES:].astype(BF16)


def text_call(words, weights, gain):
    rows, depth = words.shape
    width = weights.shape[1] // 2
    return pl.pallas_call(
        text_kernel,
        grid=(width // LANES,),
        in_specs=[whole((rows, depth)), columns(depth, 2 * LANES), whole((1, LANES))],
        out_specs=[columns(rows, LANES), columns(rows, 2 * LANES)],
        out_shape=[
            jax.ShapeDtypeStruct((rows, width), F32),
            jax.ShapeDtypeStruct((rows, 2 * width), BF16),
        ],
        compiler_params=params(),
        cost_estimate=pl.CostEstimate(
            flops=4 * rows * depth * width, bytes_accessed=4_000_000, transcendentals=0
        ),
        name="text_kv",
    )(words, weights, gain)


def text_back_kernel(dkv, k_pre, gain, out, d_gain):
    key, d_gain[...] = pair_norm_back(k_pre[...], gain[...], dkv[:, :LANES])
    out[:, :LANES] = key.astype(BF16)
    out[:, LANES:] = dkv[:, LANES:].astype(BF16)


def text_back_call(dkv, k_pre, gain):
    rows, width = k_pre.shape
    return pl.pallas_call(
        text_back_kernel,
        grid=(width // LANES,),
        in_specs=[columns(rows, 2 * LANES), columns(rows, LANES), whole((1, LANES))],
        out_specs=[columns(rows, 2 * LANES), columns(1, LANES)],
        out_shape=[
            jax.ShapeDtypeStruct((rows, 2 * width), BF16),
            jax.ShapeDtypeStruct((1, width), F32),
        ],
        compiler_params=params(),
        cost_estimate=pl.CostEstimate(flops=0, bytes_accessed=2_000_000, transcendentals=0),
        name="text_kv_back",
    )(dkv, k_pre, gain)


class Meta:
    def __init__(self, ref, runs, blocks, wide, text_rows):
        self.ref, self.runs, self.blocks = (ref, runs, blocks)
        self.wide, self.text_rows = (wide, text_rows)

    def group(self, block):
        return self.ref[self.runs + block]

    def own(self):
        return self.ref[self.runs + self.blocks]

    def self_flag(self, block):
        return self.ref[self.runs + self.blocks + 1 + block]

    def cross_flag(self, block):
        return self.ref[self.runs + 2 * self.blocks + 1 + block]

    def run_items(self, group, count, axis):
        shape = (count, 1) if axis == 0 else (1, count)
        spot = lax.broadcasted_iota(jnp.int32, shape, axis) + group * count
        item = jnp.zeros(shape, jnp.int32)
        for run in range(self.runs):
            item = item + (spot >= self.ref[run]).astype(jnp.int32)
        return item

    def all_items(self, group, count, axis):
        shape = (count, 1) if axis == 0 else (1, count)
        row = lax.broadcasted_iota(jnp.int32, shape, axis)
        spot = row - self.wide + group * (count - self.wide)
        item = jnp.zeros(shape, jnp.int32)
        for run in range(self.runs):
            item = item + (spot >= self.ref[run]).astype(jnp.int32)
        return jnp.where(row < self.wide, self.runs, item)

    def text_items(self, group, axis):
        shape = (self.text_rows, 1) if axis == 0 else (1, self.text_rows)
        return (lax.broadcasted_iota(jnp.int32, shape, axis) + group * self.text_rows) // TTOK


def nt_dot(left, right):
    return lax.dot_general(left, right, (((1,), (1,)), ((), ())), preferred_element_type=F32)


def nn_dot(left, right):
    return jnp.dot(left, right, preferred_element_type=F32)


def tn_dot(left, right):
    return lax.dot_general(left, right, (((0,), (0,)), ((), ())), preferred_element_type=F32)


SCALING = 64 ** (-0.5) * SCORE_BASE
GRAD_SCALING = 64 ** (-0.5) * SCORE_BASE * TWO_NATURAL


def attend(query, key, value, allowed):
    sums, totals = (None, [])
    for query_head, value_head in zip(halves(query), halves(value)):
        weights = jnp.exp2(nt_dot(query_head, key) * SCALING)
        if allowed is not None:
            weights = jnp.where(allowed, weights, 0.0)
        totals.append(jnp.sum(weights, axis=-1, keepdims=True))
        fresh = nn_dot(weights.astype(BF16), value_head)
        sums = fresh if sums is None else sums + fresh
    return (sums, pair_select(*totals))


def attention_kernel(
    runs, highs, wide, text_rows, ref, q, kv0, kv1, kv2, kv3, t0, t1, t2, t3, gate,
    combined, self_out, cross_out, self_total, cross_total,
):
    meta = Meta(ref, runs, 4 * highs, wide, text_rows)
    rows = q.shape[0]
    run_rows = rows - wide
    self_out[...] = jnp.zeros(self_out.shape, F32)
    self_total[...] = jnp.zeros(self_total.shape, F32)
    cross_out[...] = jnp.zeros(cross_out.shape, F32)
    cross_total[...] = jnp.zeros(cross_total.shape, F32)
    own = meta.own()
    run_items = meta.run_items(own, run_rows, 0)
    all_items = meta.all_items(own, rows, 0)
    for number, (kv, text) in enumerate(((kv0, t0), (kv1, t1), (kv2, t2), (kv3, t3))):
        keys = kv[:, :wide, :LANES].reshape(highs * wide, LANES)
        values = kv[:, :wide, LANES:].reshape(highs * wide, LANES)
        sums, totals = attend(q[:wide, :], keys, values, None)
        self_out[:wide, :] += sums
        self_total[:wide, :] += totals

        @pl.loop(0, highs)
        def _(high, number=number, kv=kv, text=text):
            block = number * highs + high

            @pl.when(meta.self_flag(block) > 0)
            def _():
                allowed = run_items == meta.run_items(meta.group(block), run_rows, 1)
                sums, totals = attend(
                    q[wide:, :], kv[high, wide:, :LANES], kv[high, wide:, LANES:], allowed
                )
                self_out[wide:, :] += sums
                self_total[wide:, :] += totals

            @pl.when(meta.cross_flag(block) > 0)
            def _():
                allowed = all_items == meta.text_items(meta.group(block), 1)
                sums, totals = attend(
                    q[...], text[high, :, :LANES], text[high, :, LANES:], allowed
                )
                cross_out[...] += sums
                cross_total[...] += totals

    ours = self_out[...] / self_total[...]
    across = cross_out[...] / cross_total[...]
    self_out[...] = ours
    cross_out[...] = across
    combined[...] = (ours + gate[...] * across).astype(BF16)


def attention_call(meta, queries, kvs, texts, gate, runs):
    rows, width = queries.shape
    highs, text_rows = (kvs[0].shape[0], texts[0].shape[1])
    wide = rows // 4
    kv_spec = pl.BlockSpec((highs, rows, 2 * LANES), lambda p, *_: (0, 0, p))
    text_spec = pl.BlockSpec((highs, text_rows, 2 * LANES), lambda p, *_: (0, 0, p))
    float_out = jax.ShapeDtypeStruct((rows, width), F32)
    return pl.pallas_call(
        functools.partial(attention_kernel, runs, highs, wide, text_rows),
        grid_spec=pltpu.PrefetchScalarGridSpec(
            num_scalar_prefetch=1,
            grid=(width // LANES,),
            in_specs=[columns(rows, LANES)]
            + [kv_spec] * 4
            + [text_spec] * 4
            + [columns(1, LANES)],
            out_specs=[columns(rows, LANES)] * 5,
        ),
        out_shape=[jax.ShapeDtypeStruct((rows, width), BF16)] + [float_out] * 4,
        compiler_params=params(56),
        cost_estimate=pl.CostEstimate(
            flops=20_000_000_000, bytes_accessed=20_000_000, transcendentals=0
        ),
        name="attention",
    )(meta, queries, *kvs, *texts, gate)


def attend_back(query, grad, less, key, value, allowed):
    d_key, d_value, d_query = (None, None, None)
    for query_head, grad_head, less_head, key_head in zip(
        halves(query), halves(grad), less, halves(key)
    ):
        weights = jnp.exp2(nt_dot(key, query_head) * SCALING)
        if allowed is not None:
            weights = jnp.where(allowed, weights, 0.0)
        raw = weights * (nt_dot(value, grad_head) + less_head) * GRAD_SCALING
        raw = raw.astype(BF16)
        terms = (
            nn_dot(raw, query_head),
            nn_dot(weights.astype(BF16), grad_head),
            tn_dot(raw, key_head),
        )
        if d_key is None:
            d_key, d_value, d_query = terms
        else:
            d_key, d_value, d_query = (
                d_key + terms[0],
                d_value + terms[1],
                d_query + terms[2],
            )
    return (d_key.astype(BF16), d_value.astype(BF16), d_query)


def attention_back_kernel(
    runs, highs, wide, text_rows, ref, q, g, self_out, cross_out, self_total, cross_total, gate,
    kv0, kv1, kv2, kv3, t0, t1, t2, t3,
    dq, d_same, d_other, dt_same, dt_other, d_gate, self_grad, cross_grad,
):
    meta = Meta(ref, runs, 4 * highs, wide, text_rows)
    rows = q.shape[0]
    run_rows = rows - wide
    own = meta.own()
    run_items = meta.run_items(own, run_rows, 1)
    all_items = meta.all_items(own, rows, 1)
    incoming = g[...]
    d_gate[...] = jnp.sum(incoming * cross_out[...], axis=0, keepdims=True)
    scaled = incoming / self_total[...]
    self_grad[...] = scaled.astype(BF16)
    turned = jnp.transpose(scaled * self_out[...])
    self_less = (
        -jnp.sum(turned[: LANES // 2], axis=0, keepdims=True),
        -jnp.sum(turned[LANES // 2 :], axis=0, keepdims=True),
    )
    scaled = incoming * gate[...] / cross_total[...]
    cross_grad[...] = scaled.astype(BF16)
    turned = jnp.transpose(scaled * cross_out[...])
    cross_less = (
        -jnp.sum(turned[: LANES // 2], axis=0, keepdims=True),
        -jnp.sum(turned[LANES // 2 :], axis=0, keepdims=True),
    )
    wide_less = tuple(row[:, :wide] for row in self_less)
    run_less = tuple(row[:, wide:] for row in self_less)
    dq[...] = jnp.zeros(dq.shape, F32)
    arrays = (
        (kv0, t0, d_same.at[0], dt_same.at[0]),
        (kv1, t1, d_same.at[1], dt_same.at[1]),
        (kv2, t2, d_other.at[0], dt_other.at[0]),
        (kv3, t3, d_other.at[1], dt_other.at[1]),
    )
    for number, (kv, text, dkv, dtext) in enumerate(arrays):
        keys = kv[:, :wide, :LANES].reshape(highs * wide, LANES)
        values = kv[:, :wide, LANES:].reshape(highs * wide, LANES)
        d_key, d_value, d_query = attend_back(
            q[:wide, :], self_grad[:wide, :], wide_less, keys, values, None
        )
        dkv[:, :wide, :LANES] = d_key.reshape(highs, wide, LANES)
        dkv[:, :wide, LANES:] = d_value.reshape(highs, wide, LANES)
        dq[:wide, :] += d_query

        @pl.loop(0, highs)
        def _(high, number=number, kv=kv, text=text, dkv=dkv, dtext=dtext):
            block = number * highs + high

            @pl.when(meta.self_flag(block) > 0)
            def _():
                allowed = meta.run_items(meta.group(block), run_rows, 0) == run_items
                d_key, d_value, d_query = attend_back(
                    q[wide:, :],
                    self_grad[wide:, :],
                    run_less,
                    kv[high, wide:, :LANES],
                    kv[high, wide:, LANES:],
                    allowed,
                )
                dkv[high, wide:, :LANES] = d_key
                dkv[high, wide:, LANES:] = d_value
                dq[wide:, :] += d_query

            @pl.when(meta.self_flag(block) == 0)
            def _():
                dkv[high, wide:, :] = jnp.zeros((run_rows, 2 * LANES), BF16)

            @pl.when(meta.cross_flag(block) > 0)
            def _():
                allowed = meta.text_items(meta.group(block), 0) == all_items
                d_key, d_value, d_query = attend_back(
                    q[...],
                    cross_grad[...],
                    cross_less,
                    text[high, :, :LANES],
                    text[high, :, LANES:],
                    allowed,
                )
                dtext[high, :, :LANES] = d_key
                dtext[high, :, LANES:] = d_value
                dq[...] += d_query

            @pl.when(meta.cross_flag(block) == 0)
            def _():
                dtext[high] = jnp.zeros((text_rows, 2 * LANES), BF16)


def attention_back_call(meta, queries, incoming, outputs, gate, kvs, texts, runs):
    rows, width = queries.shape
    highs, text_rows = (kvs[0].shape[0], texts[0].shape[1])
    wide = rows // 4
    kv_spec = pl.BlockSpec((highs, rows, 2 * LANES), lambda p, *_: (0, 0, p))
    text_spec = pl.BlockSpec((highs, text_rows, 2 * LANES), lambda p, *_: (0, 0, p))
    d_kv = jax.ShapeDtypeStruct((2, *kvs[0].shape), BF16)
    d_text = jax.ShapeDtypeStruct((2, *texts[0].shape), BF16)
    return pl.pallas_call(
        functools.partial(attention_back_kernel, runs, highs, wide, text_rows),
        grid_spec=pltpu.PrefetchScalarGridSpec(
            num_scalar_prefetch=1,
            grid=(width // LANES,),
            in_specs=[columns(rows, LANES)] * 6
            + [columns(1, LANES)]
            + [kv_spec] * 4
            + [text_spec] * 4,
            out_specs=[columns(rows, LANES)]
            + [pl.BlockSpec((2, highs, rows, 2 * LANES), lambda p, *_: (0, 0, 0, p))] * 2
            + [pl.BlockSpec((2, highs, text_rows, 2 * LANES), lambda p, *_: (0, 0, 0, p))] * 2
            + [columns(1, LANES)],
            scratch_shapes=[pltpu.VMEM((rows, LANES), BF16)] * 2,
        ),
        out_shape=[jax.ShapeDtypeStruct((rows, width), F32), d_kv, d_kv, d_text, d_text]
        + [jax.ShapeDtypeStruct((1, width), F32)],
        compiler_params=params(60),
        cost_estimate=pl.CostEstimate(
            flops=30_000_000_000, bytes_accessed=30_000_000, transcendentals=0
        ),
        name="attention_back",
    )(meta, queries, incoming, *outputs, gate, *kvs, *texts)


def separate(array, kinds):
    pairs = array.shape[-1] // LANES // kinds
    return [
        jnp.concatenate(
            [
                array[..., (p * kinds + kind) * LANES : (p * kinds + kind + 1) * LANES]
                for p in range(pairs)
            ],
            axis=-1,
        )
        for kind in range(kinds)
    ]


def on_device(
    patches,
    cotangent,
    item_lengths,
    timesteps,
    patch_rows,
    patch_cols,
    conditioning,
    text_states,
    gain_attn,
    gain_ffn,
    query_gain,
    key_gain,
    text_key_gain,
    cross_gate,
    w_query,
    w_key,
    w_value,
    w_out,
    w_text_key,
    w_text_value,
    w_gate,
    w_up,
    w_down,
    w_ada,
    w_text,
):
    at = Place()
    tok_dev, model_width = patches.shape
    shard_rows = w_query.shape[0]
    head_dim = query_gain.shape[0]
    local_width = w_query.shape[1]
    heads_local = local_width // head_dim
    text_rows = text_states.shape[0]
    item_count = conditioning.shape[0]
    quarter = tok_dev // 4
    hidden_width = w_gate.shape[1]

    shards = [w_query, w_key, w_value]
    shared_qkv = share(shards, by_pairs(shards), at)
    qkv_rows = GatherRows(shared_qkv, 0, [3 * local_width], at)
    qkv_rows.z()
    first = [shared_qkv[2]]
    text_width = w_text.shape[1]
    shards = [w_text, w_text_key, w_text_value, w_out, w_down, w_gate, w_up]
    order = side_by_side(shards)
    order[1:3] = [
        (1 + source, start, width)
        for source, start, width in by_pairs([w_text_key, w_text_value])
    ]
    shared = share(shards, order, at, [qkv_rows.stacked])
    places = [0]
    for width in (text_width + 2 * local_width, local_width, hidden_width):
        places.append(places[-1] + width)
    qkv_rows.y()
    text_rows_all = GatherRows(shared, places[0], [text_width, 2 * local_width], at)
    out_rows = GatherRows(shared, places[1], [local_width], at)
    down_rows = GatherRows(shared, places[2], [hidden_width], at)
    gu_rows = GatherRows(shared, places[3], [2 * hidden_width], at)
    embed_pre = conditioning.astype(F32) + time_embed(timesteps, model_width)
    embed = jax.nn.silu(embed_pre).astype(BF16)
    own_embed = lax.dynamic_slice_in_dim(embed, at.data * shard_rows, shard_rows, 1)
    gains = lax.dynamic_update_slice(
        jnp.zeros((2, model_width), F32),
        jnp.stack([gain_attn, gain_ffn]).astype(F32),
        (0, at.data * shard_rows),
    )
    head_sums = butterfly(
        after(jnp.concatenate([multiply(own_embed, w_ada), gains], axis=0), *first),
        at,
        model=False,
        z_wait=[qkv_rows.near],
    )
    my_patches = swap_rows(after(patches, *first), at)
    text_rows_all.z()
    (full_qkv,) = qkv_rows.core()
    positions = swap_roles(
        after(jnp.stack([patch_rows, patch_cols]).astype(F32), head_sums)
    )
    gain_attn32, gain_ffn32 = (head_sums[item_count], head_sums[item_count + 1])
    mod_part = head_sums[:item_count]
    mod_pair = jnp.stack(
        unmix([mod_part, lax.ppermute(mod_part, "mp", [(i, i ^ 1) for i in range(4)])], at.c)
    )
    mod_all = jnp.stack(
        unmix([mod_pair, lax.ppermute(mod_pair, "mp", [(i, i ^ 2) for i in range(4)])], at.x)
    )
    shift1_t, gate1_t, shift2_t, gate2_t = mod_all.reshape(4, item_count, model_width)

    token_items = item_ids(item_lengths, tok_dev, at.n_dp).reshape(at.n_dp, tok_dev)
    own_items = pick(token_items, at.tokens)
    item_labels = jnp.arange(item_count, dtype=jnp.int32)
    onehot = (own_items[:, None] == item_labels[None, :]).astype(F32)
    runs = item_lengths.shape[0]
    groups = jnp.stack(relative_groups(at)).astype(jnp.int32)
    firsts, lasts = (token_items[:, tok_dev // 4], token_items[:, tok_dev - 1])
    my_first, my_last = (pick(firsts, at.tokens), pick(lasts, at.tokens))
    self_flags = (firsts[groups] <= my_last) & (lasts[groups] >= my_first)
    text_first = groups * text_rows // TTOK
    text_last = (groups * text_rows + text_rows - 1) // TTOK
    cross_flags = ((text_first <= my_last) & (text_last >= my_first)) | (text_last >= runs)
    meta = jnp.concatenate(
        [
            jnp.cumsum(item_lengths),
            groups,
            at.tokens[None],
            self_flags.astype(jnp.int32),
            cross_flags.astype(jnp.int32),
        ]
    ).astype(jnp.int32)
    few_items = lax.dynamic_slice_in_dim(own_items, at.features * quarter, quarter)
    few_onehot = lax.dynamic_slice_in_dim(onehot, at.features * quarter, quarter)

    shift1 = rows_of(shift1_t, own_items)
    inputs = my_patches.astype(F32)
    normed1, _ = norm_fwd(inputs, gain_attn32)
    hidden1 = (normed1 * (1.0 + shift1)).astype(BF16)

    angles = rope_angles(positions[0], positions[1], head_dim)
    both_heads = (1, LANES // head_dim)
    cosine, sine = (jnp.cos(angles), jnp.sin(angles))
    split = head_dim // 4
    cosine = jnp.tile(
        jnp.concatenate([cosine[:, :split]] * 2 + [cosine[:, split:]] * 2, axis=1), both_heads
    )
    sine = jnp.tile(
        jnp.concatenate(
            [-sine[:, :split], sine[:, :split], -sine[:, split:], sine[:, split:]], axis=1
        ),
        both_heads,
    )
    query_gain32, key_gain32, text_gain32 = (
        jnp.tile(gain.astype(F32)[None], both_heads)
        for gain in (query_gain, key_gain, text_key_gain)
    )
    query_pre, key_pre, queries, own_kv = qkv_call(
        hidden1, full_qkv, cosine, sine, query_gain32, key_gain32
    )
    kv_tokens = GatherTokens(own_kv, at)
    kv_tokens.z()
    text_rows_all.y()
    kv_tokens.y()
    my_text = swap_roles(after(text_states, head_sums))
    full_text, full_tkv = text_rows_all.core(kv_tokens.near)
    out_rows.z()
    words = sum_features(multiply_trans(my_text, full_text).astype(BF16), at)
    out_rows.y()
    text_pre, own_text_kv = text_call(words, full_tkv, text_gain32)
    text_tokens = GatherTokens(own_text_kv, at)
    text_tokens.z()
    text_tokens.y()
    my_cotangent = swap_rows(cotangent, at)
    gu_rows.z()
    gu_rows.y()
    (full_out,) = out_rows.core()
    gate_local = jnp.tanh(
        lax.dynamic_slice_in_dim(cross_gate.astype(F32), at.features * heads_local, heads_local)
    )
    gate_wide = jnp.repeat(gate_local, head_dim)[None]
    all_kv, all_text_kv = (kv_tokens.core(), text_tokens.core())
    combined, *outputs = attention_call(meta, queries, all_kv, all_text_kv, gate_wide, runs)
    few_inputs = lax.dynamic_slice_in_dim(inputs, at.features * quarter, quarter)
    few_normed1 = lax.dynamic_slice_in_dim(normed1, at.features * quarter, quarter)
    tanh_one = jnp.tanh(rows_of(gate1_t, few_items))
    tanh_two = jnp.tanh(rows_of(gate2_t, few_items))
    shift2 = rows_of(shift2_t, few_items)
    few_shift1 = rows_of(shift1_t, few_items)
    combined_out = after(combined, gu_rows.near)
    branch = sum_quarters(multiply_trans(combined_out, full_out).astype(BF16), at)
    down_rows.z()
    down_rows.y()
    middle = few_inputs + tanh_one * branch
    normed2, scale2 = norm_fwd(middle, gain_ffn32)
    hidden2 = gather_quarters((normed2 * (1.0 + shift2)).astype(BF16), at)
    (full_gu,) = gu_rows.core(combined)
    (full_down,) = down_rows.core(combined)
    gate_up = multiply(hidden2, full_gu)
    gate_pre, up_pre = (gate_up[:, :hidden_width], gate_up[:, hidden_width:])
    logistic = jax.nn.sigmoid(gate_pre)
    silu_gate = gate_pre * logistic
    inner_act = (silu_gate * up_pre).astype(BF16)

    grad_output = my_cotangent.astype(F32)
    few_output = lax.dynamic_slice_in_dim(grad_output, at.features * quarter, quarter)
    grad_ffn = (grad_output * rows_of(jnp.tanh(gate2_t), own_items)).astype(BF16)
    grad_inner = multiply(grad_ffn, full_down)
    grad_gate = (grad_inner * up_pre * logistic * (1.0 + gate_pre * (1.0 - logistic))).astype(BF16)
    grad_up = (grad_inner * silu_gate).astype(BF16)
    grad_gu = jnp.concatenate([grad_gate, grad_up], axis=1)
    hidden2_part = multiply_trans(grad_gu, full_gu).astype(BF16)
    grad_hidden2 = sum_quarters(hidden2_part, at)
    ffn_sums = ScatterRows(
        [
            trans_multiply(after(grad_ffn, hidden2_part), inner_act),
            trans_multiply(after(hidden2, hidden2_part), grad_gu),
        ],
        at,
    )
    ffn_sums.y()
    grad_middle_norm, gain_ffn_term = norm_back(
        middle, scale2, gain_ffn32, grad_hidden2 * (1.0 + shift2)
    )
    grad_middle = few_output + grad_middle_norm
    grad_branch = gather_quarters((grad_middle * tanh_one).astype(BF16), at)
    grad_combined = multiply(grad_branch, full_out)
    ffn_part = multiply_trans(after(inner_act, grad_combined), full_down).astype(BF16)
    ffn_out = sum_quarters(ffn_part, at)
    out_sums = ScatterRows([trans_multiply(grad_branch, combined)], at)
    out_sums.y()
    grad_queries, d_same, d_other, dt_same, dt_other, gate_terms = attention_back_call(
        meta, queries, grad_combined, outputs, gate_wide, all_kv, all_text_kv, runs
    )
    out_sums.z()
    text_sums = ScatterTokens(dt_same, dt_other, at)
    kv_sums = ScatterTokens(d_same, d_other, at)
    text_sums.y()
    kv_sums.y()
    text_back = text_sums.z()
    ffn_sums.z()
    grad_gate_local = jnp.sum(gate_terms.reshape(heads_local, head_dim), axis=1) * (
        1.0 - gate_local * gate_local
    )
    grad_tkv, text_gain_term = text_back_call(text_back, text_pre, text_gain32)
    grad_words = sum_features(multiply_trans(grad_tkv, full_tkv).astype(BF16), at)
    kv_back = kv_sums.z()
    mixed_out = gather_output((middle + tanh_two * ffn_out).astype(BF16), at)
    words_sums = ScatterRows(
        [trans_multiply(grad_words, my_text), trans_multiply(words, grad_tkv)], at
    )
    words_sums.y()
    grad_qkv, query_gain_term, key_gain_term = qkv_back_call(
        grad_queries, kv_back, query_pre, key_pre, cosine, sine, query_gain32, key_gain32
    )
    hidden1_part = multiply_trans(grad_qkv, full_qkv).astype(BF16)
    grad_hidden1 = sum_quarters(hidden1_part, at)
    qkv_sums = ScatterRows([trans_multiply(after(hidden1, hidden1_part), grad_qkv)], at)
    few_scale1 = lax.rsqrt(jnp.mean(few_inputs * few_inputs, axis=-1, keepdims=True) + EPSILON)
    grad_inputs_norm, gain_attn_term = norm_back(
        few_inputs, few_scale1, gain_attn32, grad_hidden1 * (1.0 + few_shift1)
    )
    grad_patches = gather_output((grad_middle + grad_inputs_norm).astype(BF16), at).astype(F32)
    words_sums.z()
    qkv_sums.y()
    qkv_sums.z()
    grads_out, grads_ffn = (out_sums.result(), ffn_sums.result())
    grads_texts, grads_qkv = (words_sums.result(), qkv_sums.result())
    grad_text = swap_roles(multiply(grad_words, full_text).astype(BF16)).astype(F32)
    def item_sums(rows):
        return trans_multiply(few_onehot, rows, HIGHEST)

    gate_full = lax.dynamic_update_slice_in_dim(
        jnp.zeros((cross_gate.shape[0],), F32),
        grad_gate_local,
        at.features * heads_local,
        0,
    )
    small = jnp.concatenate(
        [
            jnp.sum(query_gain_term.reshape(heads_local, head_dim), axis=0),
            jnp.sum(key_gain_term.reshape(heads_local, head_dim), axis=0),
            jnp.sum(text_gain_term.reshape(heads_local, head_dim), axis=0),
            gate_full,
        ]
    )
    small = jnp.pad(small, (0, model_width - small.shape[0]))
    late = butterfly(
        jnp.concatenate(
            [
                item_sums(
                    jnp.concatenate(
                        [
                            grad_hidden1 * few_normed1,
                            grad_middle * branch * (1.0 - tanh_one * tanh_one),
                            grad_hidden2 * normed2,
                            few_output * ffn_out * (1.0 - tanh_two * tanh_two),
                        ],
                        axis=1,
                    )
                )
                .reshape(item_count, 4, model_width)
                .swapaxes(0, 1)
                .reshape(4 * item_count, model_width),
                jnp.sum(gain_attn_term, axis=0, keepdims=True),
                jnp.sum(gain_ffn_term, axis=0, keepdims=True),
                small[None],
            ],
            axis=0,
        ),
        at,
    )
    grad_mod_own = pick(late[: 4 * item_count].reshape(4, item_count, model_width), at.model)
    late = late[4 * item_count :]
    small = late[2]
    grad_ada = trans_multiply(own_embed.astype(F32), grad_mod_own, HIGHEST)
    grad_embed_part = multiply_trans(grad_mod_own, w_ada.astype(F32), HIGHEST)
    grad_embed = butterfly(
        lax.dynamic_update_slice(
            jnp.zeros((item_count, model_width), F32),
            grad_embed_part,
            (0, at.data * shard_rows),
        ),
        at,
    )
    embed_logistic = jax.nn.sigmoid(embed_pre)
    grad_conditioning = grad_embed * embed_logistic * (1.0 + embed_pre * (1.0 - embed_logistic))
    own_gain = lambda row: lax.dynamic_slice_in_dim(row, at.data * shard_rows, shard_rows)
    grad_wq, grad_wk, grad_wv = separate(grads_qkv, 3)
    grad_wtk, grad_wtv = separate(grads_texts[:, text_width:], 2)
    return (
        mixed_out,
        grad_patches,
        grad_conditioning,
        grad_text,
        own_gain(late[0]),
        own_gain(late[1]),
        small[:head_dim],
        small[head_dim : 2 * head_dim],
        small[2 * head_dim : 3 * head_dim],
        small[3 * head_dim : 3 * head_dim + cross_gate.shape[0]],
        grad_wq,
        grad_wk,
        grad_wv,
        grads_out,
        grad_wtk,
        grad_wtv,
        grads_ffn[:, hidden_width : 2 * hidden_width],
        grads_ffn[:, 2 * hidden_width :],
        grads_ffn[:, :hidden_width],
        grad_ada,
        grads_texts[:, :text_width],
    )


def solution(mesh):
    rows, both, one = (P("dp", None), P("dp", "mp"), P("dp"))
    whole = P()
    in_specs = (
        (rows, rows, whole, whole, one, one, whole, both, one, one)
        + (whole,) * 4
        + (both,) * 11
    )
    out_specs = (
        (rows, rows, whole, both, one, one) + (whole,) * 4 + (both,) * 11
    )
    return jax.shard_map(
        on_device, mesh=mesh, in_specs=in_specs, out_specs=out_specs, check_vma=False
    )
```

```python
import functools
import math

import jax
import jax.numpy as jnp
from jax import lax
from jax.experimental import pallas as pl
from jax.experimental.pallas import tpu as pltpu
from jax.sharding import PartitionSpec as P

TTOK = 256
HIGHEST = lax.Precision.HIGHEST
EPSILON = 1e-06
SCORE_BASE = 1.4426950408889634
TWO_NATURAL = 0.6931471805599453
AXES = ("dp", "mp")
DEPTH = 2
LANES = 128
F32 = jnp.float32
BF16 = jnp.bfloat16


def contract(left, right, pairing, precision=None):
    return lax.dot_general(
        left, right, (pairing, ((), ())), precision=precision, preferred_element_type=F32
    )


def multiply(left, right):
    return contract(left, right, ((1,), (0,)))


def multiply_trans(left, right, precision=None):
    return contract(left, right, ((1,), (1,)), precision)


def trans_multiply(left, right, precision=None):
    return contract(left, right, ((0,), (0,)), precision)


def time_embed(steps, model_width):
    halfway = model_width // 2
    frequency = jnp.exp(-math.log(10000.0) * jnp.arange(halfway, dtype=F32) / halfway)
    phases = steps.astype(F32)[:, None] * frequency[None, :]
    return jnp.concatenate([jnp.cos(phases), jnp.sin(phases)], axis=1)


def rope_angles(rows_pos, cols_pos, head_dim):
    quarter = head_dim // 4
    frequency = jnp.exp(-math.log(10000.0) * jnp.arange(quarter, dtype=F32) / quarter)
    return jnp.concatenate(
        [
            rows_pos.astype(F32)[:, None] * frequency[None, :],
            cols_pos.astype(F32)[:, None] * frequency[None, :],
        ],
        axis=1,
    )


def item_ids(lengths, tok_dev, n_dev):
    wide_dev = tok_dev // 4
    boundary = jnp.cumsum(lengths)
    position = jnp.arange(tok_dev * n_dev, dtype=jnp.int32)
    within = position % tok_dev
    placed = position // tok_dev * (tok_dev - wide_dev) + within - wide_dev
    counted = jnp.sum((boundary[None, :] <= placed[:, None]).astype(jnp.int32), axis=1)
    return jnp.where(within < wide_dev, lengths.shape[0], counted)


def norm_fwd(values, gain_vec):
    scaling = lax.rsqrt(jnp.mean(values * values, axis=-1, keepdims=True) + EPSILON)
    return (values * scaling * gain_vec, scaling)


def norm_back(values, scaling, gain_vec, incoming):
    weighted = incoming * gain_vec
    inner_mean = jnp.mean(weighted * values, axis=-1, keepdims=True)
    return (
        scaling * weighted - values * scaling * scaling * scaling * inner_mean,
        incoming * values * scaling,
    )


def codes(index):
    data, model = divmod(index, 4)
    return (data // 4, data // 2 % 2, data % 2, model // 2, model % 2)


def place(dh, zl, dy, x, c):
    return ((dh * 2 + zl) * 2 + dy) * 4 + x * 2 + c


def move(values, where, only=None):
    count = lax.axis_size("dp") * lax.axis_size("mp")
    pairs = [
        (i, place(*where(*codes(i)))) for i in range(count) if only is None or only(*codes(i))
    ]
    return lax.ppermute(values, AXES, pairs)


def swap_roles(values):
    return move(values, lambda dh, zl, dy, x, c: (dh, c, dy, x, zl))


def swap_rows(values, at):
    rows, width = values.shape
    away = lambda dh, zl, dy, x, c: zl != c
    over_z = lambda piece: move(piece, lambda dh, zl, dy, x, c: (dh, zl ^ 1, dy, x, c ^ 1), away)
    got = at.along_z.send(over_z, pick(values.reshape(2, rows // 2, width), at.x))
    other = move(got, lambda dh, zl, dy, x, c: (dh, zl, dy, x ^ 1, c), away)
    swapped = jnp.concatenate(unmix([got, other], at.x), axis=0)
    return jnp.where(at.c == at.zl, values, swapped)


def other_core(values):
    return move(values, lambda dh, zl, dy, x, c: (dh, zl, dy, x, c ^ 1))


def other_y(values):
    return move(values, lambda dh, zl, dy, x, c: (dh, zl, dy ^ 1, x, c))


def other_high(values, high):
    return move(values, lambda dh, zl, dy, x, c: (dh ^ high, zl, dy, x, c))


def other_feature(values, other):
    return move(values, lambda dh, zl, dy, x, c: (dh, zl ^ (other & 1), dy, x ^ (other >> 1), c))


def pick(values, index, axis=0):
    return lax.dynamic_index_in_dim(values, index, axis, keepdims=False)


def after(values, *events):
    if not events:
        return values
    return lax.optimization_barrier((values, *events))[0]


class Link:
    def __init__(self, depth):
        self.depth = depth
        self.ended = []

    def send(self, how, values, *rest):
        if len(self.ended) >= self.depth:
            values = after(values, self.ended[-self.depth])
        result = how(values, *rest)
        self.ended.append(result)
        return result


class Place:
    def __init__(self):
        self.along_z, self.along_y = (Link(DEPTH), Link(1))
        data, model = (lax.axis_index("dp"), lax.axis_index("mp"))
        self.data, self.model = (data, model)
        self.n_dp = lax.axis_size("dp")
        self.highs = self.n_dp // 4
        self.dh, self.zl, self.dy = (data // 4, data // 2 % 2, data % 2)
        self.x, self.c = (model // 2, model % 2)
        self.tokens = (self.dh * 2 + self.c) * 2 + self.dy
        self.features = self.x * 2 + self.zl


def unmix(parts, index):
    count = len(parts)
    ordered = []
    for spot in range(count):
        value = parts[spot]
        for other in range(1, count):
            value = jnp.where(index == other, parts[spot ^ other], value)
        ordered.append(value)
    return ordered


def pack_kernel(order, *refs):
    core = lax.axis_index("mp") % 2
    for out, side in zip(refs[-2:], (core, core ^ 1)):
        start = 0
        for source, first, width in order:
            out[:, start : start + width] = refs[source][side, :, first : first + width]
            start += width


def pack(shards, order):
    half = shards[0].shape[0] // 2
    width = sum(part[2] for part in order)
    result = jax.ShapeDtypeStruct((half, width), shards[0].dtype)
    return pl.pallas_call(
        functools.partial(pack_kernel, order),
        out_shape=[result, result],
        compiler_params=params(),
        cost_estimate=pl.CostEstimate(
            flops=0, bytes_accessed=8 * half * width, transcendentals=0
        ),
        name="pack",
    )(*[shard.reshape(2, half, shard.shape[1]) for shard in shards])


def by_pairs(shards):
    return [
        (source, first, LANES)
        for first in range(0, shards[0].shape[1], LANES)
        for source in range(len(shards))
    ]


def side_by_side(shards):
    return [(source, 0, shard.shape[1]) for source, shard in enumerate(shards)]


def pack_kernel(order, *refs):
    core = lax.axis_index("mp") % 2
    for out, side in zip(refs[-2:], (core, core ^ 1)):
        start = 0
        for source, first, width in order:
            out[:, start : start + width] = refs[source][side, :, first : first + width]
            start += width


def pack(shards, order):
    half = shards[0].shape[0] // 2
    width = sum(part[2] for part in order)
    result = jax.ShapeDtypeStruct((half, width), shards[0].dtype)
    return pl.pallas_call(
        functools.partial(pack_kernel, order),
        out_shape=[result, result],
        compiler_params=params(),
        cost_estimate=pl.CostEstimate(
            flops=0, bytes_accessed=8 * half * width, transcendentals=0
        ),
        name="pack",
    )(*[shard.reshape(2, half, shard.shape[1]) for shard in shards])


def by_pairs(shards):
    return [
        (source, first, LANES)
        for first in range(0, shards[0].shape[1], LANES)
        for source in range(len(shards))
    ]


def side_by_side(shards):
    return [(source, 0, shard.shape[1]) for source, shard in enumerate(shards)]


def assemble_kernel(highs, near, beside, near_core, beside_core, full):
    data, core = (lax.axis_index("dp"), lax.axis_index("mp") % 2)
    high, y = (data // 4, data % 2)
    for block, from_y, from_core in (
        (near, y, core),
        (beside, y ^ 1, core),
        (near_core, y, core ^ 1),
        (beside_core, y ^ 1, core ^ 1),
    ):
        for a in range(highs):
            for b in (0, 1):
                full[high ^ a, from_core ^ b, from_y, from_core] = block[a, b]


def assemble(near, beside, near_core, beside_core):
    highs, _, half, width = near.shape
    step = math.gcd(width, 512) if width % 384 else 384
    part = pl.BlockSpec((highs, 2, half, step), lambda i: (0, 0, 0, i))
    return pl.pallas_call(
        functools.partial(assemble_kernel, highs),
        grid=(width // step,),
        in_specs=[part] * 4,
        out_specs=pl.BlockSpec((highs, 2, 2, 2, half, step), lambda i: (0,) * 5 + (i,)),
        out_shape=jax.ShapeDtypeStruct((highs, 2, 2, 2, half, width), near.dtype),
        compiler_params=params(),
        cost_estimate=pl.CostEstimate(
            flops=0, bytes_accessed=32 * highs * half * width, transcendentals=0
        ),
        name="assemble",
    )(near, beside, near_core, beside_core)


class Events:
    def __init__(self, **events):
        self.__dict__.update(events)


def assemble_kernel(near, beside, near_core, beside_core, full):
    y, core = (lax.axis_index("dp") % 2, lax.axis_index("mp") % 2)
    for block, from_y, from_core in (
        (near, y, core),
        (beside, y ^ 1, core),
        (near_core, y, core ^ 1),
        (beside_core, y ^ 1, core ^ 1),
    ):
        for z in range(near.shape[0]):
            full[z, from_y, from_core] = block[z]


def assemble(blocks, first, width):
    count, half, _ = blocks[0].shape
    step = next(step for step in (512, 384, 256, LANES) if first % step == width % step == 0)
    part = pl.BlockSpec((count, half, step), lambda i: (0, 0, first // step + i))
    full = pl.pallas_call(
        assemble_kernel,
        grid=(width // step,),
        in_specs=[part] * 4,
        out_specs=pl.BlockSpec((count, 2, 2, half, step), lambda i: (0,) * 4 + (i,)),
        out_shape=jax.ShapeDtypeStruct((count, 2, 2, half, width), BF16),
        compiler_params=params(),
        cost_estimate=pl.CostEstimate(
            flops=0, bytes_accessed=16 * count * half * width, transcendentals=0
        ),
        name="assemble",
    )(*blocks)
    return full.reshape(4 * count * half, width)


def exchange_z(values):
    count = lax.axis_size("dp")
    return lax.all_to_all(
        values, "dp", 0, 0, axis_index_groups=[list(range(y, count, 2)) for y in (0, 1)], tiled=True
    )


def exchange_features(values):
    highs = lax.axis_size("dp") // 4
    groups = [
        [place(dh, zl, dy, x, c) for x in (0, 1) for zl in (0, 1)]
        for dh in range(highs)
        for dy in (0, 1)
        for c in (0, 1)
    ]
    return lax.all_to_all(values, AXES, 0, 0, axis_index_groups=groups, tiled=True)


def share(shards, order, at, c_wait=()):
    mine, theirs = pack([after(shard, *c_wait) for shard in shards], order)
    got = other_core(theirs)
    return (jnp.where(at.c == 0, mine, got), jnp.where(at.c == 0, got, mine), got)


class GatherRows:
    def __init__(self, shared, first, widths, at):
        self.at, self.widths = (at, widths)
        pieces = [piece[:, first : first + sum(widths)] for piece in shared[:2]]
        self.stacked = jnp.stack(pieces * at.highs)

    def z(self):
        self.near = self.at.along_z.send(exchange_z, self.stacked)

    def y(self):
        self.beside = self.at.along_y.send(other_y, self.near)

    def core(self, *events):
        near, beside = (after(self.near, *events), after(self.beside, *events))
        blocks = (near, beside, other_core(near), other_core(beside))
        fulls, start = ([], 0)
        for width in self.widths:
            fulls.append(assemble(blocks, start, width))
            start += width
        return fulls


class ScatterRows:
    def __init__(self, grads, at):
        self.at = at
        half = grads[0].shape[0] // at.n_dp // 2
        self.views = [grad.astype(BF16).reshape(at.n_dp // 2, 2, 2, half, -1) for grad in grads]
        self.from_core = other_core(
            jnp.concatenate([pick(view, 1 - at.c, 2) for view in self.views], axis=-1)
        )
        self.to_y = self.kept_rows(1 - at.dy).astype(BF16)

    def kept_rows(self, y):
        own = [pick(pick(view, y, 1), self.at.c, 1) for view in self.views]
        own = jnp.concatenate(own, axis=-1).astype(F32)
        return own + pick(self.from_core, y, 1).astype(F32)

    def y(self):
        from_y = self.at.along_y.send(other_y, self.to_y)
        self.to_z = (self.kept_rows(self.at.dy) + from_y.astype(F32)).astype(BF16)

    def z(self):
        self.from_z = self.at.along_z.send(exchange_z, self.to_z)

    def result(self):
        at = self.at
        sums = [
            sum(self.from_z[2 * a + zl].astype(F32) for a in range(at.highs)) for zl in (0, 1)
        ]
        mine, theirs = (jnp.where(at.c == 0, *sums), jnp.where(at.c == 0, *sums[::-1]))
        other = other_core(theirs.astype(BF16)).astype(F32)
        return jnp.concatenate(unmix([mine, other], at.c), axis=0)


class GatherTokens:
    def __init__(self, block, at):
        self.block, self.at = (block, at)

    def z(self):
        far = [
            self.at.along_z.send(other_high, self.block, a) for a in range(1, self.at.highs)
        ]
        self.near = jnp.stack([self.block] + far)

    def y(self):
        self.beside = self.at.along_y.send(other_y, self.near)

    def core(self):
        return [self.near, self.beside, other_core(self.near), other_core(self.beside)]


class ScatterTokens:
    def __init__(self, same, other, at):
        self.at = at
        self.total = same.astype(F32) + other_core(other).astype(F32)
        self.to_y = self.total[1].astype(BF16)

    def y(self):
        from_y = self.at.along_y.send(other_y, self.to_y)
        self.total = self.total[0] + from_y.astype(F32)

    def z(self):
        result = self.total[0]
        for a in range(1, self.at.highs):
            got = self.at.along_z.send(other_high, self.total[a].astype(BF16), a)
            result = result + got.astype(F32)
        return result


def relative_groups(at):
    return [
        ((at.dh ^ a) * 2 + (at.c ^ core)) * 2 + (at.dy ^ y)
        for core in (0, 1)
        for y in (0, 1)
        for a in range(at.highs)
    ]


def sum_quarters(part, at):
    rows, width = part.shape
    parts = at.along_z.send(exchange_features, part.reshape(4, rows // 4, width))
    return jnp.sum(parts.astype(F32), axis=0)


def gather_quarters(own, at):
    rows, width = own.shape
    parts = at.along_z.send(
        exchange_features, jnp.broadcast_to(own[None], (4, rows, width))
    )
    return parts.reshape(4 * rows, width)


def sum_features(part, at):
    for other, link in ((1, at.along_z), (2, None)):
        got = link.send(other_feature, part, other) if link else other_feature(part, other)
        part = (part.astype(F32) + got.astype(F32)).astype(BF16)
    return part


def gather_output(own, at):
    to_x = lambda part, a: move(part, lambda dh, zl, dy, x, c: (dh, c, dy, x ^ a, zl))
    near = [at.along_z.send(to_x, own, a) for a in (0, 1)]
    near = jnp.stack(unmix(near, at.x))
    far = other_core(near)
    first, second = (jnp.where(at.c == 0, near, far), jnp.where(at.c == 0, far, near))
    return jnp.stack([first, second], axis=1).reshape(4 * own.shape[0], own.shape[1])


def butterfly(values, at, data=True, model=True, z_wait=()):
    for bit in (1, 2) if model else ():
        values = values + lax.ppermute(values, "mp", [(i, i ^ bit) for i in range(4)])
    bit = 1
    while data and bit < at.n_dp:
        if bit == 2:
            values = after(values, *z_wait)
        values = values + lax.ppermute(values, "dp", [(i, i ^ bit) for i in range(at.n_dp)])
        bit *= 2
    return values


def rows_of(table, items):
    value = jnp.broadcast_to(table[0][None], (items.shape[0], table.shape[1]))
    for item in range(1, table.shape[0]):
        value = jnp.where(items[:, None] == item, table[item][None], value)
    return value


def halves(values):
    lane = lax.broadcasted_iota(jnp.int32, (1, LANES), 1)
    low = lane < LANES // 2
    zero = jnp.zeros((), values.dtype)
    return (jnp.where(low, values, zero), jnp.where(low, zero, values))


def pair_select(first, second):
    lane = lax.broadcasted_iota(jnp.int32, (1, LANES), 1)
    return jnp.where(lane < LANES // 2, first, second)


def pair_mean(values):
    low, high = halves(values)
    return pair_select(
        jnp.sum(low, axis=-1, keepdims=True), jnp.sum(high, axis=-1, keepdims=True)
    ) * (2.0 / LANES)


def partner(values):
    lane = lax.broadcasted_iota(jnp.int32, (1, LANES), 1)
    return jnp.where(
        lane % 32 < 16, pltpu.roll(values, LANES - 16, 1), pltpu.roll(values, 16, 1)
    )


def pair_norm(values, gain):
    return values * lax.rsqrt(pair_mean(values * values) + EPSILON) * gain


def pair_norm_back(values, gain, incoming):
    scaling = lax.rsqrt(pair_mean(values * values) + EPSILON)
    weighted = incoming * gain
    inner_mean = pair_mean(weighted * values)
    return (
        scaling * weighted - values * scaling * scaling * scaling * inner_mean,
        jnp.sum(incoming * values * scaling, axis=0, keepdims=True),
    )


def params(megabytes=48):
    return pltpu.CompilerParams(vmem_limit_bytes=megabytes * 1024 * 1024)


def whole(shape):
    return pl.BlockSpec(shape, lambda p, *_: (0,) * len(shape))


def columns(rows, width):
    return pl.BlockSpec((rows, width), lambda p, *_: (0, p))


def qkv_kernel(x, w, cosine, sine, q_gain, k_gain, q_pre, k_pre, q_out, kv_out):
    made = jnp.dot(x[...], w[...], preferred_element_type=F32)
    query, key = (made[:, :LANES], made[:, LANES : 2 * LANES])
    q_pre[...] = query
    k_pre[...] = key
    query = pair_norm(query, q_gain[...])
    key = pair_norm(key, k_gain[...])
    q_out[...] = (query * cosine[...] + partner(query) * sine[...]).astype(BF16)
    kv_out[:, :LANES] = (key * cosine[...] + partner(key) * sine[...]).astype(BF16)
    kv_out[:, LANES:] = made[:, 2 * LANES :].astype(BF16)


def qkv_call(hidden, weights, cosine, sine, q_gain, k_gain):
    rows, depth = hidden.shape
    pairs = weights.shape[1] // (3 * LANES)
    width = pairs * LANES
    return pl.pallas_call(
        qkv_kernel,
        grid=(pairs,),
        in_specs=[
            whole((rows, depth)),
            columns(depth, 3 * LANES),
            whole((rows, LANES)),
            whole((rows, LANES)),
            whole((1, LANES)),
            whole((1, LANES)),
        ],
        out_specs=[columns(rows, LANES)] * 3 + [columns(rows, 2 * LANES)],
        out_shape=[
            jax.ShapeDtypeStruct((rows, width), F32),
            jax.ShapeDtypeStruct((rows, width), F32),
            jax.ShapeDtypeStruct((rows, width), BF16),
            jax.ShapeDtypeStruct((rows, 2 * width), BF16),
        ],
        compiler_params=params(),
        cost_estimate=pl.CostEstimate(
            flops=6 * rows * depth * width, bytes_accessed=8_000_000, transcendentals=0
        ),
        name="qkv",
    )(hidden, weights, cosine, sine, q_gain, k_gain)


def qkv_back_kernel(dq, dkv, q_pre, k_pre, cosine, sine, q_gain, k_gain, out, dq_gain, dk_gain):
    query, key = (dq[...], dkv[:, :LANES])
    query = query * cosine[...] - partner(query) * sine[...]
    key = key * cosine[...] - partner(key) * sine[...]
    query, dq_gain[...] = pair_norm_back(q_pre[...], q_gain[...], query)
    key, dk_gain[...] = pair_norm_back(k_pre[...], k_gain[...], key)
    out[:, :LANES] = query.astype(BF16)
    out[:, LANES : 2 * LANES] = key.astype(BF16)
    out[:, 2 * LANES :] = dkv[:, LANES:].astype(BF16)


def qkv_back_call(dq, dkv, q_pre, k_pre, cosine, sine, q_gain, k_gain):
    rows, width = dq.shape
    pairs = width // LANES
    return pl.pallas_call(
        qkv_back_kernel,
        grid=(pairs,),
        in_specs=[columns(rows, LANES), columns(rows, 2 * LANES)]
        + [columns(rows, LANES)] * 2
        + [whole((rows, LANES))] * 2
        + [whole((1, LANES))] * 2,
        out_specs=[columns(rows, 3 * LANES), columns(1, LANES), columns(1, LANES)],
        out_shape=[
            jax.ShapeDtypeStruct((rows, 3 * width), BF16),
            jax.ShapeDtypeStruct((1, width), F32),
            jax.ShapeDtypeStruct((1, width), F32),
        ],
        compiler_params=params(),
        cost_estimate=pl.CostEstimate(flops=0, bytes_accessed=8_000_000, transcendentals=0),
        name="qkv_back",
    )(dq, dkv, q_pre, k_pre, cosine, sine, q_gain, k_gain)


def text_kernel(x, w, gain, k_pre, kv_out):
    made = jnp.dot(x[...], w[...], preferred_element_type=F32)
    k_pre[...] = made[:, :LANES]
    kv_out[:, :LANES] = pair_norm(made[:, :LANES], gain[...]).astype(BF16)
    kv_out[:, LANES:] = made[:, LANES:].astype(BF16)


def text_call(words, weights, gain):
    rows, depth = words.shape
    width = weights.shape[1] // 2
    return pl.pallas_call(
        text_kernel,
        grid=(width // LANES,),
        in_specs=[whole((rows, depth)), columns(depth, 2 * LANES), whole((1, LANES))],
        out_specs=[columns(rows, LANES), columns(rows, 2 * LANES)],
        out_shape=[
            jax.ShapeDtypeStruct((rows, width), F32),
            jax.ShapeDtypeStruct((rows, 2 * width), BF16),
        ],
        compiler_params=params(),
        cost_estimate=pl.CostEstimate(
            flops=4 * rows * depth * width, bytes_accessed=4_000_000, transcendentals=0
        ),
        name="text_kv",
    )(words, weights, gain)


def text_back_kernel(dkv, k_pre, gain, out, d_gain):
    key, d_gain[...] = pair_norm_back(k_pre[...], gain[...], dkv[:, :LANES])
    out[:, :LANES] = key.astype(BF16)
    out[:, LANES:] = dkv[:, LANES:].astype(BF16)


def text_back_call(dkv, k_pre, gain):
    rows, width = k_pre.shape
    return pl.pallas_call(
        text_back_kernel,
        grid=(width // LANES,),
        in_specs=[columns(rows, 2 * LANES), columns(rows, LANES), whole((1, LANES))],
        out_specs=[columns(rows, 2 * LANES), columns(1, LANES)],
        out_shape=[
            jax.ShapeDtypeStruct((rows, 2 * width), BF16),
            jax.ShapeDtypeStruct((1, width), F32),
        ],
        compiler_params=params(),
        cost_estimate=pl.CostEstimate(flops=0, bytes_accessed=2_000_000, transcendentals=0),
        name="text_kv_back",
    )(dkv, k_pre, gain)


class Meta:
    def __init__(self, ref, runs, blocks, wide, text_rows):
        self.ref, self.runs, self.blocks = (ref, runs, blocks)
        self.wide, self.text_rows = (wide, text_rows)

    def group(self, block):
        return self.ref[self.runs + block]

    def own(self):
        return self.ref[self.runs + self.blocks]

    def self_flag(self, block):
        return self.ref[self.runs + self.blocks + 1 + block]

    def cross_flag(self, block):
        return self.ref[self.runs + 2 * self.blocks + 1 + block]

    def run_items(self, group, count, axis):
        shape = (count, 1) if axis == 0 else (1, count)
        spot = lax.broadcasted_iota(jnp.int32, shape, axis) + group * count
        item = jnp.zeros(shape, jnp.int32)
        for run in range(self.runs):
            item = item + (spot >= self.ref[run]).astype(jnp.int32)
        return item

    def all_items(self, group, count, axis):
        shape = (count, 1) if axis == 0 else (1, count)
        row = lax.broadcasted_iota(jnp.int32, shape, axis)
        spot = row - self.wide + group * (count - self.wide)
        item = jnp.zeros(shape, jnp.int32)
        for run in range(self.runs):
            item = item + (spot >= self.ref[run]).astype(jnp.int32)
        return jnp.where(row < self.wide, self.runs, item)

    def text_items(self, group, axis):
        shape = (self.text_rows, 1) if axis == 0 else (1, self.text_rows)
        return (lax.broadcasted_iota(jnp.int32, shape, axis) + group * self.text_rows) // TTOK


def nt_dot(left, right):
    return lax.dot_general(left, right, (((1,), (1,)), ((), ())), preferred_element_type=F32)


def nn_dot(left, right):
    return jnp.dot(left, right, preferred_element_type=F32)


def tn_dot(left, right):
    return lax.dot_general(left, right, (((0,), (0,)), ((), ())), preferred_element_type=F32)


SCALING = 64 ** (-0.5) * SCORE_BASE
GRAD_SCALING = 64 ** (-0.5) * SCORE_BASE * TWO_NATURAL


def attend(query, key, value, allowed):
    sums, totals = (None, [])
    for query_head, value_head in zip(halves(query), halves(value)):
        weights = jnp.exp2(nt_dot(query_head, key) * SCALING)
        if allowed is not None:
            weights = jnp.where(allowed, weights, 0.0)
        totals.append(jnp.sum(weights, axis=-1, keepdims=True))
        fresh = nn_dot(weights.astype(BF16), value_head)
        sums = fresh if sums is None else sums + fresh
    return (sums, pair_select(*totals))


def attention_kernel(
    runs, highs, wide, text_rows, ref, q, kv0, kv1, kv2, kv3, t0, t1, t2, t3, gate,
    combined, self_out, cross_out, self_total, cross_total,
):
    meta = Meta(ref, runs, 4 * highs, wide, text_rows)
    rows = q.shape[0]
    run_rows = rows - wide
    self_out[...] = jnp.zeros(self_out.shape, F32)
    self_total[...] = jnp.zeros(self_total.shape, F32)
    cross_out[...] = jnp.zeros(cross_out.shape, F32)
    cross_total[...] = jnp.zeros(cross_total.shape, F32)
    own = meta.own()
    run_items = meta.run_items(own, run_rows, 0)
    all_items = meta.all_items(own, rows, 0)
    for number, (kv, text) in enumerate(((kv0, t0), (kv1, t1), (kv2, t2), (kv3, t3))):
        keys = kv[:, :wide, :LANES].reshape(highs * wide, LANES)
        values = kv[:, :wide, LANES:].reshape(highs * wide, LANES)
        sums, totals = attend(q[:wide, :], keys, values, None)
        self_out[:wide, :] += sums
        self_total[:wide, :] += totals

        @pl.loop(0, highs)
        def _(high, number=number, kv=kv, text=text):
            block = number * highs + high

            @pl.when(meta.self_flag(block) > 0)
            def _():
                allowed = run_items == meta.run_items(meta.group(block), run_rows, 1)
                sums, totals = attend(
                    q[wide:, :], kv[high, wide:, :LANES], kv[high, wide:, LANES:], allowed
                )
                self_out[wide:, :] += sums
                self_total[wide:, :] += totals

            @pl.when(meta.cross_flag(block) > 0)
            def _():
                allowed = all_items == meta.text_items(meta.group(block), 1)
                sums, totals = attend(
                    q[...], text[high, :, :LANES], text[high, :, LANES:], allowed
                )
                cross_out[...] += sums
                cross_total[...] += totals

    ours = self_out[...] / self_total[...]
    across = cross_out[...] / cross_total[...]
    self_out[...] = ours
    cross_out[...] = across
    combined[...] = (ours + gate[...] * across).astype(BF16)


def attention_call(meta, queries, kvs, texts, gate, runs):
    rows, width = queries.shape
    highs, text_rows = (kvs[0].shape[0], texts[0].shape[1])
    wide = rows // 4
    kv_spec = pl.BlockSpec((highs, rows, 2 * LANES), lambda p, *_: (0, 0, p))
    text_spec = pl.BlockSpec((highs, text_rows, 2 * LANES), lambda p, *_: (0, 0, p))
    float_out = jax.ShapeDtypeStruct((rows, width), F32)
    return pl.pallas_call(
        functools.partial(attention_kernel, runs, highs, wide, text_rows),
        grid_spec=pltpu.PrefetchScalarGridSpec(
            num_scalar_prefetch=1,
            grid=(width // LANES,),
            in_specs=[columns(rows, LANES)]
            + [kv_spec] * 4
            + [text_spec] * 4
            + [columns(1, LANES)],
            out_specs=[columns(rows, LANES)] * 5,
        ),
        out_shape=[jax.ShapeDtypeStruct((rows, width), BF16)] + [float_out] * 4,
        compiler_params=params(56),
        cost_estimate=pl.CostEstimate(
            flops=20_000_000_000, bytes_accessed=20_000_000, transcendentals=0
        ),
        name="attention",
    )(meta, queries, *kvs, *texts, gate)


def attend_back(query, grad, less, key, value, allowed):
    d_key, d_value, d_query = (None, None, None)
    for query_head, grad_head, less_head, key_head in zip(
        halves(query), halves(grad), less, halves(key)
    ):
        weights = jnp.exp2(nt_dot(key, query_head) * SCALING)
        if allowed is not None:
            weights = jnp.where(allowed, weights, 0.0)
        raw = weights * (nt_dot(value, grad_head) + less_head) * GRAD_SCALING
        raw = raw.astype(BF16)
        terms = (
            nn_dot(raw, query_head),
            nn_dot(weights.astype(BF16), grad_head),
            tn_dot(raw, key_head),
        )
        if d_key is None:
            d_key, d_value, d_query = terms
        else:
            d_key, d_value, d_query = (
                d_key + terms[0],
                d_value + terms[1],
                d_query + terms[2],
            )
    return (d_key.astype(BF16), d_value.astype(BF16), d_query)


def attention_back_kernel(
    runs, highs, wide, text_rows, ref, q, g, self_out, cross_out, self_total, cross_total, gate,
    kv0, kv1, kv2, kv3, t0, t1, t2, t3,
    dq, d_same, d_other, dt_same, dt_other, d_gate, self_grad, cross_grad,
):
    meta = Meta(ref, runs, 4 * highs, wide, text_rows)
    rows = q.shape[0]
    run_rows = rows - wide
    own = meta.own()
    run_items = meta.run_items(own, run_rows, 1)
    all_items = meta.all_items(own, rows, 1)
    incoming = g[...]
    d_gate[...] = jnp.sum(incoming * cross_out[...], axis=0, keepdims=True)
    scaled = incoming / self_total[...]
    self_grad[...] = scaled.astype(BF16)
    turned = jnp.transpose(scaled * self_out[...])
    self_less = (
        -jnp.sum(turned[: LANES // 2], axis=0, keepdims=True),
        -jnp.sum(turned[LANES // 2 :], axis=0, keepdims=True),
    )
    scaled = incoming * gate[...] / cross_total[...]
    cross_grad[...] = scaled.astype(BF16)
    turned = jnp.transpose(scaled * cross_out[...])
    cross_less = (
        -jnp.sum(turned[: LANES // 2], axis=0, keepdims=True),
        -jnp.sum(turned[LANES // 2 :], axis=0, keepdims=True),
    )
    wide_less = tuple(row[:, :wide] for row in self_less)
    run_less = tuple(row[:, wide:] for row in self_less)
    dq[...] = jnp.zeros(dq.shape, F32)
    arrays = (
        (kv0, t0, d_same.at[0], dt_same.at[0]),
        (kv1, t1, d_same.at[1], dt_same.at[1]),
        (kv2, t2, d_other.at[0], dt_other.at[0]),
        (kv3, t3, d_other.at[1], dt_other.at[1]),
    )
    for number, (kv, text, dkv, dtext) in enumerate(arrays):
        keys = kv[:, :wide, :LANES].reshape(highs * wide, LANES)
        values = kv[:, :wide, LANES:].reshape(highs * wide, LANES)
        d_key, d_value, d_query = attend_back(
            q[:wide, :], self_grad[:wide, :], wide_less, keys, values, None
        )
        dkv[:, :wide, :LANES] = d_key.reshape(highs, wide, LANES)
        dkv[:, :wide, LANES:] = d_value.reshape(highs, wide, LANES)
        dq[:wide, :] += d_query

        @pl.loop(0, highs)
        def _(high, number=number, kv=kv, text=text, dkv=dkv, dtext=dtext):
            block = number * highs + high

            @pl.when(meta.self_flag(block) > 0)
            def _():
                allowed = meta.run_items(meta.group(block), run_rows, 0) == run_items
                d_key, d_value, d_query = attend_back(
                    q[wide:, :],
                    self_grad[wide:, :],
                    run_less,
                    kv[high, wide:, :LANES],
                    kv[high, wide:, LANES:],
                    allowed,
                )
                dkv[high, wide:, :LANES] = d_key
                dkv[high, wide:, LANES:] = d_value
                dq[wide:, :] += d_query

            @pl.when(meta.self_flag(block) == 0)
            def _():
                dkv[high, wide:, :] = jnp.zeros((run_rows, 2 * LANES), BF16)

            @pl.when(meta.cross_flag(block) > 0)
            def _():
                allowed = meta.text_items(meta.group(block), 0) == all_items
                d_key, d_value, d_query = attend_back(
                    q[...],
                    cross_grad[...],
                    cross_less,
                    text[high, :, :LANES],
                    text[high, :, LANES:],
                    allowed,
                )
                dtext[high, :, :LANES] = d_key
                dtext[high, :, LANES:] = d_value
                dq[...] += d_query

            @pl.when(meta.cross_flag(block) == 0)
            def _():
                dtext[high] = jnp.zeros((text_rows, 2 * LANES), BF16)


def attention_back_call(meta, queries, incoming, outputs, gate, kvs, texts, runs):
    rows, width = queries.shape
    highs, text_rows = (kvs[0].shape[0], texts[0].shape[1])
    wide = rows // 4
    kv_spec = pl.BlockSpec((highs, rows, 2 * LANES), lambda p, *_: (0, 0, p))
    text_spec = pl.BlockSpec((highs, text_rows, 2 * LANES), lambda p, *_: (0, 0, p))
    d_kv = jax.ShapeDtypeStruct((2, *kvs[0].shape), BF16)
    d_text = jax.ShapeDtypeStruct((2, *texts[0].shape), BF16)
    return pl.pallas_call(
        functools.partial(attention_back_kernel, runs, highs, wide, text_rows),
        grid_spec=pltpu.PrefetchScalarGridSpec(
            num_scalar_prefetch=1,
            grid=(width // LANES,),
            in_specs=[columns(rows, LANES)] * 6
            + [columns(1, LANES)]
            + [kv_spec] * 4
            + [text_spec] * 4,
            out_specs=[columns(rows, LANES)]
            + [pl.BlockSpec((2, highs, rows, 2 * LANES), lambda p, *_: (0, 0, 0, p))] * 2
            + [pl.BlockSpec((2, highs, text_rows, 2 * LANES), lambda p, *_: (0, 0, 0, p))] * 2
            + [columns(1, LANES)],
            scratch_shapes=[pltpu.VMEM((rows, LANES), BF16)] * 2,
        ),
        out_shape=[jax.ShapeDtypeStruct((rows, width), F32), d_kv, d_kv, d_text, d_text]
        + [jax.ShapeDtypeStruct((1, width), F32)],
        compiler_params=params(60),
        cost_estimate=pl.CostEstimate(
            flops=30_000_000_000, bytes_accessed=30_000_000, transcendentals=0
        ),
        name="attention_back",
    )(meta, queries, incoming, *outputs, gate, *kvs, *texts)


def separate(array, kinds):
    pairs = array.shape[-1] // LANES // kinds
    return [
        jnp.concatenate(
            [
                array[..., (p * kinds + kind) * LANES : (p * kinds + kind + 1) * LANES]
                for p in range(pairs)
            ],
            axis=-1,
        )
        for kind in range(kinds)
    ]


def on_device(
    patches,
    cotangent,
    item_lengths,
    timesteps,
    patch_rows,
    patch_cols,
    conditioning,
    text_states,
    gain_attn,
    gain_ffn,
    query_gain,
    key_gain,
    text_key_gain,
    cross_gate,
    w_query,
    w_key,
    w_value,
    w_out,
    w_text_key,
    w_text_value,
    w_gate,
    w_up,
    w_down,
    w_ada,
    w_text,
):
    at = Place()
    tok_dev, model_width = patches.shape
    shard_rows = w_query.shape[0]
    head_dim = query_gain.shape[0]
    local_width = w_query.shape[1]
    heads_local = local_width // head_dim
    text_rows = text_states.shape[0]
    item_count = conditioning.shape[0]
    quarter = tok_dev // 4
    hidden_width = w_gate.shape[1]

    shards = [w_query, w_key, w_value]
    shared_qkv = share(shards, by_pairs(shards), at)
    qkv_rows = GatherRows(shared_qkv, 0, [3 * local_width], at)
    qkv_rows.z()
    first = [shared_qkv[2]]
    text_width = w_text.shape[1]
    shards = [w_text, w_text_key, w_text_value, w_out, w_down, w_gate, w_up]
    order = side_by_side(shards)
    order[1:3] = [
        (1 + source, start, width)
        for source, start, width in by_pairs([w_text_key, w_text_value])
    ]
    shared = share(shards, order, at, [qkv_rows.stacked])
    places = [0]
    for width in (text_width + 2 * local_width, local_width, hidden_width):
        places.append(places[-1] + width)
    qkv_rows.y()
    text_rows_all = GatherRows(shared, places[0], [text_width, 2 * local_width], at)
    out_rows = GatherRows(shared, places[1], [local_width], at)
    down_rows = GatherRows(shared, places[2], [hidden_width], at)
    gu_rows = GatherRows(shared, places[3], [2 * hidden_width], at)
    embed_pre = conditioning.astype(F32) + time_embed(timesteps, model_width)
    embed = jax.nn.silu(embed_pre).astype(BF16)
    own_embed = lax.dynamic_slice_in_dim(embed, at.data * shard_rows, shard_rows, 1)
    gains = lax.dynamic_update_slice(
        jnp.zeros((2, model_width), F32),
        jnp.stack([gain_attn, gain_ffn]).astype(F32),
        (0, at.data * shard_rows),
    )
    head_sums = butterfly(
        after(jnp.concatenate([multiply(own_embed, w_ada), gains], axis=0), *first),
        at,
        model=False,
        z_wait=[qkv_rows.near],
    )
    my_patches = swap_rows(after(patches, *first), at)
    text_rows_all.z()
    (full_qkv,) = qkv_rows.core()
    positions = swap_roles(
        after(jnp.stack([patch_rows, patch_cols]).astype(F32), head_sums)
    )
    gain_attn32, gain_ffn32 = (head_sums[item_count], head_sums[item_count + 1])
    mod_part = head_sums[:item_count]
    mod_pair = jnp.stack(
        unmix([mod_part, lax.ppermute(mod_part, "mp", [(i, i ^ 1) for i in range(4)])], at.c)
    )
    mod_all = jnp.stack(
        unmix([mod_pair, lax.ppermute(mod_pair, "mp", [(i, i ^ 2) for i in range(4)])], at.x)
    )
    shift1_t, gate1_t, shift2_t, gate2_t = mod_all.reshape(4, item_count, model_width)

    token_items = item_ids(item_lengths, tok_dev, at.n_dp).reshape(at.n_dp, tok_dev)
    own_items = pick(token_items, at.tokens)
    item_labels = jnp.arange(item_count, dtype=jnp.int32)
    onehot = (own_items[:, None] == item_labels[None, :]).astype(F32)
    runs = item_lengths.shape[0]
    groups = jnp.stack(relative_groups(at)).astype(jnp.int32)
    firsts, lasts = (token_items[:, tok_dev // 4], token_items[:, tok_dev - 1])
    my_first, my_last = (pick(firsts, at.tokens), pick(lasts, at.tokens))
    self_flags = (firsts[groups] <= my_last) & (lasts[groups] >= my_first)
    text_first = groups * text_rows // TTOK
    text_last = (groups * text_rows + text_rows - 1) // TTOK
    cross_flags = ((text_first <= my_last) & (text_last >= my_first)) | (text_last >= runs)
    meta = jnp.concatenate(
        [
            jnp.cumsum(item_lengths),
            groups,
            at.tokens[None],
            self_flags.astype(jnp.int32),
            cross_flags.astype(jnp.int32),
        ]
    ).astype(jnp.int32)
    few_items = lax.dynamic_slice_in_dim(own_items, at.features * quarter, quarter)
    few_onehot = lax.dynamic_slice_in_dim(onehot, at.features * quarter, quarter)

    shift1 = rows_of(shift1_t, own_items)
    inputs = my_patches.astype(F32)
    normed1, _ = norm_fwd(inputs, gain_attn32)
    hidden1 = (normed1 * (1.0 + shift1)).astype(BF16)

    angles = rope_angles(positions[0], positions[1], head_dim)
    both_heads = (1, LANES // head_dim)
    cosine, sine = (jnp.cos(angles), jnp.sin(angles))
    split = head_dim // 4
    cosine = jnp.tile(
        jnp.concatenate([cosine[:, :split]] * 2 + [cosine[:, split:]] * 2, axis=1), both_heads
    )
    sine = jnp.tile(
        jnp.concatenate(
            [-sine[:, :split], sine[:, :split], -sine[:, split:], sine[:, split:]], axis=1
        ),
        both_heads,
    )
    query_gain32, key_gain32, text_gain32 = (
        jnp.tile(gain.astype(F32)[None], both_heads)
        for gain in (query_gain, key_gain, text_key_gain)
    )
    query_pre, key_pre, queries, own_kv = qkv_call(
        hidden1, full_qkv, cosine, sine, query_gain32, key_gain32
    )
    kv_tokens = GatherTokens(own_kv, at)
    kv_tokens.z()
    text_rows_all.y()
    kv_tokens.y()
    my_text = swap_roles(after(text_states, head_sums))
    full_text, full_tkv = text_rows_all.core(kv_tokens.near)
    out_rows.z()
    words = sum_features(multiply_trans(my_text, full_text).astype(BF16), at)
    out_rows.y()
    text_pre, own_text_kv = text_call(words, full_tkv, text_gain32)
    text_tokens = GatherTokens(own_text_kv, at)
    text_tokens.z()
    text_tokens.y()
    my_cotangent = swap_rows(cotangent, at)
    gu_rows.z()
    gu_rows.y()
    (full_out,) = out_rows.core()
    gate_local = jnp.tanh(
        lax.dynamic_slice_in_dim(cross_gate.astype(F32), at.features * heads_local, heads_local)
    )
    gate_wide = jnp.repeat(gate_local, head_dim)[None]
    all_kv, all_text_kv = (kv_tokens.core(), text_tokens.core())
    combined, *outputs = attention_call(meta, queries, all_kv, all_text_kv, gate_wide, runs)
    few_inputs = lax.dynamic_slice_in_dim(inputs, at.features * quarter, quarter)
    few_normed1 = lax.dynamic_slice_in_dim(normed1, at.features * quarter, quarter)
    tanh_one = jnp.tanh(rows_of(gate1_t, few_items))
    tanh_two = jnp.tanh(rows_of(gate2_t, few_items))
    shift2 = rows_of(shift2_t, few_items)
    few_shift1 = rows_of(shift1_t, few_items)
    combined_out = after(combined, gu_rows.near)
    branch = sum_quarters(multiply_trans(combined_out, full_out).astype(BF16), at)
    down_rows.z()
    down_rows.y()
    middle = few_inputs + tanh_one * branch
    normed2, scale2 = norm_fwd(middle, gain_ffn32)
    hidden2 = gather_quarters((normed2 * (1.0 + shift2)).astype(BF16), at)
    (full_gu,) = gu_rows.core(combined)
    (full_down,) = down_rows.core(combined)
    gate_up = multiply(hidden2, full_gu)
    gate_pre, up_pre = (gate_up[:, :hidden_width], gate_up[:, hidden_width:])
    logistic = jax.nn.sigmoid(gate_pre)
    silu_gate = gate_pre * logistic
    inner_act = (silu_gate * up_pre).astype(BF16)

    grad_output = my_cotangent.astype(F32)
    few_output = lax.dynamic_slice_in_dim(grad_output, at.features * quarter, quarter)
    grad_ffn = (grad_output * rows_of(jnp.tanh(gate2_t), own_items)).astype(BF16)
    grad_inner = multiply(grad_ffn, full_down)
    grad_gate = (grad_inner * up_pre * logistic * (1.0 + gate_pre * (1.0 - logistic))).astype(BF16)
    grad_up = (grad_inner * silu_gate).astype(BF16)
    grad_gu = jnp.concatenate([grad_gate, grad_up], axis=1)
    hidden2_part = multiply_trans(grad_gu, full_gu).astype(BF16)
    grad_hidden2 = sum_quarters(hidden2_part, at)
    ffn_sums = ScatterRows(
        [
            trans_multiply(after(grad_ffn, hidden2_part), inner_act),
            trans_multiply(after(hidden2, hidden2_part), grad_gu),
        ],
        at,
    )
    ffn_sums.y()
    grad_middle_norm, gain_ffn_term = norm_back(
        middle, scale2, gain_ffn32, grad_hidden2 * (1.0 + shift2)
    )
    grad_middle = few_output + grad_middle_norm
    grad_branch = gather_quarters((grad_middle * tanh_one).astype(BF16), at)
    grad_combined = multiply(grad_branch, full_out)
    ffn_part = multiply_trans(after(inner_act, grad_combined), full_down).astype(BF16)
    ffn_out = sum_quarters(ffn_part, at)
    out_sums = ScatterRows([trans_multiply(grad_branch, combined)], at)
    out_sums.y()
    grad_queries, d_same, d_other, dt_same, dt_other, gate_terms = attention_back_call(
        meta, queries, grad_combined, outputs, gate_wide, all_kv, all_text_kv, runs
    )
    out_sums.z()
    text_sums = ScatterTokens(dt_same, dt_other, at)
    kv_sums = ScatterTokens(d_same, d_other, at)
    text_sums.y()
    kv_sums.y()
    text_back = text_sums.z()
    ffn_sums.z()
    grad_gate_local = jnp.sum(gate_terms.reshape(heads_local, head_dim), axis=1) * (
        1.0 - gate_local * gate_local
    )
    grad_tkv, text_gain_term = text_back_call(text_back, text_pre, text_gain32)
    grad_words = sum_features(multiply_trans(grad_tkv, full_tkv).astype(BF16), at)
    kv_back = kv_sums.z()
    mixed_out = gather_output((middle + tanh_two * ffn_out).astype(BF16), at)
    words_sums = ScatterRows(
        [trans_multiply(grad_words, my_text), trans_multiply(words, grad_tkv)], at
    )
    words_sums.y()
    grad_qkv, query_gain_term, key_gain_term = qkv_back_call(
        grad_queries, kv_back, query_pre, key_pre, cosine, sine, query_gain32, key_gain32
    )
    hidden1_part = multiply_trans(grad_qkv, full_qkv).astype(BF16)
    grad_hidden1 = sum_quarters(hidden1_part, at)
    qkv_sums = ScatterRows([trans_multiply(after(hidden1, hidden1_part), grad_qkv)], at)
    few_scale1 = lax.rsqrt(jnp.mean(few_inputs * few_inputs, axis=-1, keepdims=True) + EPSILON)
    grad_inputs_norm, gain_attn_term = norm_back(
        few_inputs, few_scale1, gain_attn32, grad_hidden1 * (1.0 + few_shift1)
    )
    grad_patches = gather_output((grad_middle + grad_inputs_norm).astype(BF16), at).astype(F32)
    qkv_sums.y()
    words_sums.z()
    qkv_sums.z()
    grads_out, grads_ffn = (out_sums.result(), ffn_sums.result())
    grads_texts, grads_qkv = (words_sums.result(), qkv_sums.result())
    grad_text = swap_roles(multiply(grad_words, full_text).astype(BF16)).astype(F32)
    def item_sums(rows):
        return trans_multiply(few_onehot, rows, HIGHEST)

    gate_full = lax.dynamic_update_slice_in_dim(
        jnp.zeros((cross_gate.shape[0],), F32),
        grad_gate_local,
        at.features * heads_local,
        0,
    )
    small = jnp.concatenate(
        [
            jnp.sum(query_gain_term.reshape(heads_local, head_dim), axis=0),
            jnp.sum(key_gain_term.reshape(heads_local, head_dim), axis=0),
            jnp.sum(text_gain_term.reshape(heads_local, head_dim), axis=0),
            gate_full,
        ]
    )
    small = jnp.pad(small, (0, model_width - small.shape[0]))
    late = butterfly(
        after(jnp.concatenate(
            [
                item_sums(
                    jnp.concatenate(
                        [
                            grad_hidden1 * few_normed1,
                            grad_middle * branch * (1.0 - tanh_one * tanh_one),
                            grad_hidden2 * normed2,
                            few_output * ffn_out * (1.0 - tanh_two * tanh_two),
                        ],
                        axis=1,
                    )
                )
                .reshape(item_count, 4, model_width)
                .swapaxes(0, 1)
                .reshape(4 * item_count, model_width),
                jnp.sum(gain_attn_term, axis=0, keepdims=True),
                jnp.sum(gain_ffn_term, axis=0, keepdims=True),
                small[None],
            ],
            axis=0,
        ), words_sums.to_z),
        at,
    )
    grad_mod_own = pick(late[: 4 * item_count].reshape(4, item_count, model_width), at.model)
    late = late[4 * item_count :]
    small = late[2]
    grad_ada = trans_multiply(own_embed.astype(F32), grad_mod_own, HIGHEST)
    grad_embed_part = multiply_trans(grad_mod_own, w_ada.astype(F32), HIGHEST)
    grad_embed = butterfly(
        lax.dynamic_update_slice(
            jnp.zeros((item_count, model_width), F32),
            grad_embed_part,
            (0, at.data * shard_rows),
        ),
        at,
    )
    embed_logistic = jax.nn.sigmoid(embed_pre)
    grad_conditioning = grad_embed * embed_logistic * (1.0 + embed_pre * (1.0 - embed_logistic))
    own_gain = lambda row: lax.dynamic_slice_in_dim(row, at.data * shard_rows, shard_rows)
    grad_wq, grad_wk, grad_wv = separate(grads_qkv, 3)
    grad_wtk, grad_wtv = separate(grads_texts[:, text_width:], 2)
    return (
        mixed_out,
        grad_patches,
        grad_conditioning,
        grad_text,
        own_gain(late[0]),
        own_gain(late[1]),
        small[:head_dim],
        small[head_dim : 2 * head_dim],
        small[2 * head_dim : 3 * head_dim],
        small[3 * head_dim : 3 * head_dim + cross_gate.shape[0]],
        grad_wq,
        grad_wk,
        grad_wv,
        grads_out,
        grad_wtk,
        grad_wtv,
        grads_ffn[:, hidden_width : 2 * hidden_width],
        grads_ffn[:, 2 * hidden_width :],
        grads_ffn[:, :hidden_width],
        grad_ada,
        grads_texts[:, :text_width],
    )


def solution(mesh):
    rows, both, one = (P("dp", None), P("dp", "mp"), P("dp"))
    whole = P()
    in_specs = (
        (rows, rows, whole, whole, one, one, whole, both, one, one)
        + (whole,) * 4
        + (both,) * 11
    )
    out_specs = (
        (rows, rows, whole, both, one, one) + (whole,) * 4 + (both,) * 11
    )
    return jax.shard_map(
        on_device, mesh=mesh, in_specs=in_specs, out_specs=out_specs, check_vma=False
    )
```

```python
import functools
import math

import jax
import jax.numpy as jnp
from jax import lax
from jax.experimental import pallas as pl
from jax.experimental.pallas import tpu as pltpu
from jax.sharding import PartitionSpec as P

TTOK = 256
HIGHEST = lax.Precision.HIGHEST
EPSILON = 1e-06
SCORE_BASE = 1.4426950408889634
TWO_NATURAL = 0.6931471805599453
AXES = ("dp", "mp")
DEPTH = 2
LANES = 128
F32 = jnp.float32
BF16 = jnp.bfloat16


def contract(left, right, pairing, precision=None):
    return lax.dot_general(
        left, right, (pairing, ((), ())), precision=precision, preferred_element_type=F32
    )


def multiply(left, right):
    return contract(left, right, ((1,), (0,)))


def multiply_trans(left, right, precision=None):
    return contract(left, right, ((1,), (1,)), precision)


def trans_multiply(left, right, precision=None):
    return contract(left, right, ((0,), (0,)), precision)


def time_embed(steps, model_width):
    halfway = model_width // 2
    frequency = jnp.exp(-math.log(10000.0) * jnp.arange(halfway, dtype=F32) / halfway)
    phases = steps.astype(F32)[:, None] * frequency[None, :]
    return jnp.concatenate([jnp.cos(phases), jnp.sin(phases)], axis=1)


def rope_angles(rows_pos, cols_pos, head_dim):
    quarter = head_dim // 4
    frequency = jnp.exp(-math.log(10000.0) * jnp.arange(quarter, dtype=F32) / quarter)
    return jnp.concatenate(
        [
            rows_pos.astype(F32)[:, None] * frequency[None, :],
            cols_pos.astype(F32)[:, None] * frequency[None, :],
        ],
        axis=1,
    )


def item_ids(lengths, tok_dev, n_dev):
    wide_dev = tok_dev // 4
    boundary = jnp.cumsum(lengths)
    position = jnp.arange(tok_dev * n_dev, dtype=jnp.int32)
    within = position % tok_dev
    placed = position // tok_dev * (tok_dev - wide_dev) + within - wide_dev
    counted = jnp.sum((boundary[None, :] <= placed[:, None]).astype(jnp.int32), axis=1)
    return jnp.where(within < wide_dev, lengths.shape[0], counted)


def norm_fwd(values, gain_vec):
    scaling = lax.rsqrt(jnp.mean(values * values, axis=-1, keepdims=True) + EPSILON)
    return (values * scaling * gain_vec, scaling)


def norm_back(values, scaling, gain_vec, incoming):
    weighted = incoming * gain_vec
    inner_mean = jnp.mean(weighted * values, axis=-1, keepdims=True)
    return (
        scaling * weighted - values * scaling * scaling * scaling * inner_mean,
        incoming * values * scaling,
    )


def codes(index):
    data, model = divmod(index, 4)
    return (data // 4, data // 2 % 2, data % 2, model // 2, model % 2)


def place(dh, zl, dy, x, c):
    return ((dh * 2 + zl) * 2 + dy) * 4 + x * 2 + c


def move(values, where, only=None):
    count = lax.axis_size("dp") * lax.axis_size("mp")
    pairs = [
        (i, place(*where(*codes(i)))) for i in range(count) if only is None or only(*codes(i))
    ]
    return lax.ppermute(values, AXES, pairs)


def swap_roles(values):
    return move(values, lambda dh, zl, dy, x, c: (dh, c, dy, x, zl))


def swap_rows(values, at):
    rows, width = values.shape
    away = lambda dh, zl, dy, x, c: zl != c
    over_z = lambda piece: move(piece, lambda dh, zl, dy, x, c: (dh, zl ^ 1, dy, x, c ^ 1), away)
    got = at.along_z.send(over_z, pick(values.reshape(2, rows // 2, width), at.x))
    other = move(got, lambda dh, zl, dy, x, c: (dh, zl, dy, x ^ 1, c), away)
    swapped = jnp.concatenate(unmix([got, other], at.x), axis=0)
    return jnp.where(at.c == at.zl, values, swapped)


def other_core(values):
    return move(values, lambda dh, zl, dy, x, c: (dh, zl, dy, x, c ^ 1))


def other_y(values):
    return move(values, lambda dh, zl, dy, x, c: (dh, zl, dy ^ 1, x, c))


def other_high(values, high):
    return move(values, lambda dh, zl, dy, x, c: (dh ^ high, zl, dy, x, c))


def other_feature(values, other):
    return move(values, lambda dh, zl, dy, x, c: (dh, zl ^ (other & 1), dy, x ^ (other >> 1), c))


def pick(values, index, axis=0):
    return lax.dynamic_index_in_dim(values, index, axis, keepdims=False)


def after(values, *events):
    if not events:
        return values
    return lax.optimization_barrier((values, *events))[0]


class Link:
    def __init__(self, depth):
        self.depth = depth
        self.ended = []

    def send(self, how, values, *rest):
        if len(self.ended) >= self.depth:
            values = after(values, self.ended[-self.depth])
        result = how(values, *rest)
        self.ended.append(result)
        return result


class Place:
    def __init__(self):
        self.along_z, self.along_y = (Link(DEPTH), Link(1))
        data, model = (lax.axis_index("dp"), lax.axis_index("mp"))
        self.data, self.model = (data, model)
        self.n_dp = lax.axis_size("dp")
        self.highs = self.n_dp // 4
        self.dh, self.zl, self.dy = (data // 4, data // 2 % 2, data % 2)
        self.x, self.c = (model // 2, model % 2)
        self.tokens = (self.dh * 2 + self.c) * 2 + self.dy
        self.features = self.x * 2 + self.zl


def unmix(parts, index):
    count = len(parts)
    ordered = []
    for spot in range(count):
        value = parts[spot]
        for other in range(1, count):
            value = jnp.where(index == other, parts[spot ^ other], value)
        ordered.append(value)
    return ordered


def pack_kernel(order, *refs):
    core = lax.axis_index("mp") % 2
    for out, side in zip(refs[-2:], (core, core ^ 1)):
        start = 0
        for source, first, width in order:
            out[:, start : start + width] = refs[source][side, :, first : first + width]
            start += width


def pack(shards, order):
    half = shards[0].shape[0] // 2
    width = sum(part[2] for part in order)
    result = jax.ShapeDtypeStruct((half, width), shards[0].dtype)
    return pl.pallas_call(
        functools.partial(pack_kernel, order),
        out_shape=[result, result],
        compiler_params=params(),
        cost_estimate=pl.CostEstimate(
            flops=0, bytes_accessed=8 * half * width, transcendentals=0
        ),
        name="pack",
    )(*[shard.reshape(2, half, shard.shape[1]) for shard in shards])


def by_pairs(shards):
    return [
        (source, first, LANES)
        for first in range(0, shards[0].shape[1], LANES)
        for source in range(len(shards))
    ]


def side_by_side(shards):
    return [(source, 0, shard.shape[1]) for source, shard in enumerate(shards)]


def pack_kernel(order, *refs):
    core = lax.axis_index("mp") % 2
    for out, side in zip(refs[-2:], (core, core ^ 1)):
        start = 0
        for source, first, width in order:
            out[:, start : start + width] = refs[source][side, :, first : first + width]
            start += width


def pack(shards, order):
    half = shards[0].shape[0] // 2
    width = sum(part[2] for part in order)
    result = jax.ShapeDtypeStruct((half, width), shards[0].dtype)
    return pl.pallas_call(
        functools.partial(pack_kernel, order),
        out_shape=[result, result],
        compiler_params=params(),
        cost_estimate=pl.CostEstimate(
            flops=0, bytes_accessed=8 * half * width, transcendentals=0
        ),
        name="pack",
    )(*[shard.reshape(2, half, shard.shape[1]) for shard in shards])


def by_pairs(shards):
    return [
        (source, first, LANES)
        for first in range(0, shards[0].shape[1], LANES)
        for source in range(len(shards))
    ]


def side_by_side(shards):
    return [(source, 0, shard.shape[1]) for source, shard in enumerate(shards)]


def assemble_kernel(highs, near, beside, near_core, beside_core, full):
    data, core = (lax.axis_index("dp"), lax.axis_index("mp") % 2)
    high, y = (data // 4, data % 2)
    for block, from_y, from_core in (
        (near, y, core),
        (beside, y ^ 1, core),
        (near_core, y, core ^ 1),
        (beside_core, y ^ 1, core ^ 1),
    ):
        for a in range(highs):
            for b in (0, 1):
                full[high ^ a, from_core ^ b, from_y, from_core] = block[a, b]


def assemble(near, beside, near_core, beside_core):
    highs, _, half, width = near.shape
    step = math.gcd(width, 512) if width % 384 else 384
    part = pl.BlockSpec((highs, 2, half, step), lambda i: (0, 0, 0, i))
    return pl.pallas_call(
        functools.partial(assemble_kernel, highs),
        grid=(width // step,),
        in_specs=[part] * 4,
        out_specs=pl.BlockSpec((highs, 2, 2, 2, half, step), lambda i: (0,) * 5 + (i,)),
        out_shape=jax.ShapeDtypeStruct((highs, 2, 2, 2, half, width), near.dtype),
        compiler_params=params(),
        cost_estimate=pl.CostEstimate(
            flops=0, bytes_accessed=32 * highs * half * width, transcendentals=0
        ),
        name="assemble",
    )(near, beside, near_core, beside_core)


class Events:
    def __init__(self, **events):
        self.__dict__.update(events)


def assemble_kernel(near, beside, near_core, beside_core, full):
    y, core = (lax.axis_index("dp") % 2, lax.axis_index("mp") % 2)
    for block, from_y, from_core in (
        (near, y, core),
        (beside, y ^ 1, core),
        (near_core, y, core ^ 1),
        (beside_core, y ^ 1, core ^ 1),
    ):
        for z in range(near.shape[0]):
            full[z, from_y, from_core] = block[z]


def assemble(blocks, first, width):
    count, half, _ = blocks[0].shape
    step = next(step for step in (512, 384, 256, LANES) if first % step == width % step == 0)
    part = pl.BlockSpec((count, half, step), lambda i: (0, 0, first // step + i))
    full = pl.pallas_call(
        assemble_kernel,
        grid=(width // step,),
        in_specs=[part] * 4,
        out_specs=pl.BlockSpec((count, 2, 2, half, step), lambda i: (0,) * 4 + (i,)),
        out_shape=jax.ShapeDtypeStruct((count, 2, 2, half, width), BF16),
        compiler_params=params(),
        cost_estimate=pl.CostEstimate(
            flops=0, bytes_accessed=16 * count * half * width, transcendentals=0
        ),
        name="assemble",
    )(*blocks)
    return full.reshape(4 * count * half, width)


def exchange_z(values):
    count = lax.axis_size("dp")
    return lax.all_to_all(
        values, "dp", 0, 0, axis_index_groups=[list(range(y, count, 2)) for y in (0, 1)], tiled=True
    )


def exchange_features(values):
    highs = lax.axis_size("dp") // 4
    groups = [
        [place(dh, zl, dy, x, c) for x in (0, 1) for zl in (0, 1)]
        for dh in range(highs)
        for dy in (0, 1)
        for c in (0, 1)
    ]
    return lax.all_to_all(values, AXES, 0, 0, axis_index_groups=groups, tiled=True)


def share(shards, order, at, c_wait=()):
    mine, theirs = pack([after(shard, *c_wait) for shard in shards], order)
    got = other_core(theirs)
    return (jnp.where(at.c == 0, mine, got), jnp.where(at.c == 0, got, mine), got)


class GatherRows:
    def __init__(self, shared, first, widths, at):
        self.at, self.widths = (at, widths)
        pieces = [piece[:, first : first + sum(widths)] for piece in shared[:2]]
        self.stacked = jnp.stack(pieces * at.highs)

    def z(self):
        self.near = self.at.along_z.send(exchange_z, self.stacked)

    def y(self):
        self.beside = self.at.along_y.send(other_y, self.near)

    def core(self, *events):
        near, beside = (after(self.near, *events), after(self.beside, *events))
        blocks = (near, beside, other_core(near), other_core(beside))
        fulls, start = ([], 0)
        for width in self.widths:
            fulls.append(assemble(blocks, start, width))
            start += width
        return fulls


class ScatterRows:
    def __init__(self, grads, at):
        self.at = at
        half = grads[0].shape[0] // at.n_dp // 2
        self.views = [grad.astype(BF16).reshape(at.n_dp // 2, 2, 2, half, -1) for grad in grads]
        self.from_core = other_core(
            jnp.concatenate([pick(view, 1 - at.c, 2) for view in self.views], axis=-1)
        )
        self.to_y = self.kept_rows(1 - at.dy).astype(BF16)

    def kept_rows(self, y):
        own = [pick(pick(view, y, 1), self.at.c, 1) for view in self.views]
        own = jnp.concatenate(own, axis=-1).astype(F32)
        return own + pick(self.from_core, y, 1).astype(F32)

    def y(self):
        from_y = self.at.along_y.send(other_y, self.to_y)
        self.to_z = (self.kept_rows(self.at.dy) + from_y.astype(F32)).astype(BF16)

    def z(self):
        self.from_z = self.at.along_z.send(exchange_z, self.to_z)

    def result(self):
        at = self.at
        sums = [
            sum(self.from_z[2 * a + zl].astype(F32) for a in range(at.highs)) for zl in (0, 1)
        ]
        mine, theirs = (jnp.where(at.c == 0, *sums), jnp.where(at.c == 0, *sums[::-1]))
        other = other_core(theirs.astype(BF16)).astype(F32)
        return jnp.concatenate(unmix([mine, other], at.c), axis=0)


class GatherTokens:
    def __init__(self, block, at):
        self.block, self.at = (block, at)

    def z(self):
        far = [
            self.at.along_z.send(other_high, self.block, a) for a in range(1, self.at.highs)
        ]
        self.near = jnp.stack([self.block] + far)

    def y(self):
        self.beside = self.at.along_y.send(other_y, self.near)

    def core(self, *events):
        near, beside = (after(self.near, *events), after(self.beside, *events))
        return [near, beside, other_core(near), other_core(beside)]


class ScatterTokens:
    def __init__(self, same, other, at):
        self.at = at
        self.total = same.astype(F32) + other_core(other).astype(F32)
        self.to_y = self.total[1].astype(BF16)

    def y(self):
        from_y = self.at.along_y.send(other_y, self.to_y)
        self.total = self.total[0] + from_y.astype(F32)

    def z(self):
        result = self.total[0]
        for a in range(1, self.at.highs):
            got = self.at.along_z.send(other_high, self.total[a].astype(BF16), a)
            result = result + got.astype(F32)
        return result


def relative_groups(at):
    return [
        ((at.dh ^ a) * 2 + (at.c ^ core)) * 2 + (at.dy ^ y)
        for core in (0, 1)
        for y in (0, 1)
        for a in range(at.highs)
    ]


def sum_quarters(part, at):
    rows, width = part.shape
    parts = at.along_z.send(exchange_features, part.reshape(4, rows // 4, width))
    return jnp.sum(parts.astype(F32), axis=0)


def gather_quarters(own, at):
    rows, width = own.shape
    parts = at.along_z.send(
        exchange_features, jnp.broadcast_to(own[None], (4, rows, width))
    )
    return parts.reshape(4 * rows, width)


def sum_features(part, at):
    for other, link in ((1, at.along_z), (2, None)):
        got = link.send(other_feature, part, other) if link else other_feature(part, other)
        part = (part.astype(F32) + got.astype(F32)).astype(BF16)
    return part


def gather_output(own, at):
    to_x = lambda part, a: move(part, lambda dh, zl, dy, x, c: (dh, c, dy, x ^ a, zl))
    near = [at.along_z.send(to_x, own, a) for a in (0, 1)]
    near = jnp.stack(unmix(near, at.x))
    far = other_core(near)
    first, second = (jnp.where(at.c == 0, near, far), jnp.where(at.c == 0, far, near))
    return jnp.stack([first, second], axis=1).reshape(4 * own.shape[0], own.shape[1])


def butterfly(values, at, data=True, model=True, z_wait=()):
    for bit in (1, 2) if model else ():
        values = values + lax.ppermute(values, "mp", [(i, i ^ bit) for i in range(4)])
    bit = 1
    while data and bit < at.n_dp:
        if bit == 2:
            values = after(values, *z_wait)
        values = values + lax.ppermute(values, "dp", [(i, i ^ bit) for i in range(at.n_dp)])
        bit *= 2
    return values


def rows_of(table, items):
    value = jnp.broadcast_to(table[0][None], (items.shape[0], table.shape[1]))
    for item in range(1, table.shape[0]):
        value = jnp.where(items[:, None] == item, table[item][None], value)
    return value


def halves(values):
    lane = lax.broadcasted_iota(jnp.int32, (1, LANES), 1)
    low = lane < LANES // 2
    zero = jnp.zeros((), values.dtype)
    return (jnp.where(low, values, zero), jnp.where(low, zero, values))


def pair_select(first, second):
    lane = lax.broadcasted_iota(jnp.int32, (1, LANES), 1)
    return jnp.where(lane < LANES // 2, first, second)


def pair_mean(values):
    low, high = halves(values)
    return pair_select(
        jnp.sum(low, axis=-1, keepdims=True), jnp.sum(high, axis=-1, keepdims=True)
    ) * (2.0 / LANES)


def partner(values):
    lane = lax.broadcasted_iota(jnp.int32, (1, LANES), 1)
    return jnp.where(
        lane % 32 < 16, pltpu.roll(values, LANES - 16, 1), pltpu.roll(values, 16, 1)
    )


def pair_norm(values, gain):
    return values * lax.rsqrt(pair_mean(values * values) + EPSILON) * gain


def pair_norm_back(values, gain, incoming):
    scaling = lax.rsqrt(pair_mean(values * values) + EPSILON)
    weighted = incoming * gain
    inner_mean = pair_mean(weighted * values)
    return (
        scaling * weighted - values * scaling * scaling * scaling * inner_mean,
        jnp.sum(incoming * values * scaling, axis=0, keepdims=True),
    )


def params(megabytes=48):
    return pltpu.CompilerParams(vmem_limit_bytes=megabytes * 1024 * 1024)


def whole(shape):
    return pl.BlockSpec(shape, lambda p, *_: (0,) * len(shape))


def columns(rows, width):
    return pl.BlockSpec((rows, width), lambda p, *_: (0, p))


def qkv_kernel(x, w, cosine, sine, q_gain, k_gain, q_pre, k_pre, q_out, kv_out):
    made = jnp.dot(x[...], w[...], preferred_element_type=F32)
    query, key = (made[:, :LANES], made[:, LANES : 2 * LANES])
    q_pre[...] = query
    k_pre[...] = key
    query = pair_norm(query, q_gain[...])
    key = pair_norm(key, k_gain[...])
    q_out[...] = (query * cosine[...] + partner(query) * sine[...]).astype(BF16)
    kv_out[:, :LANES] = (key * cosine[...] + partner(key) * sine[...]).astype(BF16)
    kv_out[:, LANES:] = made[:, 2 * LANES :].astype(BF16)


def qkv_call(hidden, weights, cosine, sine, q_gain, k_gain):
    rows, depth = hidden.shape
    pairs = weights.shape[1] // (3 * LANES)
    width = pairs * LANES
    return pl.pallas_call(
        qkv_kernel,
        grid=(pairs,),
        in_specs=[
            whole((rows, depth)),
            columns(depth, 3 * LANES),
            whole((rows, LANES)),
            whole((rows, LANES)),
            whole((1, LANES)),
            whole((1, LANES)),
        ],
        out_specs=[columns(rows, LANES)] * 3 + [columns(rows, 2 * LANES)],
        out_shape=[
            jax.ShapeDtypeStruct((rows, width), F32),
            jax.ShapeDtypeStruct((rows, width), F32),
            jax.ShapeDtypeStruct((rows, width), BF16),
            jax.ShapeDtypeStruct((rows, 2 * width), BF16),
        ],
        compiler_params=params(),
        cost_estimate=pl.CostEstimate(
            flops=6 * rows * depth * width, bytes_accessed=8_000_000, transcendentals=0
        ),
        name="qkv",
    )(hidden, weights, cosine, sine, q_gain, k_gain)


def qkv_back_kernel(dq, dkv, q_pre, k_pre, cosine, sine, q_gain, k_gain, out, dq_gain, dk_gain):
    query, key = (dq[...], dkv[:, :LANES])
    query = query * cosine[...] - partner(query) * sine[...]
    key = key * cosine[...] - partner(key) * sine[...]
    query, dq_gain[...] = pair_norm_back(q_pre[...], q_gain[...], query)
    key, dk_gain[...] = pair_norm_back(k_pre[...], k_gain[...], key)
    out[:, :LANES] = query.astype(BF16)
    out[:, LANES : 2 * LANES] = key.astype(BF16)
    out[:, 2 * LANES :] = dkv[:, LANES:].astype(BF16)


def qkv_back_call(dq, dkv, q_pre, k_pre, cosine, sine, q_gain, k_gain):
    rows, width = dq.shape
    pairs = width // LANES
    return pl.pallas_call(
        qkv_back_kernel,
        grid=(pairs,),
        in_specs=[columns(rows, LANES), columns(rows, 2 * LANES)]
        + [columns(rows, LANES)] * 2
        + [whole((rows, LANES))] * 2
        + [whole((1, LANES))] * 2,
        out_specs=[columns(rows, 3 * LANES), columns(1, LANES), columns(1, LANES)],
        out_shape=[
            jax.ShapeDtypeStruct((rows, 3 * width), BF16),
            jax.ShapeDtypeStruct((1, width), F32),
            jax.ShapeDtypeStruct((1, width), F32),
        ],
        compiler_params=params(),
        cost_estimate=pl.CostEstimate(flops=0, bytes_accessed=8_000_000, transcendentals=0),
        name="qkv_back",
    )(dq, dkv, q_pre, k_pre, cosine, sine, q_gain, k_gain)


def text_kernel(x, w, gain, k_pre, kv_out):
    made = jnp.dot(x[...], w[...], preferred_element_type=F32)
    k_pre[...] = made[:, :LANES]
    kv_out[:, :LANES] = pair_norm(made[:, :LANES], gain[...]).astype(BF16)
    kv_out[:, LANES:] = made[:, LANES:].astype(BF16)


def text_call(words, weights, gain):
    rows, depth = words.shape
    width = weights.shape[1] // 2
    return pl.pallas_call(
        text_kernel,
        grid=(width // LANES,),
        in_specs=[whole((rows, depth)), columns(depth, 2 * LANES), whole((1, LANES))],
        out_specs=[columns(rows, LANES), columns(rows, 2 * LANES)],
        out_shape=[
            jax.ShapeDtypeStruct((rows, width), F32),
            jax.ShapeDtypeStruct((rows, 2 * width), BF16),
        ],
        compiler_params=params(),
        cost_estimate=pl.CostEstimate(
            flops=4 * rows * depth * width, bytes_accessed=4_000_000, transcendentals=0
        ),
        name="text_kv",
    )(words, weights, gain)


def text_back_kernel(dkv, k_pre, gain, out, d_gain):
    key, d_gain[...] = pair_norm_back(k_pre[...], gain[...], dkv[:, :LANES])
    out[:, :LANES] = key.astype(BF16)
    out[:, LANES:] = dkv[:, LANES:].astype(BF16)


def text_back_call(dkv, k_pre, gain):
    rows, width = k_pre.shape
    return pl.pallas_call(
        text_back_kernel,
        grid=(width // LANES,),
        in_specs=[columns(rows, 2 * LANES), columns(rows, LANES), whole((1, LANES))],
        out_specs=[columns(rows, 2 * LANES), columns(1, LANES)],
        out_shape=[
            jax.ShapeDtypeStruct((rows, 2 * width), BF16),
            jax.ShapeDtypeStruct((1, width), F32),
        ],
        compiler_params=params(),
        cost_estimate=pl.CostEstimate(flops=0, bytes_accessed=2_000_000, transcendentals=0),
        name="text_kv_back",
    )(dkv, k_pre, gain)


class Meta:
    def __init__(self, ref, runs, blocks, wide, text_rows):
        self.ref, self.runs, self.blocks = (ref, runs, blocks)
        self.wide, self.text_rows = (wide, text_rows)

    def group(self, block):
        return self.ref[self.runs + block]

    def own(self):
        return self.ref[self.runs + self.blocks]

    def self_flag(self, block):
        return self.ref[self.runs + self.blocks + 1 + block]

    def cross_flag(self, block):
        return self.ref[self.runs + 2 * self.blocks + 1 + block]

    def run_items(self, group, count, axis):
        shape = (count, 1) if axis == 0 else (1, count)
        spot = lax.broadcasted_iota(jnp.int32, shape, axis) + group * count
        item = jnp.zeros(shape, jnp.int32)
        for run in range(self.runs):
            item = item + (spot >= self.ref[run]).astype(jnp.int32)
        return item

    def all_items(self, group, count, axis):
        shape = (count, 1) if axis == 0 else (1, count)
        row = lax.broadcasted_iota(jnp.int32, shape, axis)
        spot = row - self.wide + group * (count - self.wide)
        item = jnp.zeros(shape, jnp.int32)
        for run in range(self.runs):
            item = item + (spot >= self.ref[run]).astype(jnp.int32)
        return jnp.where(row < self.wide, self.runs, item)

    def text_items(self, group, axis):
        shape = (self.text_rows, 1) if axis == 0 else (1, self.text_rows)
        return (lax.broadcasted_iota(jnp.int32, shape, axis) + group * self.text_rows) // TTOK


def nt_dot(left, right):
    return lax.dot_general(left, right, (((1,), (1,)), ((), ())), preferred_element_type=F32)


def nn_dot(left, right):
    return jnp.dot(left, right, preferred_element_type=F32)


def tn_dot(left, right):
    return lax.dot_general(left, right, (((0,), (0,)), ((), ())), preferred_element_type=F32)


SCALING = 64 ** (-0.5) * SCORE_BASE
GRAD_SCALING = 64 ** (-0.5) * SCORE_BASE * TWO_NATURAL


def attend(query, key, value, allowed):
    sums, totals = (None, [])
    for query_head, value_head in zip(halves(query), halves(value)):
        weights = jnp.exp2(nt_dot(query_head, key) * SCALING)
        if allowed is not None:
            weights = jnp.where(allowed, weights, 0.0)
        totals.append(jnp.sum(weights, axis=-1, keepdims=True))
        fresh = nn_dot(weights.astype(BF16), value_head)
        sums = fresh if sums is None else sums + fresh
    return (sums, pair_select(*totals))


def self_kernel(runs, highs, wide, text_rows, ref, q, kv0, kv1, kv2, kv3, self_out, self_total):
    meta = Meta(ref, runs, 4 * highs, wide, text_rows)
    run_rows = q.shape[0] - wide
    self_out[...] = jnp.zeros(self_out.shape, F32)
    self_total[...] = jnp.zeros(self_total.shape, F32)
    run_items = meta.run_items(meta.own(), run_rows, 0)
    for number, kv in enumerate((kv0, kv1, kv2, kv3)):
        keys = kv[:, :wide, :LANES].reshape(highs * wide, LANES)
        values = kv[:, :wide, LANES:].reshape(highs * wide, LANES)
        sums, totals = attend(q[:wide, :], keys, values, None)
        self_out[:wide, :] += sums
        self_total[:wide, :] += totals

        @pl.loop(0, highs)
        def _(high, number=number, kv=kv):
            block = number * highs + high

            @pl.when(meta.self_flag(block) > 0)
            def _():
                allowed = run_items == meta.run_items(meta.group(block), run_rows, 1)
                sums, totals = attend(
                    q[wide:, :], kv[high, wide:, :LANES], kv[high, wide:, LANES:], allowed
                )
                self_out[wide:, :] += sums
                self_total[wide:, :] += totals

    self_out[...] = self_out[...] / self_total[...]


def cross_kernel(
    runs, highs, wide, text_rows, ref, q, self_out, t0, t1, t2, t3, gate,
    combined, cross_out, cross_total,
):
    meta = Meta(ref, runs, 4 * highs, wide, text_rows)
    cross_out[...] = jnp.zeros(cross_out.shape, F32)
    cross_total[...] = jnp.zeros(cross_total.shape, F32)
    all_items = meta.all_items(meta.own(), q.shape[0], 0)
    for number, text in enumerate((t0, t1, t2, t3)):

        @pl.loop(0, highs)
        def _(high, number=number, text=text):
            block = number * highs + high

            @pl.when(meta.cross_flag(block) > 0)
            def _():
                allowed = all_items == meta.text_items(meta.group(block), 1)
                sums, totals = attend(
                    q[...], text[high, :, :LANES], text[high, :, LANES:], allowed
                )
                cross_out[...] += sums
                cross_total[...] += totals

    across = cross_out[...] / cross_total[...]
    cross_out[...] = across
    combined[...] = (self_out[...] + gate[...] * across).astype(BF16)


def self_call(meta, queries, kvs, runs, text_rows):
    rows, width = queries.shape
    highs = kvs[0].shape[0]
    kv_spec = pl.BlockSpec((highs, rows, 2 * LANES), lambda p, *_: (0, 0, p))
    return pl.pallas_call(
        functools.partial(self_kernel, runs, highs, rows // 4, text_rows),
        grid_spec=pltpu.PrefetchScalarGridSpec(
            num_scalar_prefetch=1,
            grid=(width // LANES,),
            in_specs=[columns(rows, LANES)] + [kv_spec] * 4,
            out_specs=[columns(rows, LANES)] * 2,
        ),
        out_shape=[jax.ShapeDtypeStruct((rows, width), F32)] * 2,
        compiler_params=params(56),
        cost_estimate=pl.CostEstimate(
            flops=15_000_000_000, bytes_accessed=15_000_000, transcendentals=0
        ),
        name="attention_self",
    )(meta, queries, *kvs)


def cross_call(meta, queries, self_out, texts, gate, runs):
    rows, width = queries.shape
    highs, text_rows = texts[0].shape[:2]
    text_spec = pl.BlockSpec((highs, text_rows, 2 * LANES), lambda p, *_: (0, 0, p))
    floats = jax.ShapeDtypeStruct((rows, width), F32)
    return pl.pallas_call(
        functools.partial(cross_kernel, runs, highs, rows // 4, text_rows),
        grid_spec=pltpu.PrefetchScalarGridSpec(
            num_scalar_prefetch=1,
            grid=(width // LANES,),
            in_specs=[columns(rows, LANES)] * 2 + [text_spec] * 4 + [columns(1, LANES)],
            out_specs=[columns(rows, LANES)] * 3,
        ),
        out_shape=[jax.ShapeDtypeStruct((rows, width), BF16), floats, floats],
        compiler_params=params(56),
        cost_estimate=pl.CostEstimate(
            flops=5_000_000_000, bytes_accessed=5_000_000, transcendentals=0
        ),
        name="attention_cross",
    )(meta, queries, self_out, *texts, gate)


def attend_back(query, grad, less, key, value, allowed):
    d_key, d_value, d_query = (None, None, None)
    for query_head, grad_head, less_head, key_head in zip(
        halves(query), halves(grad), less, halves(key)
    ):
        weights = jnp.exp2(nt_dot(key, query_head) * SCALING)
        if allowed is not None:
            weights = jnp.where(allowed, weights, 0.0)
        raw = weights * (nt_dot(value, grad_head) + less_head) * GRAD_SCALING
        raw = raw.astype(BF16)
        terms = (
            nn_dot(raw, query_head),
            nn_dot(weights.astype(BF16), grad_head),
            tn_dot(raw, key_head),
        )
        if d_key is None:
            d_key, d_value, d_query = terms
        else:
            d_key, d_value, d_query = (
                d_key + terms[0],
                d_value + terms[1],
                d_query + terms[2],
            )
    return (d_key.astype(BF16), d_value.astype(BF16), d_query)


def attention_back_kernel(
    runs, highs, wide, text_rows, ref, q, g, self_out, cross_out, self_total, cross_total, gate,
    kv0, kv1, kv2, kv3, t0, t1, t2, t3,
    dq, d_same, d_other, dt_same, dt_other, d_gate, self_grad, cross_grad,
):
    meta = Meta(ref, runs, 4 * highs, wide, text_rows)
    rows = q.shape[0]
    run_rows = rows - wide
    own = meta.own()
    run_items = meta.run_items(own, run_rows, 1)
    all_items = meta.all_items(own, rows, 1)
    incoming = g[...]
    d_gate[...] = jnp.sum(incoming * cross_out[...], axis=0, keepdims=True)
    scaled = incoming / self_total[...]
    self_grad[...] = scaled.astype(BF16)
    turned = jnp.transpose(scaled * self_out[...])
    self_less = (
        -jnp.sum(turned[: LANES // 2], axis=0, keepdims=True),
        -jnp.sum(turned[LANES // 2 :], axis=0, keepdims=True),
    )
    scaled = incoming * gate[...] / cross_total[...]
    cross_grad[...] = scaled.astype(BF16)
    turned = jnp.transpose(scaled * cross_out[...])
    cross_less = (
        -jnp.sum(turned[: LANES // 2], axis=0, keepdims=True),
        -jnp.sum(turned[LANES // 2 :], axis=0, keepdims=True),
    )
    wide_less = tuple(row[:, :wide] for row in self_less)
    run_less = tuple(row[:, wide:] for row in self_less)
    dq[...] = jnp.zeros(dq.shape, F32)
    arrays = (
        (kv0, t0, d_same.at[0], dt_same.at[0]),
        (kv1, t1, d_same.at[1], dt_same.at[1]),
        (kv2, t2, d_other.at[0], dt_other.at[0]),
        (kv3, t3, d_other.at[1], dt_other.at[1]),
    )
    for number, (kv, text, dkv, dtext) in enumerate(arrays):
        keys = kv[:, :wide, :LANES].reshape(highs * wide, LANES)
        values = kv[:, :wide, LANES:].reshape(highs * wide, LANES)
        d_key, d_value, d_query = attend_back(
            q[:wide, :], self_grad[:wide, :], wide_less, keys, values, None
        )
        dkv[:, :wide, :LANES] = d_key.reshape(highs, wide, LANES)
        dkv[:, :wide, LANES:] = d_value.reshape(highs, wide, LANES)
        dq[:wide, :] += d_query

        @pl.loop(0, highs)
        def _(high, number=number, kv=kv, text=text, dkv=dkv, dtext=dtext):
            block = number * highs + high

            @pl.when(meta.self_flag(block) > 0)
            def _():
                allowed = meta.run_items(meta.group(block), run_rows, 0) == run_items
                d_key, d_value, d_query = attend_back(
                    q[wide:, :],
                    self_grad[wide:, :],
                    run_less,
                    kv[high, wide:, :LANES],
                    kv[high, wide:, LANES:],
                    allowed,
                )
                dkv[high, wide:, :LANES] = d_key
                dkv[high, wide:, LANES:] = d_value
                dq[wide:, :] += d_query

            @pl.when(meta.self_flag(block) == 0)
            def _():
                dkv[high, wide:, :] = jnp.zeros((run_rows, 2 * LANES), BF16)

            @pl.when(meta.cross_flag(block) > 0)
            def _():
                allowed = meta.text_items(meta.group(block), 0) == all_items
                d_key, d_value, d_query = attend_back(
                    q[...],
                    cross_grad[...],
                    cross_less,
                    text[high, :, :LANES],
                    text[high, :, LANES:],
                    allowed,
                )
                dtext[high, :, :LANES] = d_key
                dtext[high, :, LANES:] = d_value
                dq[...] += d_query

            @pl.when(meta.cross_flag(block) == 0)
            def _():
                dtext[high] = jnp.zeros((text_rows, 2 * LANES), BF16)


def attention_back_call(meta, queries, incoming, outputs, gate, kvs, texts, runs):
    rows, width = queries.shape
    highs, text_rows = (kvs[0].shape[0], texts[0].shape[1])
    wide = rows // 4
    kv_spec = pl.BlockSpec((highs, rows, 2 * LANES), lambda p, *_: (0, 0, p))
    text_spec = pl.BlockSpec((highs, text_rows, 2 * LANES), lambda p, *_: (0, 0, p))
    d_kv = jax.ShapeDtypeStruct((2, *kvs[0].shape), BF16)
    d_text = jax.ShapeDtypeStruct((2, *texts[0].shape), BF16)
    return pl.pallas_call(
        functools.partial(attention_back_kernel, runs, highs, wide, text_rows),
        grid_spec=pltpu.PrefetchScalarGridSpec(
            num_scalar_prefetch=1,
            grid=(width // LANES,),
            in_specs=[columns(rows, LANES)] * 6
            + [columns(1, LANES)]
            + [kv_spec] * 4
            + [text_spec] * 4,
            out_specs=[columns(rows, LANES)]
            + [pl.BlockSpec((2, highs, rows, 2 * LANES), lambda p, *_: (0, 0, 0, p))] * 2
            + [pl.BlockSpec((2, highs, text_rows, 2 * LANES), lambda p, *_: (0, 0, 0, p))] * 2
            + [columns(1, LANES)],
            scratch_shapes=[pltpu.VMEM((rows, LANES), BF16)] * 2,
        ),
        out_shape=[jax.ShapeDtypeStruct((rows, width), F32), d_kv, d_kv, d_text, d_text]
        + [jax.ShapeDtypeStruct((1, width), F32)],
        compiler_params=params(60),
        cost_estimate=pl.CostEstimate(
            flops=30_000_000_000, bytes_accessed=30_000_000, transcendentals=0
        ),
        name="attention_back",
    )(meta, queries, incoming, *outputs, gate, *kvs, *texts)


def separate(array, kinds):
    pairs = array.shape[-1] // LANES // kinds
    return [
        jnp.concatenate(
            [
                array[..., (p * kinds + kind) * LANES : (p * kinds + kind + 1) * LANES]
                for p in range(pairs)
            ],
            axis=-1,
        )
        for kind in range(kinds)
    ]


def on_device(
    patches,
    cotangent,
    item_lengths,
    timesteps,
    patch_rows,
    patch_cols,
    conditioning,
    text_states,
    gain_attn,
    gain_ffn,
    query_gain,
    key_gain,
    text_key_gain,
    cross_gate,
    w_query,
    w_key,
    w_value,
    w_out,
    w_text_key,
    w_text_value,
    w_gate,
    w_up,
    w_down,
    w_ada,
    w_text,
):
    at = Place()
    tok_dev, model_width = patches.shape
    shard_rows = w_query.shape[0]
    head_dim = query_gain.shape[0]
    local_width = w_query.shape[1]
    heads_local = local_width // head_dim
    text_rows = text_states.shape[0]
    item_count = conditioning.shape[0]
    quarter = tok_dev // 4
    hidden_width = w_gate.shape[1]

    shards = [w_query, w_key, w_value]
    shared_qkv = share(shards, by_pairs(shards), at)
    qkv_rows = GatherRows(shared_qkv, 0, [3 * local_width], at)
    qkv_rows.z()
    first = [shared_qkv[2]]
    text_width = w_text.shape[1]
    shards = [w_text, w_text_key, w_text_value, w_out, w_down, w_gate, w_up]
    order = side_by_side(shards)
    order[1:3] = [
        (1 + source, start, width)
        for source, start, width in by_pairs([w_text_key, w_text_value])
    ]
    shared = share(shards, order, at, [qkv_rows.stacked])
    places = [0]
    for width in (text_width + 2 * local_width, local_width, hidden_width):
        places.append(places[-1] + width)
    qkv_rows.y()
    text_rows_all = GatherRows(shared, places[0], [text_width, 2 * local_width], at)
    out_rows = GatherRows(shared, places[1], [local_width], at)
    down_rows = GatherRows(shared, places[2], [hidden_width], at)
    gu_rows = GatherRows(shared, places[3], [2 * hidden_width], at)
    embed_pre = conditioning.astype(F32) + time_embed(timesteps, model_width)
    embed = jax.nn.silu(embed_pre).astype(BF16)
    own_embed = lax.dynamic_slice_in_dim(embed, at.data * shard_rows, shard_rows, 1)
    gains = lax.dynamic_update_slice(
        jnp.zeros((2, model_width), F32),
        jnp.stack([gain_attn, gain_ffn]).astype(F32),
        (0, at.data * shard_rows),
    )
    head_sums = butterfly(
        after(jnp.concatenate([multiply(own_embed, w_ada), gains], axis=0), *first),
        at,
        model=False,
        z_wait=[qkv_rows.near],
    )
    my_patches = swap_rows(after(patches, *first), at)
    text_rows_all.z()
    (full_qkv,) = qkv_rows.core()
    positions = swap_roles(
        after(jnp.stack([patch_rows, patch_cols]).astype(F32), head_sums)
    )
    gain_attn32, gain_ffn32 = (head_sums[item_count], head_sums[item_count + 1])
    mod_part = head_sums[:item_count]
    mod_pair = jnp.stack(
        unmix([mod_part, lax.ppermute(mod_part, "mp", [(i, i ^ 1) for i in range(4)])], at.c)
    )
    mod_all = jnp.stack(
        unmix([mod_pair, lax.ppermute(mod_pair, "mp", [(i, i ^ 2) for i in range(4)])], at.x)
    )
    shift1_t, gate1_t, shift2_t, gate2_t = mod_all.reshape(4, item_count, model_width)

    token_items = item_ids(item_lengths, tok_dev, at.n_dp).reshape(at.n_dp, tok_dev)
    own_items = pick(token_items, at.tokens)
    item_labels = jnp.arange(item_count, dtype=jnp.int32)
    onehot = (own_items[:, None] == item_labels[None, :]).astype(F32)
    runs = item_lengths.shape[0]
    groups = jnp.stack(relative_groups(at)).astype(jnp.int32)
    firsts, lasts = (token_items[:, tok_dev // 4], token_items[:, tok_dev - 1])
    my_first, my_last = (pick(firsts, at.tokens), pick(lasts, at.tokens))
    self_flags = (firsts[groups] <= my_last) & (lasts[groups] >= my_first)
    text_first = groups * text_rows // TTOK
    text_last = (groups * text_rows + text_rows - 1) // TTOK
    cross_flags = ((text_first <= my_last) & (text_last >= my_first)) | (text_last >= runs)
    meta = jnp.concatenate(
        [
            jnp.cumsum(item_lengths),
            groups,
            at.tokens[None],
            self_flags.astype(jnp.int32),
            cross_flags.astype(jnp.int32),
        ]
    ).astype(jnp.int32)
    few_items = lax.dynamic_slice_in_dim(own_items, at.features * quarter, quarter)
    few_onehot = lax.dynamic_slice_in_dim(onehot, at.features * quarter, quarter)

    shift1 = rows_of(shift1_t, own_items)
    inputs = my_patches.astype(F32)
    normed1, _ = norm_fwd(inputs, gain_attn32)
    hidden1 = (normed1 * (1.0 + shift1)).astype(BF16)

    angles = rope_angles(positions[0], positions[1], head_dim)
    both_heads = (1, LANES // head_dim)
    cosine, sine = (jnp.cos(angles), jnp.sin(angles))
    split = head_dim // 4
    cosine = jnp.tile(
        jnp.concatenate([cosine[:, :split]] * 2 + [cosine[:, split:]] * 2, axis=1), both_heads
    )
    sine = jnp.tile(
        jnp.concatenate(
            [-sine[:, :split], sine[:, :split], -sine[:, split:], sine[:, split:]], axis=1
        ),
        both_heads,
    )
    query_gain32, key_gain32, text_gain32 = (
        jnp.tile(gain.astype(F32)[None], both_heads)
        for gain in (query_gain, key_gain, text_key_gain)
    )
    query_pre, key_pre, queries, own_kv = qkv_call(
        hidden1, full_qkv, cosine, sine, query_gain32, key_gain32
    )
    kv_tokens = GatherTokens(own_kv, at)
    kv_tokens.z()
    text_rows_all.y()
    kv_tokens.y()
    my_text = swap_roles(after(text_states, head_sums))
    full_text, full_tkv = text_rows_all.core(kv_tokens.near)
    out_rows.z()
    words = sum_features(multiply_trans(my_text, full_text).astype(BF16), at)
    out_rows.y()
    text_pre, own_text_kv = text_call(words, full_tkv, text_gain32)
    text_tokens = GatherTokens(own_text_kv, at)
    text_tokens.z()
    text_tokens.y()
    my_cotangent = swap_rows(cotangent, at)
    gu_rows.z()
    gu_rows.y()
    (full_out,) = out_rows.core()
    gate_local = jnp.tanh(
        lax.dynamic_slice_in_dim(cross_gate.astype(F32), at.features * heads_local, heads_local)
    )
    gate_wide = jnp.repeat(gate_local, head_dim)[None]
    all_kv = kv_tokens.core()
    self_out, self_total = self_call(meta, queries, all_kv, runs, text_rows)
    all_text_kv = text_tokens.core()
    combined, cross_out, cross_total = cross_call(
        meta, queries, self_out, all_text_kv, gate_wide, runs
    )
    outputs = (self_out, cross_out, self_total, cross_total)
    few_inputs = lax.dynamic_slice_in_dim(inputs, at.features * quarter, quarter)
    few_normed1 = lax.dynamic_slice_in_dim(normed1, at.features * quarter, quarter)
    tanh_one = jnp.tanh(rows_of(gate1_t, few_items))
    tanh_two = jnp.tanh(rows_of(gate2_t, few_items))
    shift2 = rows_of(shift2_t, few_items)
    few_shift1 = rows_of(shift1_t, few_items)
    combined_out = after(combined, gu_rows.near)
    branch = sum_quarters(multiply_trans(combined_out, full_out).astype(BF16), at)
    down_rows.z()
    down_rows.y()
    middle = few_inputs + tanh_one * branch
    normed2, scale2 = norm_fwd(middle, gain_ffn32)
    hidden2 = gather_quarters((normed2 * (1.0 + shift2)).astype(BF16), at)
    (full_gu,) = gu_rows.core(combined)
    (full_down,) = down_rows.core(combined)
    gate_up = multiply(hidden2, full_gu)
    gate_pre, up_pre = (gate_up[:, :hidden_width], gate_up[:, hidden_width:])
    logistic = jax.nn.sigmoid(gate_pre)
    silu_gate = gate_pre * logistic
    inner_act = (silu_gate * up_pre).astype(BF16)

    grad_output = my_cotangent.astype(F32)
    few_output = lax.dynamic_slice_in_dim(grad_output, at.features * quarter, quarter)
    grad_ffn = (grad_output * rows_of(jnp.tanh(gate2_t), own_items)).astype(BF16)
    grad_inner = multiply(grad_ffn, full_down)
    grad_gate = (grad_inner * up_pre * logistic * (1.0 + gate_pre * (1.0 - logistic))).astype(BF16)
    grad_up = (grad_inner * silu_gate).astype(BF16)
    grad_gu = jnp.concatenate([grad_gate, grad_up], axis=1)
    hidden2_part = multiply_trans(grad_gu, full_gu).astype(BF16)
    grad_hidden2 = sum_quarters(hidden2_part, at)
    ffn_sums = ScatterRows(
        [
            trans_multiply(after(grad_ffn, hidden2_part), inner_act),
            trans_multiply(after(hidden2, hidden2_part), grad_gu),
        ],
        at,
    )
    ffn_sums.y()
    grad_middle_norm, gain_ffn_term = norm_back(
        middle, scale2, gain_ffn32, grad_hidden2 * (1.0 + shift2)
    )
    grad_middle = few_output + grad_middle_norm
    grad_branch = gather_quarters((grad_middle * tanh_one).astype(BF16), at)
    grad_combined = multiply(grad_branch, full_out)
    ffn_part = multiply_trans(after(inner_act, grad_combined), full_down).astype(BF16)
    ffn_out = sum_quarters(ffn_part, at)
    out_sums = ScatterRows([trans_multiply(grad_branch, combined)], at)
    out_sums.y()
    grad_queries, d_same, d_other, dt_same, dt_other, gate_terms = attention_back_call(
        meta, queries, grad_combined, outputs, gate_wide, all_kv, all_text_kv, runs
    )
    out_sums.z()
    text_sums = ScatterTokens(dt_same, dt_other, at)
    kv_sums = ScatterTokens(d_same, d_other, at)
    text_sums.y()
    kv_sums.y()
    text_back = text_sums.z()
    ffn_sums.z()
    grad_gate_local = jnp.sum(gate_terms.reshape(heads_local, head_dim), axis=1) * (
        1.0 - gate_local * gate_local
    )
    grad_tkv, text_gain_term = text_back_call(text_back, text_pre, text_gain32)
    grad_words = sum_features(multiply_trans(grad_tkv, full_tkv).astype(BF16), at)
    kv_back = kv_sums.z()
    mixed_out = gather_output((middle + tanh_two * ffn_out).astype(BF16), at)
    words_sums = ScatterRows(
        [trans_multiply(grad_words, my_text), trans_multiply(words, grad_tkv)], at
    )
    words_sums.y()
    grad_qkv, query_gain_term, key_gain_term = qkv_back_call(
        grad_queries, kv_back, query_pre, key_pre, cosine, sine, query_gain32, key_gain32
    )
    hidden1_part = multiply_trans(grad_qkv, full_qkv).astype(BF16)
    grad_hidden1 = sum_quarters(hidden1_part, at)
    qkv_sums = ScatterRows([trans_multiply(after(hidden1, hidden1_part), grad_qkv)], at)
    few_scale1 = lax.rsqrt(jnp.mean(few_inputs * few_inputs, axis=-1, keepdims=True) + EPSILON)
    grad_inputs_norm, gain_attn_term = norm_back(
        few_inputs, few_scale1, gain_attn32, grad_hidden1 * (1.0 + few_shift1)
    )
    grad_patches = gather_output((grad_middle + grad_inputs_norm).astype(BF16), at).astype(F32)
    qkv_sums.y()
    words_sums.z()
    qkv_sums.z()
    grads_out, grads_ffn = (out_sums.result(), ffn_sums.result())
    grads_texts, grads_qkv = (words_sums.result(), qkv_sums.result())
    grad_text = swap_roles(multiply(grad_words, full_text).astype(BF16)).astype(F32)
    def item_sums(rows):
        return trans_multiply(few_onehot, rows, HIGHEST)

    gate_full = lax.dynamic_update_slice_in_dim(
        jnp.zeros((cross_gate.shape[0],), F32),
        grad_gate_local,
        at.features * heads_local,
        0,
    )
    small = jnp.concatenate(
        [
            jnp.sum(query_gain_term.reshape(heads_local, head_dim), axis=0),
            jnp.sum(key_gain_term.reshape(heads_local, head_dim), axis=0),
            jnp.sum(text_gain_term.reshape(heads_local, head_dim), axis=0),
            gate_full,
        ]
    )
    small = jnp.pad(small, (0, model_width - small.shape[0]))
    late = butterfly(
        after(jnp.concatenate(
            [
                item_sums(
                    jnp.concatenate(
                        [
                            grad_hidden1 * few_normed1,
                            grad_middle * branch * (1.0 - tanh_one * tanh_one),
                            grad_hidden2 * normed2,
                            few_output * ffn_out * (1.0 - tanh_two * tanh_two),
                        ],
                        axis=1,
                    )
                )
                .reshape(item_count, 4, model_width)
                .swapaxes(0, 1)
                .reshape(4 * item_count, model_width),
                jnp.sum(gain_attn_term, axis=0, keepdims=True),
                jnp.sum(gain_ffn_term, axis=0, keepdims=True),
                small[None],
            ],
            axis=0,
        ), words_sums.to_z),
        at,
    )
    grad_mod_own = pick(late[: 4 * item_count].reshape(4, item_count, model_width), at.model)
    late = late[4 * item_count :]
    small = late[2]
    grad_ada = trans_multiply(own_embed.astype(F32), grad_mod_own, HIGHEST)
    grad_embed_part = multiply_trans(grad_mod_own, w_ada.astype(F32), HIGHEST)
    grad_embed = butterfly(
        lax.dynamic_update_slice(
            jnp.zeros((item_count, model_width), F32),
            grad_embed_part,
            (0, at.data * shard_rows),
        ),
        at,
    )
    embed_logistic = jax.nn.sigmoid(embed_pre)
    grad_conditioning = grad_embed * embed_logistic * (1.0 + embed_pre * (1.0 - embed_logistic))
    own_gain = lambda row: lax.dynamic_slice_in_dim(row, at.data * shard_rows, shard_rows)
    grad_wq, grad_wk, grad_wv = separate(grads_qkv, 3)
    grad_wtk, grad_wtv = separate(grads_texts[:, text_width:], 2)
    return (
        mixed_out,
        grad_patches,
        grad_conditioning,
        grad_text,
        own_gain(late[0]),
        own_gain(late[1]),
        small[:head_dim],
        small[head_dim : 2 * head_dim],
        small[2 * head_dim : 3 * head_dim],
        small[3 * head_dim : 3 * head_dim + cross_gate.shape[0]],
        grad_wq,
        grad_wk,
        grad_wv,
        grads_out,
        grad_wtk,
        grad_wtv,
        grads_ffn[:, hidden_width : 2 * hidden_width],
        grads_ffn[:, 2 * hidden_width :],
        grads_ffn[:, :hidden_width],
        grad_ada,
        grads_texts[:, :text_width],
    )


def solution(mesh):
    rows, both, one = (P("dp", None), P("dp", "mp"), P("dp"))
    whole = P()
    in_specs = (
        (rows, rows, whole, whole, one, one, whole, both, one, one)
        + (whole,) * 4
        + (both,) * 11
    )
    out_specs = (
        (rows, rows, whole, both, one, one) + (whole,) * 4 + (both,) * 11
    )
    return jax.shard_map(
        on_device, mesh=mesh, in_specs=in_specs, out_specs=out_specs, check_vma=False
    )
```
